256 devices in a mesh: group: 4 (over z_lo), fsdp: 32 (over x, z_hi, y), seq: 2 (over core).
Axes of the slice: x: 4, y: 4, z: 8 (z_hi: 2, z_lo: 4; z = z_hi * 4 + z_lo), core: 2. Of those that a mesh axis runs over, the one named last changes fastest.
Arguments:
- gen_noise: bfloat16 [3, 4096, 64], P(None, 'fsdp'), may hold values from -5 to 5
- score_noise: bfloat16 [3, 4096, 64], P(None, 'fsdp'), may hold values from -128 to 128
- gen_steps: int32 [3], replicated, may hold values from 0 to 999
- score_steps: int32 [3], replicated, may hold values from 0 to 999
- gen_embed: bfloat16 [64, 3072], replicated, may hold values from -0.75 to 0.75
- gen_modulation: bfloat16 [256, 15360], P(None, 'fsdp'), may hold values from -0.375 to 0.375
- gen_proj: bfloat16 [3072, 3072], P('fsdp', ('group', 'seq')), may hold values from -0.109375 to 0.109375
- gen_final: bfloat16 [3072, 64], replicated, may hold values from -0.109375 to 0.109375
- teacher_embed: bfloat16 [64, 3072], replicated, may hold values from -0.75 to 0.75
- teacher_modulation: bfloat16 [256, 15360], P(None, 'fsdp'), may hold values from -0.375 to 0.375
- teacher_proj: bfloat16 [3072, 3072], P('fsdp', ('group', 'seq')), may hold values from -0.109375 to 0.109375
- teacher_final: bfloat16 [3072, 64], replicated, may hold values from -0.109375 to 0.109375
- fake_embed: bfloat16 [64, 3072], replicated, may hold values from -0.75 to 0.75
- fake_modulation: bfloat16 [256, 15360], P(None, 'fsdp'), may hold values from -0.375 to 0.375
- fake_proj: bfloat16 [3072, 3072], P('fsdp', ('group', 'seq')), may hold values from -0.109375 to 0.109375
- fake_final: bfloat16 [3072, 64], replicated, may hold values from -0.109375 to 0.109375
Outputs:
- samples: float32 [3, 4096, 64], P(None, 'fsdp')
- gen_grad: float32 [3072, 3072], P('fsdp', ('group', 'seq'))
- fake_grad: float32 [3072, 3072], P('fsdp', ('group', 'seq'))
The draws below stay inside these ranges and needn't reach their ends.
All inputs are finite; a program needn't handle non-finite values.
Results may differ from the reference program's by a relative error of at most 0.0063.
Values may be sent and summed in bfloat16 or wider, within the bound.
No kernel may reach another device: no remote copies, remote signals or barrier semaphores. Data moves between devices by JAX's collectives and lax.ppermute only.
A program may use at most 128 MiB of HBM per device.

```python
import math
import jax
import jax.numpy as jnp
from jax import lax

D = 3072
C = 64
TE = 256
S = 4096
STEPS = 1000
IMAGES = 3


def draw_score_noise(key, part):
    key = jax.random.fold_in(key, 7)
    key_values, key_rows, key_columns = jax.random.split(key, 3)
    rising = 1.0 + 2.0 * jnp.arange(S, dtype=jnp.float32) / S
    column_scale = jnp.exp(jax.random.uniform(key_columns, (1, 1, C), jnp.float32, -1.15, 1.15))
    values = jnp.clip(jax.random.normal(key_values, (IMAGES, S, C), jnp.float32), -4.0, 4.0)
    row_scale = jnp.exp(jax.random.uniform(key_rows, (IMAGES, S, 1), jnp.float32, -1.15, 1.15))
    return (values * rising[None, :, None] * row_scale * column_scale).astype(jnp.bfloat16)


def block_levels(own_key, dims, cuts, least, high):
    level = 1.0
    for dim, blocks in cuts:
        heights = jax.random.uniform(jax.random.fold_in(jax.random.fold_in(own_key, 6), dim), (blocks,), jnp.float32, least / len(cuts), high / len(cuts))
        level = level * jnp.repeat(jnp.exp(heights), dims[dim] // blocks).reshape((-1,) + (1,) * (len(dims) - 1 - dim))
    return level


def scatter_about(own_key, dims, spread, bound, cuts=(), kind=jnp.bfloat16):
    entries = spread * jax.random.normal(own_key, dims, jnp.float32)
    if cuts:
        entries = entries * block_levels(own_key, dims, cuts, -0.22, 0.18)
    return jnp.clip(entries, -bound, bound).astype(kind)


def setup_inputs(seed: int = 0) -> dict:
    splits = jax.random.split(jax.random.key(seed), 17)
    gen_noise = scatter_about(splits[0], (IMAGES, S, C), 1.0, 5.0, ((1, 32),))
    score_noise = draw_score_noise(jax.random.fold_in(splits[16], 71), 0)
    gen_steps = jax.random.randint(splits[2], (IMAGES,), 0, STEPS).astype(jnp.int32)
    score_steps = jax.random.randint(splits[3], (IMAGES,), 0, STEPS).astype(jnp.int32)
    gen_embed = scatter_about(splits[4], (C, D), C ** -0.5, 0.75)
    gen_modulation = scatter_about(splits[5], (TE, 5 * D), TE ** -0.5, 0.375, ((1, 32),))
    gen_proj = scatter_about(splits[6], (D, D), D ** -0.5, 0.109375, ((0, 32), (1, 8)))
    gen_final = scatter_about(splits[7], (D, C), D ** -0.5, 0.109375)
    teacher_embed = scatter_about(splits[8], (C, D), C ** -0.5, 0.75)
    teacher_modulation = scatter_about(splits[9], (TE, 5 * D), TE ** -0.5, 0.375, ((1, 32),))
    teacher_proj = scatter_about(splits[10], (D, D), D ** -0.5, 0.109375, ((0, 32), (1, 8)))
    teacher_final = scatter_about(splits[11], (D, C), D ** -0.5, 0.109375)
    fake_embed = scatter_about(splits[12], (C, D), C ** -0.5, 0.75)
    fake_modulation = scatter_about(splits[13], (TE, 5 * D), TE ** -0.5, 0.375, ((1, 32),))
    fake_proj = scatter_about(splits[14], (D, D), D ** -0.5, 0.109375, ((0, 32), (1, 8)))
    fake_final = scatter_about(splits[15], (D, C), D ** -0.5, 0.109375)
    return dict(gen_noise=gen_noise, score_noise=score_noise, gen_steps=gen_steps, score_steps=score_steps, gen_embed=gen_embed, gen_modulation=gen_modulation, gen_proj=gen_proj, gen_final=gen_final, teacher_embed=teacher_embed, teacher_modulation=teacher_modulation, teacher_proj=teacher_proj, teacher_final=teacher_final, fake_embed=fake_embed, fake_modulation=fake_modulation, fake_proj=fake_proj, fake_final=fake_final)


norm_epsilon = 1e-06
gap_epsilon = 1e-05

def time_features(steps):
    times = (steps.astype(jnp.float32) + 1.0) / (STEPS + 1.0)
    half = TE // 2
    frequency = jnp.exp(-jnp.log(10000.0) * jnp.arange(half, dtype=jnp.float32) / half)
    angles = 1000.0 * times[:, None] * frequency[None, :]
    embedding = jnp.concatenate([jnp.cos(angles), jnp.sin(angles)], axis=1)
    return (times, jax.nn.silu(embedding).astype(jnp.bfloat16))

def modulate(conditioning, weights):
    rounded = lax.optimization_barrier(jnp.dot(conditioning, weights, preferred_element_type=jnp.float32).astype(jnp.bfloat16))
    return rounded.astype(jnp.float32).reshape(conditioning.shape[0], 5, -1)

def layer_norm(values):
    average = lax.optimization_barrier(jnp.mean(values, axis=-1, keepdims=True))
    squares = lax.optimization_barrier(jnp.mean(values * values, axis=-1, keepdims=True))
    inverse_rms = lax.rsqrt(squares - average * average + norm_epsilon)
    return ((values - average) * inverse_rms, inverse_rms)

def gelu_grad(preactivation, upstream):
    return jax.vjp(lambda inner_value: jax.nn.gelu(inner_value, approximate=True), preactivation)[1](upstream)[0]

def forward(latents, modulations, w_embed, w_proj, w_final):
    images, tokens, channels = latents.shape
    model_width = w_embed.shape[1]
    hidden = jnp.dot(latents.reshape(images * tokens, channels), w_embed, preferred_element_type=jnp.float32).reshape(images, tokens, model_width)
    normed, _ = layer_norm(hidden)
    shaped = (normed * (1.0 + modulations[:, 1:2, :]) + modulations[:, 0:1, :]).astype(jnp.bfloat16).reshape(images * tokens, model_width)
    preactivation = jnp.dot(shaped, w_proj, preferred_element_type=jnp.float32)
    activated = lax.optimization_barrier(jax.nn.gelu(preactivation, approximate=True).astype(jnp.bfloat16))
    residual = hidden + modulations[:, 2:3, :] * activated.astype(jnp.float32).reshape(images, tokens, model_width)
    normed_two, inverse_rms = layer_norm(residual)
    output = (normed_two * (1.0 + modulations[:, 4:5, :]) + modulations[:, 3:4, :]).astype(jnp.bfloat16)
    velocity = jnp.dot(output.reshape(images * tokens, model_width), w_final, preferred_element_type=jnp.float32)
    return (velocity.reshape(images, tokens, -1), (shaped, preactivation, normed_two, inverse_rms))

def backward(cotangent, stored, modulations, w_final):
    shaped, preactivation, normed_two, inverse_rms = stored
    images, tokens, model_width = normed_two.shape
    cot_small = cotangent.reshape(images * tokens, -1).astype(jnp.bfloat16)
    out_grad = lax.dot_general(cot_small, w_final, (((1,), (1,)), ((), ())), preferred_element_type=jnp.float32).reshape(images, tokens, model_width)
    norm_grad = out_grad * (1.0 + modulations[:, 4:5, :])
    first_moment = lax.optimization_barrier(jnp.mean(norm_grad, axis=-1, keepdims=True))
    second_moment = lax.optimization_barrier(jnp.mean(norm_grad * normed_two, axis=-1, keepdims=True))
    residual_grad = inverse_rms * (norm_grad - first_moment - normed_two * second_moment)
    activation_grad = (residual_grad * modulations[:, 2:3, :]).reshape(images * tokens, model_width)
    preact_grad = gelu_grad(preactivation, activation_grad).astype(jnp.bfloat16)
    return lax.dot_general(shaped, preact_grad, (((0,), (0,)), ((), ())), preferred_element_type=jnp.float32)

def reference(gen_noise, score_noise, gen_steps, score_steps, gen_embed, gen_modulation, gen_proj, gen_final, teacher_embed, teacher_modulation, teacher_proj, teacher_final, fake_embed, fake_modulation, fake_proj, fake_final):
    loss_scale = 1.0 / math.sqrt(IMAGES * S)
    gen_time, gen_cond = time_features(gen_steps)
    score_time, score_cond = time_features(score_steps)
    gen_mods = modulate(gen_cond, gen_modulation)
    teacher_mods = modulate(score_cond, teacher_modulation)
    fake_mods = modulate(score_cond, fake_modulation)
    gen_velocity, gen_stored = forward(gen_noise, gen_mods, gen_embed, gen_proj, gen_final)
    samples = gen_noise.astype(jnp.float32) - gen_time[:, None, None] * gen_velocity
    noise_values = score_noise.astype(jnp.float32)
    noise_time = score_time[:, None, None]
    noised = ((1.0 - noise_time) * samples + noise_time * noise_values).astype(jnp.bfloat16)
    teacher_vel, _ = forward(noised, teacher_mods, teacher_embed, teacher_proj, teacher_final)
    fake_vel, fake_stored = forward(noised, fake_mods, fake_embed, fake_proj, fake_final)
    distance = jnp.abs(samples - noised.astype(jnp.float32) + noise_time * teacher_vel)
    gap = lax.optimization_barrier(jnp.mean(distance, axis=(1, 2))) + gap_epsilon
    gen_cot = -(gen_time[:, None, None] * noise_time * loss_scale) * (teacher_vel - fake_vel) / gap[:, None, None]
    fake_cot = loss_scale * (fake_vel - noise_values + samples)
    gen_grad = backward(gen_cot, gen_stored, gen_mods, gen_final)
    fake_grad = backward(fake_cot, fake_stored, fake_mods, fake_final)
    return (samples, gen_grad, fake_grad)
```

```python
import functools
import math

import jax
import jax.numpy as jnp
from jax import lax
from jax.experimental import pallas as pl
from jax.experimental.pallas import tpu as pltpu
from jax.sharding import Mesh
from jax.sharding import PartitionSpec as P

S = 4096
STEPS = 1000
D = 3072
C = 64
IMAGES = 3

norm_epsilon = 1e-06
gap_epsilon = 1e-05

F32 = jnp.float32
BF16 = jnp.bfloat16

XY = ("x", "y")
XHY = ("x", "h", "y")
COMBINE = ("h", "g", "s")
OWNERS = 16
TOKENS = 256
HALF = 128
OWNED = 16
ROWS = 96
WIDE = 128
NARROW = 64
COLS = WIDE + NARROW
PACKED = 864
BLOCK = 512

SWAP_H = [(0, 1), (1, 0)]


def params():
    return pltpu.CompilerParams(vmem_limit_bytes=56 * 1024 * 1024)


def smem():
    return pl.BlockSpec(memory_space=pltpu.SMEM)


def whole(shape):
    zeros = (0,) * len(shape)
    return pl.BlockSpec(shape, lambda *_: zeros)


def dot(a, b):
    return jnp.dot(a, b, preferred_element_type=F32)


def time_features(steps, embed_width):
    times = (steps.astype(F32) + 1.0) / (STEPS + 1.0)
    half = embed_width // 2
    frequency = jnp.exp(-jnp.log(10000.0) * jnp.arange(half, dtype=F32) / half)
    angles = 1000.0 * times[:, None] * frequency[None, :]
    embedding = jnp.concatenate([jnp.cos(angles), jnp.sin(angles)], axis=1)
    return (times, jax.nn.silu(embedding).astype(BF16))


def to_row(numbers):
    shape = (numbers[0].shape[0], OWNED, 128)
    lane = lax.broadcasted_iota(jnp.int32, shape, 2)
    token = lax.broadcasted_iota(jnp.int32, shape, 1)
    total = jnp.zeros(shape, F32)
    for k, number in enumerate(numbers):
        total = jnp.where(lane == token + OWNED * k, number, total)
    return jnp.sum(total, axis=1, keepdims=True)


def from_row(row, k):
    shape = (row.shape[0], OWNED, 128)
    lane = lax.broadcasted_iota(jnp.int32, shape, 2)
    token = lax.broadcasted_iota(jnp.int32, shape, 1)
    return jnp.sum(jnp.where(lane == token + OWNED * k, row, 0.0), axis=2, keepdims=True)


def local_lanes(load, place_ref):
    h = place_ref[0]
    tile = load(pl.ds(pl.multiple_of(place_ref[1], 128), 128))
    middle = load(pl.ds(pl.multiple_of(place_ref[2], 128), 128))
    part = jnp.where(h == 0, middle[:, :NARROW], middle[:, NARROW:])
    return jnp.concatenate([tile, part], axis=1)


def local_rows(final_ref, place_ref):
    tile = final_ref[pl.ds(pl.multiple_of(place_ref[1], 128), 128), :]
    part = final_ref[pl.ds(pl.multiple_of(place_ref[3], 64), NARROW), :]
    return jnp.concatenate([tile, part], axis=0)


def unpack_weights(packed_ref, net, w_ref):
    for chunk in range(16):
        x, y = chunk // 4, chunk % 4
        for h in range(2):
            k = (x * 8 + h * 4 + y) * ROWS
            w_ref[k : k + ROWS, :WIDE] = packed_ref[chunk, net * 192 + h * ROWS : net * 192 + (h + 1) * ROWS, :]
            if net < 2:
                part = packed_ref[chunk, 576 + h * ROWS : 576 + (h + 1) * ROWS, net * NARROW : (net + 1) * NARROW]
            else:
                part = packed_ref[chunk, 768:864, h * NARROW : (h + 1) * NARROW]
            w_ref[k : k + ROWS, WIDE:] = part


def forward(x, embed_ref, mods_ref, final_ref, w_ref, hidden_ref, shaped_ref, place_ref):
    sums = jnp.zeros((TOKENS, 128), F32)
    squares = jnp.zeros((TOKENS, 128), F32)
    for b in range(D // BLOCK):
        cut = slice(b * BLOCK, (b + 1) * BLOCK)
        hidden = dot(x, embed_ref[:, cut])
        hidden_ref[:, cut] = hidden
        for j in range(BLOCK // 128):
            piece = hidden[:, j * 128 : (j + 1) * 128]
            sums = sums + piece
            squares = squares + piece * piece
    average = jnp.sum(sums, axis=1, keepdims=True) / D
    square = jnp.sum(squares, axis=1, keepdims=True) / D
    inverse = lax.rsqrt(square - average * average + norm_epsilon)
    preactivation = jnp.zeros((TOKENS, COLS), F32)
    for b in range(D // BLOCK):
        cut = slice(b * BLOCK, (b + 1) * BLOCK)
        normed = (hidden_ref[:, cut] - average) * inverse
        shaped = (normed * (1.0 + mods_ref[0, 1:2, cut]) + mods_ref[0, 0:1, cut]).astype(BF16)
        shaped_ref[:, cut] = shaped
        preactivation = preactivation + dot(shaped, w_ref[cut, :])
    activated = jax.nn.gelu(preactivation, approximate=True).astype(BF16).astype(F32)
    own_hidden = dot(x, local_lanes(lambda at: embed_ref[:, at], place_ref))
    gate = local_lanes(lambda at: mods_ref[0, 2:3, at], place_ref)
    scale = local_lanes(lambda at: mods_ref[0, 4:5, at], place_ref)
    residual = own_hidden + gate * activated
    total = jnp.sum(residual, axis=1, keepdims=True)
    total_square = jnp.sum(residual * residual, axis=1, keepdims=True)
    own_mean = total / COLS
    final = local_rows(final_ref, place_ref)
    centred = ((residual - own_mean) * (1.0 + scale)).astype(BF16)
    ones = jnp.ones((8, COLS), BF16)
    column = dot(jnp.concatenate([ones, jnp.broadcast_to(scale, (8, COLS)).astype(BF16)], axis=0), final)
    column = column[0:1] + column[8:9]
    partial = dot(centred, final) + own_mean * column
    return preactivation, residual, partial, total, total_square


def owned(value):
    return value.reshape(OWNERS, OWNED, value.shape[-1])


def final_sums(mods_ref, final_ref):
    scales = [mods_ref[i, 4:5, :] for i in range(IMAGES)]
    shifts = [mods_ref[i, 3:4, :] for i in range(IMAGES)]
    left = jnp.concatenate(scales + shifts + [jnp.ones((2, D), F32)], axis=0).astype(BF16)
    sums = dot(left, final_ref[...])
    return [sums[i : i + 1] + sums[6:7] for i in range(IMAGES)], [sums[3 + i : 4 + i] for i in range(IMAGES)]


def pack_kernel(place_ref, *refs):
    mine, other, out_ref = refs[:3], refs[3], refs[4]
    h = place_ref[0]

    def half(block, which):
        return jnp.where(which == 0, block[:, :NARROW], block[:, NARROW:])

    tiles, parts = [], []
    for n in range(3):
        block = mine[n][...]
        tile = jnp.where(h == 0, block[:, :128], block[:, 256:])
        part = half(block[:, 128:256], h)
        sent = other[n]
        if n < 2:
            sent_part = other[3][:, n * NARROW : (n + 1) * NARROW]
        else:
            sent_part = other[4][:, :NARROW]
        tiles.append(jnp.where(h == 0, tile, sent))
        tiles.append(jnp.where(h == 0, sent, tile))
        parts.append((jnp.where(h == 0, part, sent_part), jnp.where(h == 0, sent_part, part)))
    low = jnp.concatenate([parts[0][0], parts[1][0]], axis=1)
    high = jnp.concatenate([parts[0][1], parts[1][1]], axis=1)
    last = jnp.concatenate([parts[2][0], parts[2][1]], axis=1)
    out_ref[0] = jnp.concatenate(tiles + [low, high, last], axis=0)


def generator_kernel(place_ref, own_ref, other_ref, embed_ref, mods_ref, final_ref, packed_ref,
                     part_ref, shaped_ref, pre_ref, res_ref, w_ref, hidden_ref):
    i = pl.program_id(0)
    h = place_ref[0]

    @pl.when(i == 0)
    def _():
        unpack_weights(packed_ref, 0, w_ref)
        part_ref[:, 24:32, :] = jnp.zeros((OWNERS, 8, 128), F32)

    own, other = own_ref[0], other_ref[0]
    x = jnp.concatenate([jnp.where(h == 0, own, other), jnp.where(h == 0, other, own)], axis=0)
    pre, res, partial, total, square = forward(
        x, embed_ref, mods_ref, final_ref, w_ref, hidden_ref, shaped_ref.at[0], place_ref
    )
    pre_ref[0] = pre
    res_ref[0] = res
    pieces = owned(partial)
    part_ref[:, pl.ds(pl.multiple_of(i * 8, 8), 8), :] = jnp.concatenate([pieces[:, :8], pieces[:, 8:]], axis=2)
    part_ref[:, pl.ds(24 + i, 1), :] = to_row([owned(total), owned(square)])


def samples_kernel(place_ref, time_ref, got_ref, noise_ref, mods_ref, final_ref,
                   out_ref, keep_ref, sums_ref):
    total = jnp.sum(got_ref[...], axis=0)
    scales, shifts = final_sums(mods_ref, final_ref)
    packed = []
    for i in range(IMAGES):
        block = total[8 * i : 8 * i + 8]
        partial = jnp.concatenate([block[:, :C], block[:, C:]], axis=0)
        row = total[24 + i : 25 + i][None]
        average = from_row(row, 0)[0] / D
        square = from_row(row, 1)[0] / D
        inverse = lax.rsqrt(square - average * average + norm_epsilon)
        inner = inverse * (partial - average * scales[i])
        velocity = inner + shifts[i]
        noise = noise_ref[i, pl.ds(pl.multiple_of(place_ref[4], 16), OWNED), :].astype(F32)
        samples = noise - time_ref[i] * velocity
        packed.append(jnp.concatenate([samples[:8], samples[8:]], axis=1))
        at = slice(i * OWNED, (i + 1) * OWNED)
        keep_ref[0, at, :] = samples
        keep_ref[1, at, :] = inner
        keep_ref[2, at, :] = jnp.broadcast_to(average, (OWNED, C))
        keep_ref[3, at, :] = jnp.broadcast_to(inverse, (OWNED, C))
    sums_ref[...] = jnp.concatenate(scales + [jnp.zeros((5, C), F32)], axis=0)
    out_ref[...] = jnp.broadcast_to(jnp.concatenate(packed, axis=0)[None], out_ref.shape)


def mix(samples, noise, t):
    return ((1.0 - t) * samples + t * noise).astype(BF16)


def score_kernel(place_ref, time_ref, got_ref, own_ref, other_ref,
                 t_embed_ref, f_embed_ref, t_mods_ref, f_mods_ref, t_final_ref, f_final_ref, packed_ref,
                 part_ref, samples_ref, shaped_ref, pre_ref, res_ref,
                 t_w_ref, f_w_ref, hidden_ref, t_shaped_ref):
    i = pl.program_id(0)
    h = place_ref[0]

    @pl.when(i == 0)
    def _():
        unpack_weights(packed_ref, 1, t_w_ref)
        unpack_weights(packed_ref, 2, f_w_ref)
        part_ref[:, 48:56, :] = jnp.zeros((OWNERS, 8, 128), F32)

    got = got_ref[:, pl.ds(pl.multiple_of(i * 8, 8), 8), :]
    samples = jnp.concatenate([got[:, :, :C], got[:, :, C:]], axis=1).reshape(TOKENS, C)
    samples_ref[0] = jnp.where(h == 0, samples[:HALF], samples[HALF:])
    own, other = own_ref[0].astype(F32), other_ref[0].astype(F32)
    noise = jnp.concatenate([jnp.where(h == 0, own, other), jnp.where(h == 0, other, own)], axis=0)
    noised = mix(samples, noise, time_ref[i])
    _, _, t_partial, t_total, t_square = forward(
        noised, t_embed_ref, t_mods_ref, t_final_ref, t_w_ref, hidden_ref, t_shaped_ref, place_ref
    )
    pre, res, f_partial, f_total, f_square = forward(
        noised, f_embed_ref, f_mods_ref, f_final_ref, f_w_ref, hidden_ref, shaped_ref.at[0], place_ref
    )
    pre_ref[0] = pre
    res_ref[0] = res
    part_ref[:, pl.ds(pl.multiple_of(i * 16, 16), 16), :] = owned(jnp.concatenate([t_partial, f_partial], axis=1))
    part_ref[:, pl.ds(48 + i, 1), :] = to_row([owned(v) for v in (t_total, t_square, f_total, f_square)])


def cotangent_kernel(place_ref, gen_time_ref, time_ref, got_ref, noise_ref, keep_ref, sums_ref,
                     t_mods_ref, f_mods_ref, t_final_ref, f_final_ref, out_ref):
    loss_scale = 1.0 / math.sqrt(IMAGES * S)
    total = jnp.sum(got_ref[...], axis=0)
    t_scales, t_shifts = final_sums(t_mods_ref, t_final_ref)
    f_scales, f_shifts = final_sums(f_mods_ref, f_final_ref)
    lane = lax.broadcasted_iota(jnp.int32, (1, 128), 1)
    cots, rows = [], []
    for i in range(IMAGES):
        block = total[16 * i : 16 * i + 16]
        row = total[48 + i : 49 + i][None]

        def inner(partial, k, scale):
            average = from_row(row, k)[0] / D
            square = from_row(row, k + 1)[0] / D
            inverse = lax.rsqrt(square - average * average + norm_epsilon)
            return inverse * (partial - average * scale), average, inverse

        t_inner, _, _ = inner(block[:, :C], 0, t_scales[i])
        f_inner, f_average, f_inverse = inner(block[:, C:], 2, f_scales[i])
        teacher, fake = t_inner + t_shifts[i], f_inner + f_shifts[i]
        at = slice(i * OWNED, (i + 1) * OWNED)
        samples, g_inner = keep_ref[0, at, :], keep_ref[1, at, :]
        g_average, g_inverse = keep_ref[2, at, 0:1], keep_ref[3, at, 0:1]
        noise = noise_ref[i, pl.ds(pl.multiple_of(place_ref[4], 16), OWNED), :].astype(F32)
        t = time_ref[i]
        noised = mix(samples, noise, t).astype(F32)
        distance = jnp.sum(jnp.abs(samples - noised + t * teacher))
        gen_cot = (-(gen_time_ref[i] * t * loss_scale) * (teacher - fake)).astype(BF16).astype(F32)
        fake_cot = (loss_scale * (fake - noise + samples)).astype(BF16).astype(F32)
        numbers = []
        for cot, column, value, average, inverse in (
            (fake_cot, f_scales[i], f_inner, f_average, f_inverse),
            (gen_cot, sums_ref[i : i + 1, :], g_inner, g_average, g_inverse),
        ):
            first = jnp.sum(cot * column, axis=1, keepdims=True) / D
            second = jnp.sum(cot * value, axis=1, keepdims=True) / D
            slope = inverse * inverse * second
            numbers += [inverse, slope, average * slope - inverse * first]
        cots.append(jnp.concatenate([fake_cot, gen_cot], axis=1))
        numbers_row = to_row([number[None] for number in numbers])[0]
        numbers_row = jnp.where(lane == 96, distance, numbers_row)
        for _ in range(3):
            rounded = numbers_row.astype(BF16).astype(F32)
            rows.append(rounded)
            numbers_row = numbers_row - rounded
    rows.append(jnp.zeros((7, 128), F32))
    packed = jnp.concatenate(cots + rows, axis=0).astype(BF16)
    out_ref[...] = jnp.broadcast_to(packed[None], out_ref.shape)


def gelu_slope(v):
    a, b = math.sqrt(2.0 / math.pi), 0.044715
    t = jnp.tanh(a * (v + b * (v * v * v)))
    return 0.5 * (1.0 + t) + 0.5 * v * (1.0 - t * t) * (a * (1.0 + 3.0 * b * (v * v)))


def gradient_kernel(place_ref, got_ref, gap_ref, f_mods_ref, g_mods_ref, f_final_ref, g_final_ref,
                    f_pre_ref, f_res_ref, g_pre_ref, g_res_ref, f_shaped_ref, g_shaped_ref,
                    out_ref, f_left_ref, g_left_ref):
    @pl.when(pl.program_id(0) == 0)
    def _():
        gaps = jnp.sum(gap_ref[...], axis=0)
        for i in range(IMAGES):
            inverse_gap = 1.0 / (gaps[i : i + 1, :] / (S * C) + gap_epsilon)
            inverse_gap = jnp.concatenate([inverse_gap, inverse_gap[:, :NARROW]], axis=1)
            cots = got_ref[:, 16 * i : 16 * i + 16, :].reshape(TOKENS, 128)
            row = got_ref[:, 48:64, :].astype(F32)
            row = row[:, 3 * i : 3 * i + 1] + row[:, 3 * i + 1 : 3 * i + 2] + row[:, 3 * i + 2 : 3 * i + 3]
            for net, (mods_ref, final_ref, pre_ref, res_ref, left_ref) in enumerate((
                (f_mods_ref, f_final_ref, f_pre_ref, f_res_ref, f_left_ref),
                (g_mods_ref, g_final_ref, g_pre_ref, g_res_ref, g_left_ref),
            )):
                inverse, slope, offset = [from_row(row, 3 * net + k).reshape(TOKENS, 1) for k in range(3)]
                final = local_rows(final_ref, place_ref)
                cot = cots[:, net * C : (net + 1) * C]
                out_grad = lax.dot_general(cot, final, (((1,), (1,)), ((), ())), preferred_element_type=F32)
                scale = local_lanes(lambda at: mods_ref[i, 4:5, at], place_ref)
                gate = local_lanes(lambda at: mods_ref[i, 2:3, at], place_ref)
                res_grad = inverse * (out_grad * (1.0 + scale)) - slope * res_ref[i] + offset
                act_grad = res_grad * gate
                if net == 1:
                    act_grad = act_grad * inverse_gap
                grad = act_grad * gelu_slope(pre_ref[i])
                turned = jnp.concatenate([grad, jnp.zeros((TOKENS, NARROW), F32)], axis=1).T
                left_ref[:, i * TOKENS : (i + 1) * TOKENS] = turned[:COLS].astype(BF16)

    f_grad = dot(f_left_ref[...], f_shaped_ref[...].reshape(IMAGES * TOKENS, 768))
    g_grad = dot(g_left_ref[...], g_shaped_ref[...].reshape(IMAGES * TOKENS, 768))
    narrow = jnp.concatenate([f_grad[WIDE:], g_grad[WIDE:]], axis=0)
    for n, block in enumerate((f_grad[:WIDE], g_grad[:WIDE], narrow)):
        turned = block.T.astype(BF16)
        for h in range(2):
            for y in range(4):
                k = (h * 4 + y) * ROWS
                out_ref[y, n, h * ROWS : (h + 1) * ROWS, :] = turned[k : k + ROWS]


def sum_kernel(place_ref, got_ref, keep_ref, send_ref):
    h = place_ref[0]
    total = got_ref[0, 0].astype(F32)
    for k in range(1, 16):
        total = total + got_ref[k, 0].astype(F32)
    keep_ref[0] = jnp.where(h == 0, total[:ROWS], total[ROWS:])
    send_ref[0] = jnp.where(h == 0, total[ROWS:], total[:ROWS])


def place_kernel(place_ref, keep_ref, other_ref, gen_ref, fake_ref):
    h = place_ref[0]

    def ordered(n):
        keep, other = keep_ref[n], other_ref[n]
        return jnp.where(h == 0, keep, other), jnp.where(h == 0, other, keep)

    low, high = ordered(2)
    for n, ref in enumerate((fake_ref, gen_ref)):
        first, last = ordered(n)
        part = slice(n * NARROW, (n + 1) * NARROW)
        ref[:, :128] = first
        ref[:, 128:256] = jnp.concatenate([low[:, part], high[:, part]], axis=1)
        ref[:, 256:] = last


def exchange(value, axes):
    return lax.all_to_all(value, axes, 0, 0)


def shards(
    gen_noise,
    score_noise,
    gen_steps,
    score_steps,
    gen_embed,
    gen_modulation,
    gen_proj,
    gen_final,
    teacher_embed,
    teacher_modulation,
    teacher_proj,
    teacher_final,
    fake_embed,
    fake_modulation,
    fake_proj,
    fake_final,
):
    h = lax.axis_index("h")
    member = lax.axis_index(("g", "s"))
    start = member * 384
    place = jnp.stack([h, start + 256 * h, start + 128, start + 128 + 64 * h, member * OWNED]).astype(jnp.int32)

    gen_time, gen_cond = time_features(gen_steps, gen_modulation.shape[0])
    score_time, score_cond = time_features(score_steps, gen_modulation.shape[0])
    own_mods = jnp.concatenate(
        [
            dot(gen_cond, gen_modulation),
            dot(score_cond, teacher_modulation),
            dot(score_cond, fake_modulation),
        ],
        axis=0,
    ).astype(BF16)
    mods = lax.all_gather(own_mods, XHY, axis=1, tiled=True)
    mods = jnp.pad(mods.astype(F32).reshape(9, 5, D), ((0, 0), (0, 3), (0, 0)))

    projections = (gen_proj, teacher_proj, fake_proj)
    sent = [jnp.where(h == 0, w[:, 256:], w[:, :128]) for w in projections]
    parts = [jnp.where(h == 0, w[:, 192:256], w[:, 128:192]) for w in projections]
    sent.append(jnp.concatenate(parts[:2], axis=1))
    sent.append(jnp.concatenate([parts[2], parts[2]], axis=1))
    other_w = lax.ppermute(jnp.stack(sent), "h", SWAP_H)
    other_noise = lax.ppermute(jnp.stack([gen_noise, score_noise]), "h", SWAP_H)

    packed = pl.pallas_call(
        pack_kernel,
        grid=(16,),
        in_specs=[smem()] + [whole((96, 384))] * 3 + [whole((5, 96, 128))],
        out_specs=pl.BlockSpec((1, PACKED, 128), lambda i: (i, 0, 0)),
        out_shape=jax.ShapeDtypeStruct((16, PACKED, 128), BF16),
        compiler_params=params(),
        name="pack",
    )(place, *projections, other_w)
    packed = exchange(packed, XY)

    by_image = lambda *shape: pl.BlockSpec((1, *shape), lambda i: (i,) + (0,) * len(shape))
    mods_of = lambda net: pl.BlockSpec((1, 8, D), lambda i: (3 * net + i, 0, 0))
    local = jax.ShapeDtypeStruct((IMAGES, TOKENS, COLS), F32)
    wide = jax.ShapeDtypeStruct((IMAGES, TOKENS, D), BF16)

    part, g_shaped, g_pre, g_res = pl.pallas_call(
        generator_kernel,
        grid=(IMAGES,),
        in_specs=[
            smem(), by_image(HALF, C), by_image(HALF, C), whole((C, D)), mods_of(0), whole((D, C)),
            whole((16, PACKED, 128)),
        ],
        out_specs=[whole((OWNERS, 32, 128)), by_image(TOKENS, D), by_image(TOKENS, COLS), by_image(TOKENS, COLS)],
        out_shape=[jax.ShapeDtypeStruct((OWNERS, 32, 128), F32), wide, local, local],
        scratch_shapes=[pltpu.VMEM((D, COLS), BF16), pltpu.VMEM((TOKENS, D), F32)],
        compiler_params=params(),
        name="generator",
    )(place, gen_noise, other_noise[0], gen_embed, mods, gen_final, packed)
    part = exchange(part, COMBINE)

    net_mods = lambda net: pl.BlockSpec((IMAGES, 8, D), lambda *_: (net, 0, 0))
    pack1, keep, sums = pl.pallas_call(
        samples_kernel,
        grid=(1,),
        in_specs=[
            smem(), smem(), whole((OWNERS, 32, 128)), whole((IMAGES, HALF, C)), net_mods(0), whole((D, C)),
        ],
        out_specs=[whole((OWNERS, 24, 128)), whole((4, 48, C)), whole((8, C))],
        out_shape=[
            jax.ShapeDtypeStruct((OWNERS, 24, 128), F32),
            jax.ShapeDtypeStruct((4, 48, C), F32),
            jax.ShapeDtypeStruct((8, C), F32),
        ],
        compiler_params=params(),
        name="samples",
    )(place, gen_time, part, gen_noise, mods, gen_final)
    pack1 = exchange(pack1, COMBINE)

    part2, samples, f_shaped, f_pre, f_res = pl.pallas_call(
        score_kernel,
        grid=(IMAGES,),
        in_specs=[
            smem(), smem(), whole((OWNERS, 24, 128)), by_image(HALF, C), by_image(HALF, C),
            whole((C, D)), whole((C, D)), mods_of(1), mods_of(2), whole((D, C)), whole((D, C)),
            whole((16, PACKED, 128)),
        ],
        out_specs=[
            whole((OWNERS, 56, 128)), by_image(HALF, C), by_image(TOKENS, D), by_image(TOKENS, COLS),
            by_image(TOKENS, COLS),
        ],
        out_shape=[
            jax.ShapeDtypeStruct((OWNERS, 56, 128), F32),
            jax.ShapeDtypeStruct((IMAGES, HALF, C), F32),
            wide, local, local,
        ],
        scratch_shapes=[
            pltpu.VMEM((D, COLS), BF16), pltpu.VMEM((D, COLS), BF16), pltpu.VMEM((TOKENS, D), F32),
            pltpu.VMEM((TOKENS, D), BF16),
        ],
        compiler_params=params(),
        name="score",
    )(place, score_time, pack1, score_noise, other_noise[1], teacher_embed, fake_embed, mods, mods,
      teacher_final, fake_final, packed)
    part2 = exchange(part2, COMBINE)

    pack2 = pl.pallas_call(
        cotangent_kernel,
        grid=(1,),
        in_specs=[
            smem(), smem(), smem(), whole((OWNERS, 56, 128)), whole((IMAGES, HALF, C)), whole((4, 48, C)),
            whole((8, C)), net_mods(1), net_mods(2), whole((D, C)), whole((D, C)),
        ],
        out_specs=whole((OWNERS, 64, 128)),
        out_shape=jax.ShapeDtypeStruct((OWNERS, 64, 128), BF16),
        compiler_params=params(),
        name="cotangents",
    )(place, gen_time, score_time, part2, score_noise, keep, sums, mods, mods, teacher_final, fake_final)
    pack2 = exchange(pack2, COMBINE)

    gap = jnp.sum(pack2[:, 48:57, 96].astype(F32).reshape(OWNERS, 3, 3), axis=(0, 2))
    gap = jnp.broadcast_to(jnp.pad(gap, (0, 5))[None, :, None], (16, 8, 128))
    gap = exchange(gap, XY)

    by_columns = pl.BlockSpec((IMAGES, TOKENS, 768), lambda x: (0, 0, x))
    grads = pl.pallas_call(
        gradient_kernel,
        grid=(4,),
        in_specs=[
            smem(), whole((OWNERS, 64, 128)), whole((16, 8, 128)), net_mods(2), net_mods(0), whole((D, C)),
            whole((D, C)), *([whole((IMAGES, TOKENS, COLS))] * 4), by_columns, by_columns,
        ],
        out_specs=pl.BlockSpec((4, 3, 192, 128), lambda x: (x, 0, 0, 0)),
        out_shape=jax.ShapeDtypeStruct((16, 3, 192, 128), BF16),
        scratch_shapes=[pltpu.VMEM((COLS, IMAGES * TOKENS), BF16)] * 2,
        compiler_params=params(),
        name="gradients",
    )(place, pack2, gap, mods, mods, fake_final, gen_final, f_pre, f_res, g_pre, g_res, f_shaped, g_shaped)
    grads = exchange(grads, XY)

    tile = jax.ShapeDtypeStruct((3, ROWS, 128), F32)
    tile_spec = pl.BlockSpec((1, ROWS, 128), lambda n: (n, 0, 0))
    kept, sent = pl.pallas_call(
        sum_kernel,
        grid=(3,),
        in_specs=[smem(), pl.BlockSpec((16, 1, 192, 128), lambda n: (0, n, 0, 0))],
        out_specs=[tile_spec, tile_spec],
        out_shape=[tile, tile],
        compiler_params=params(),
        name="add",
    )(place, grads)
    other = lax.ppermute(sent, "h", SWAP_H)
    gen_grad, fake_grad = pl.pallas_call(
        place_kernel,
        grid=(1,),
        in_specs=[smem(), whole((3, ROWS, 128)), whole((3, ROWS, 128))],
        out_specs=[whole((ROWS, 384))] * 2,
        out_shape=[jax.ShapeDtypeStruct((ROWS, 384), F32)] * 2,
        compiler_params=params(),
        name="place",
    )(place, kept, other)
    return (samples, gen_grad, fake_grad)


def solution(mesh):
    split = Mesh(mesh.devices.reshape(4, 4, 2, 4, 2), ("g", "x", "h", "y", "s"))
    tokens = P(None, XHY, None)
    columns = P(None, XHY)
    block = P(XHY, ("g", "s"))
    net = (P(), columns, block, P())
    return jax.shard_map(
        shards,
        mesh=split,
        in_specs=(tokens, tokens, P(), P(), *net, *net, *net),
        out_specs=(tokens, block, block),
        check_vma=False,
    )
```

```python
import functools
import math

import jax
import jax.numpy as jnp
from jax import lax
from jax.experimental import pallas as pl
from jax.experimental.pallas import tpu as pltpu
from jax.sharding import Mesh
from jax.sharding import PartitionSpec as P

S = 4096
STEPS = 1000
D = 3072
C = 64
IMAGES = 3

norm_epsilon = 1e-06
gap_epsilon = 1e-05

F32 = jnp.float32
BF16 = jnp.bfloat16

GATHER = ("x", "w")
ROW_AXES = ("x", "h", "v", "w")
COMBINE = ("v", "h", "g")
TOKEN_AXES = ("x", "w", "s")
OWNERS = 16
TOKENS = 256
HALF = 128
OWNED = 16
ROWS = 96
WIDE = 128
NARROW = 64
COLS = WIDE + NARROW
GEN_ROWS = 288
NOISE_ROWS = 384
MODS_AT = 864
MODS_ROWS = 36
SENT_ROWS = 912
GEN_CHUNK = 368
SCORE_ROWS = 576
CHUNKS = 8
BLOCK = 512

PLACES = ("h", "v", "s")
SWAP = [(h * 4 + v * 2 + s, s * 4 + v * 2 + h) for h in range(2) for v in range(2) for s in range(2)]
SWAP_TURNED = [(h * 4 + v * 2 + s, s * 4 + (1 - v) * 2 + h) for h in range(2) for v in range(2) for s in range(2)]
SIBLING = [(0, 1), (1, 0)]


def params(mib):
    return pltpu.CompilerParams(vmem_limit_bytes=mib * 1024 * 1024)


def smem():
    return pl.BlockSpec(memory_space=pltpu.SMEM)


def whole(shape):
    zeros = (0,) * len(shape)
    return pl.BlockSpec(shape, lambda *_: zeros)


def dot(a, b):
    return jnp.dot(a, b, preferred_element_type=F32)


def dot_turned(a, b):
    return lax.dot_general(a, b, (((1,), (1,)), ((), ())), preferred_element_type=F32)


def time_features(steps, embed_width):
    times = (steps.astype(F32) + 1.0) / (STEPS + 1.0)
    half = embed_width // 2
    frequency = jnp.exp(-jnp.log(10000.0) * jnp.arange(half, dtype=F32) / half)
    angles = 1000.0 * times[:, None] * frequency[None, :]
    embedding = jnp.concatenate([jnp.cos(angles), jnp.sin(angles)], axis=1)
    return (times, jax.nn.silu(embedding).astype(BF16))


def to_row(numbers):
    shape = (numbers[0].shape[0], OWNED, 128)
    lane = lax.broadcasted_iota(jnp.int32, shape, 2)
    token = lax.broadcasted_iota(jnp.int32, shape, 1)
    total = jnp.zeros(shape, F32)
    for k, number in enumerate(numbers):
        total = jnp.where(lane == token + OWNED * k, number, total)
    return jnp.sum(total, axis=1, keepdims=True)


def from_row(row, k):
    shape = (row.shape[0], OWNED, 128)
    lane = lax.broadcasted_iota(jnp.int32, shape, 2)
    token = lax.broadcasted_iota(jnp.int32, shape, 1)
    return jnp.sum(jnp.where(lane == token + OWNED * k, row, 0.0), axis=2, keepdims=True)


def local_lanes(load, place_ref):
    tile = load(pl.ds(pl.multiple_of(place_ref[1], 128), 128))
    middle = load(pl.ds(pl.multiple_of(place_ref[2], 128), 128))
    part = jnp.where(place_ref[0] == 0, middle[:, :NARROW], middle[:, NARROW:])
    return jnp.concatenate([tile, part], axis=1)


def unpack_weights(place_ref, own_ref, other_ref, net, w_ref):
    s = place_ref[4]
    for packed_ref, side in ((own_ref, s), (other_ref, 1 - s)):
        for chunk in range(CHUNKS):
            x, w = chunk // 2, chunk % 2
            for v in range(2):
                k = pl.multiple_of((x * 8 + v * 2 + w) * ROWS + side * (4 * ROWS), 32)
                first = max(net - 1, 0) * 192 + v * ROWS
                w_ref[pl.ds(k, ROWS), :WIDE] = packed_ref[chunk, first : first + ROWS, :]
                if net == 0:
                    part = packed_ref[chunk, 192:288, v * NARROW : (v + 1) * NARROW]
                else:
                    part = packed_ref[chunk, 384 + v * ROWS : 384 + (v + 1) * ROWS, (net - 1) * NARROW : net * NARROW]
                w_ref[pl.ds(k, ROWS), WIDE:] = part


def forward(x, embed_ref, mods_ref, final_ref, w_ref, hidden_ref, shaped_ref, place_ref):
    sums = jnp.zeros((TOKENS, 128), F32)
    squares = jnp.zeros((TOKENS, 128), F32)
    for b in range(D // BLOCK):
        cut = slice(b * BLOCK, (b + 1) * BLOCK)
        hidden = dot(x, embed_ref[:, cut])
        hidden_ref[:, cut] = hidden
        for j in range(BLOCK // 128):
            piece = hidden[:, j * 128 : (j + 1) * 128]
            sums = sums + piece
            squares = squares + piece * piece
    average = jnp.sum(sums, axis=1, keepdims=True) / D
    square = jnp.sum(squares, axis=1, keepdims=True) / D
    inverse = lax.rsqrt(square - average * average + norm_epsilon)
    preactivation = jnp.zeros((TOKENS, COLS), F32)
    for b in range(D // BLOCK):
        cut = slice(b * BLOCK, (b + 1) * BLOCK)
        normed = (hidden_ref[:, cut] - average) * inverse
        shaped = (normed * (1.0 + mods_ref[0, 1:2, cut]) + mods_ref[0, 0:1, cut]).astype(BF16)
        shaped_ref[:, cut] = shaped
        preactivation = preactivation + dot(shaped, w_ref[cut, :])
    activated = jax.nn.gelu(preactivation, approximate=True).astype(BF16).astype(F32)
    own_hidden = dot(x, local_lanes(lambda at: embed_ref[:, at], place_ref))
    gate = local_lanes(lambda at: mods_ref[0, 2:3, at], place_ref)
    scale = local_lanes(lambda at: mods_ref[0, 4:5, at], place_ref)
    residual = own_hidden + gate * activated
    total = jnp.sum(residual, axis=1, keepdims=True)
    total_square = jnp.sum(residual * residual, axis=1, keepdims=True)
    own_mean = total / COLS
    final = local_lanes(lambda at: final_ref[:, at], place_ref)
    centred = ((residual - own_mean) * (1.0 + scale)).astype(BF16)
    ones = jnp.ones((8, COLS), BF16)
    column = dot_turned(jnp.concatenate([ones, jnp.broadcast_to(scale, (8, COLS)).astype(BF16)], axis=0), final)
    column = column[0:1] + column[8:9]
    partial = dot_turned(centred, final) + own_mean * column
    return preactivation, residual, partial, total, total_square


def owned(value):
    return value.reshape(OWNERS, OWNED, value.shape[-1])


def final_sums(mods_ref, final_ref):
    scales = [mods_ref[i, 4:5, :] for i in range(IMAGES)]
    shifts = [mods_ref[i, 3:4, :] for i in range(IMAGES)]
    left = jnp.concatenate(scales + shifts + [jnp.ones((2, D), F32)], axis=0).astype(BF16)
    sums = dot_turned(left, final_ref[...])
    return [sums[i : i + 1] + sums[6:7] for i in range(IMAGES)], [sums[3 + i : 4 + i] for i in range(IMAGES)]


def split_kernel(place_ref, cond_ref, gen_noise_ref, score_noise_ref, gen_ref, teacher_ref, fake_ref,
                 gen_mod_ref, teacher_mod_ref, fake_mod_ref, mine_ref, other_ref):
    for i in range(IMAGES):
        noise = jnp.concatenate([gen_noise_ref[i], score_noise_ref[i]], axis=0).astype(F32).T.astype(BF16)
        mine_ref[i * HALF : (i + 1) * HALF] = noise
        other_ref[i * HALF : (i + 1) * HALF] = noise
    cond = cond_ref[...]
    mods = [dot_turned(cond, ref[...]) for ref in (gen_mod_ref, teacher_mod_ref, fake_mod_ref)]
    mods = jnp.concatenate([mods[0][0:3], mods[1][3:6], mods[2][3:6]], axis=0)
    mods = jnp.concatenate([mods, jnp.zeros((9, 32), F32)], axis=1)
    mods = jnp.concatenate([mods[:, 128 * p : 128 * (p + 1)] for p in range(4)] + [jnp.zeros((12, 128), F32)], axis=0)
    mine_ref[MODS_AT:] = mods.astype(BF16)
    other_ref[MODS_AT:] = mods.astype(BF16)
    first = place_ref[0] == 0
    mine, other = [], []
    for n, ref in enumerate((gen_ref, teacher_ref, fake_ref)):
        rows = slice(NOISE_ROWS + n * ROWS, NOISE_ROWS + (n + 1) * ROWS)
        low, high = ref[:, :128], ref[:, 256:]
        mine_ref[rows] = jnp.where(first, low, high)
        other_ref[rows] = jnp.where(first, high, low)
        low, high = ref[:, 128:192], ref[:, 192:256]
        mine.append(jnp.where(first, low, high))
        other.append(jnp.where(first, high, low))
    for ref, parts in ((mine_ref, mine), (other_ref, other)):
        ref[NOISE_ROWS + 3 * ROWS : NOISE_ROWS + 4 * ROWS] = jnp.concatenate(parts[1:], axis=1)
        ref[NOISE_ROWS + 4 * ROWS : MODS_AT] = jnp.concatenate([parts[0], parts[0]], axis=1)


def in_order(v, mine, other):
    return jnp.where(v == 0, mine, other), jnp.where(v == 0, other, mine)


def pack_kernel(place_ref, mine_ref, other_ref, gen_ref, score_ref):
    v = place_ref[0]
    cuts = [slice(NOISE_ROWS + n * ROWS, NOISE_ROWS + (n + 1) * ROWS) for n in range(5)]
    ordered = [in_order(v, mine_ref[rows], other_ref[rows]) for rows in cuts]
    parts = jnp.concatenate([ordered[4][0][:, :NARROW], ordered[4][1][:, :NARROW]], axis=1)
    mods = in_order(v, mine_ref[MODS_AT:].astype(F32), other_ref[MODS_AT:].astype(F32))
    mods = jnp.concatenate([mods[0][:MODS_ROWS], mods[1][:MODS_ROWS], jnp.zeros((8, 128), F32)], axis=0)
    gen = jnp.concatenate([*ordered[0], parts, mods.astype(BF16)], axis=0)
    score = jnp.concatenate([*ordered[1], *ordered[2], *ordered[3]], axis=0)
    for k in range(CHUNKS):
        gen_ref[k] = gen
        score_ref[k] = score


def generator_kernel(place_ref, own_ref, other_ref, embed_ref, mods_ref, final_ref, own_w_ref, other_w_ref,
                     part_ref, shaped_ref, pre_ref, res_ref, w_ref, hidden_ref):
    i = pl.program_id(0)
    v = place_ref[0]

    @pl.when(i == 0)
    def _():
        unpack_weights(place_ref, own_w_ref, other_w_ref, 0, w_ref)
        part_ref[:, 24:32, :] = jnp.zeros((OWNERS, 8, 128), F32)

    x = jnp.concatenate(in_order(v, own_ref[:, :C], other_ref[:, :C]), axis=0)
    pre, res, partial, total, square = forward(
        x, embed_ref, mods_ref, final_ref, w_ref, hidden_ref, shaped_ref.at[0], place_ref
    )
    pre_ref[0] = pre
    res_ref[0] = res
    pieces = owned(partial)
    part_ref[:, pl.ds(pl.multiple_of(i * 8, 8), 8), :] = jnp.concatenate([pieces[:, :8], pieces[:, 8:]], axis=2)
    part_ref[:, pl.ds(24 + i, 1), :] = to_row([owned(total), owned(square)])


def samples_kernel(place_ref, time_ref, got_ref, noise_ref, mods_ref, final_ref,
                   out_ref, keep_ref, sums_ref):
    total = jnp.sum(got_ref[...], axis=0)
    scales, shifts = final_sums(mods_ref, final_ref)
    packed = []
    for i in range(IMAGES):
        block = total[8 * i : 8 * i + 8]
        partial = jnp.concatenate([block[:, :C], block[:, C:]], axis=0)
        row = total[24 + i : 25 + i][None]
        average = from_row(row, 0)[0] / D
        square = from_row(row, 1)[0] / D
        inverse = lax.rsqrt(square - average * average + norm_epsilon)
        inner = inverse * (partial - average * scales[i])
        velocity = inner + shifts[i]
        noise = noise_ref[pl.ds(pl.multiple_of(place_ref[3] + i * HALF, 16), OWNED), :][:, :C].astype(F32)
        samples = noise - time_ref[i] * velocity
        packed.append(jnp.concatenate([samples[:8], samples[8:]], axis=1))
        at = slice(i * OWNED, (i + 1) * OWNED)
        keep_ref[0, at, :] = samples
        keep_ref[1, at, :] = inner
        keep_ref[2, at, :] = jnp.broadcast_to(average, (OWNED, C))
        keep_ref[3, at, :] = jnp.broadcast_to(inverse, (OWNED, C))
    sums_ref[...] = jnp.concatenate(scales + [jnp.zeros((5, C), F32)], axis=0)
    out_ref[...] = jnp.broadcast_to(jnp.concatenate(packed, axis=0)[None], out_ref.shape)


def mix(samples, noise, t):
    return ((1.0 - t) * samples + t * noise).astype(BF16)


def score_kernel(place_ref, time_ref, got_ref, own_ref, other_ref,
                 t_embed_ref, f_embed_ref, t_mods_ref, f_mods_ref, t_final_ref, f_final_ref, own_w_ref, other_w_ref,
                 part_ref, samples_ref, shaped_ref, pre_ref, res_ref,
                 t_w_ref, f_w_ref, hidden_ref, t_shaped_ref):
    i = pl.program_id(0)
    v = place_ref[0]

    @pl.when(i == 0)
    def _():
        unpack_weights(place_ref, own_w_ref, other_w_ref, 1, t_w_ref)
        unpack_weights(place_ref, own_w_ref, other_w_ref, 2, f_w_ref)
        part_ref[:, 48:56, :] = jnp.zeros((OWNERS, 8, 128), F32)

    got = got_ref[:, pl.ds(pl.multiple_of(i * 8, 8), 8), :]
    samples = jnp.concatenate([got[:, :, :C], got[:, :, C:]], axis=1).reshape(TOKENS, C)
    turned = jnp.concatenate([samples[:HALF], samples[HALF:]], axis=1).T
    samples_ref[0] = jnp.where(v == 0, turned[:C], turned[C:])
    own, other = own_ref[:, C:].astype(F32), other_ref[:, C:].astype(F32)
    noise = jnp.concatenate(in_order(v, own, other), axis=0)
    noised = mix(samples, noise, time_ref[i])
    _, _, t_partial, t_total, t_square = forward(
        noised, t_embed_ref, t_mods_ref, t_final_ref, t_w_ref, hidden_ref, t_shaped_ref, place_ref
    )
    pre, res, f_partial, f_total, f_square = forward(
        noised, f_embed_ref, f_mods_ref, f_final_ref, f_w_ref, hidden_ref, shaped_ref.at[0], place_ref
    )
    pre_ref[0] = pre
    res_ref[0] = res
    part_ref[:, pl.ds(pl.multiple_of(i * 16, 16), 16), :] = owned(jnp.concatenate([t_partial, f_partial], axis=1))
    part_ref[:, pl.ds(48 + i, 1), :] = to_row([owned(v) for v in (t_total, t_square, f_total, f_square)])


def cotangent_kernel(place_ref, gen_time_ref, time_ref, got_ref, noise_ref, keep_ref, sums_ref,
                     t_mods_ref, f_mods_ref, t_final_ref, f_final_ref, out_ref):
    loss_scale = 1.0 / math.sqrt(IMAGES * S)
    total = jnp.sum(got_ref[...], axis=0)
    t_scales, t_shifts = final_sums(t_mods_ref, t_final_ref)
    f_scales, f_shifts = final_sums(f_mods_ref, f_final_ref)
    lane = lax.broadcasted_iota(jnp.int32, (1, 128), 1)
    cots, rows = [], []
    for i in range(IMAGES):
        block = total[16 * i : 16 * i + 16]
        row = total[48 + i : 49 + i][None]

        def inner(partial, k, scale):
            average = from_row(row, k)[0] / D
            square = from_row(row, k + 1)[0] / D
            inverse = lax.rsqrt(square - average * average + norm_epsilon)
            return inverse * (partial - average * scale), average, inverse

        t_inner, _, _ = inner(block[:, :C], 0, t_scales[i])
        f_inner, f_average, f_inverse = inner(block[:, C:], 2, f_scales[i])
        teacher, fake = t_inner + t_shifts[i], f_inner + f_shifts[i]
        at = slice(i * OWNED, (i + 1) * OWNED)
        samples, g_inner = keep_ref[0, at, :], keep_ref[1, at, :]
        g_average, g_inverse = keep_ref[2, at, 0:1], keep_ref[3, at, 0:1]
        noise = noise_ref[pl.ds(pl.multiple_of(place_ref[3] + i * HALF, 16), OWNED), :][:, C:].astype(F32)
        t = time_ref[i]
        noised = mix(samples, noise, t).astype(F32)
        distance = jnp.sum(jnp.abs(samples - noised + t * teacher))
        gen_cot = (-(gen_time_ref[i] * t * loss_scale) * (teacher - fake)).astype(BF16).astype(F32)
        fake_cot = (loss_scale * (fake - noise + samples)).astype(BF16).astype(F32)
        numbers = []
        for cot, column, value, average, inverse in (
            (fake_cot, f_scales[i], f_inner, f_average, f_inverse),
            (gen_cot, sums_ref[i : i + 1, :], g_inner, g_average, g_inverse),
        ):
            first = jnp.sum(cot * column, axis=1, keepdims=True) / D
            second = jnp.sum(cot * value, axis=1, keepdims=True) / D
            slope = inverse * inverse * second
            numbers += [inverse, slope, average * slope - inverse * first]
        cots.append(jnp.concatenate([fake_cot, gen_cot], axis=1))
        numbers_row = to_row([number[None] for number in numbers])[0]
        numbers_row = jnp.where(lane == 96, distance, numbers_row)
        for _ in range(3):
            rounded = numbers_row.astype(BF16).astype(F32)
            rows.append(rounded)
            numbers_row = numbers_row - rounded
    rows.append(jnp.zeros((7, 128), F32))
    packed = jnp.concatenate(cots + rows, axis=0).astype(BF16)
    out_ref[...] = jnp.broadcast_to(packed[None], out_ref.shape)


def gelu_slope(v):
    a, b = math.sqrt(2.0 / math.pi), 0.044715
    t = jnp.tanh(a * (v + b * (v * v * v)))
    return 0.5 * (1.0 + t) + 0.5 * v * (1.0 - t * t) * (a * (1.0 + 3.0 * b * (v * v)))


def gradient_kernel(net, place_ref, got_ref, *refs):
    gap_ref, refs = (refs[0], refs[1:]) if net == 1 else (None, refs)
    mods_ref, final_ref, pre_ref, res_ref, shaped_ref, keep_ref, send_ref, left_ref = refs

    @pl.when(pl.program_id(0) == 0)
    def _():
        final = local_lanes(lambda at: final_ref[:, at], place_ref)
        if net == 1:
            gaps = jnp.sum(gap_ref[...], axis=0)
        for i in range(IMAGES):
            row = got_ref[:, 48:64, :].astype(F32)
            row = row[:, 3 * i : 3 * i + 1] + row[:, 3 * i + 1 : 3 * i + 2] + row[:, 3 * i + 2 : 3 * i + 3]
            inverse, slope, offset = [from_row(row, 3 * net + k).reshape(TOKENS, 1) for k in range(3)]
            cot = got_ref[:, 16 * i : 16 * i + 16, :].reshape(TOKENS, 128)[:, net * C : (net + 1) * C]
            out_grad = dot(cot, final)
            scale = local_lanes(lambda at: mods_ref[i, 4:5, at], place_ref)
            gate = local_lanes(lambda at: mods_ref[i, 2:3, at], place_ref)
            res_grad = inverse * (out_grad * (1.0 + scale)) - slope * res_ref[i] + offset
            act_grad = res_grad * gate
            if net == 1:
                inverse_gap = 1.0 / (gaps[i : i + 1, :] / (S * C) + gap_epsilon)
                act_grad = act_grad * jnp.concatenate([inverse_gap, inverse_gap[:, :NARROW]], axis=1)
            grad = act_grad * gelu_slope(pre_ref[i])
            turned = jnp.concatenate([grad, jnp.zeros((TOKENS, NARROW), F32)], axis=1).T
            left_ref[:, i * TOKENS : (i + 1) * TOKENS] = turned[:COLS].astype(BF16)

    grad = dot(left_ref[...], shaped_ref[...].reshape(IMAGES * TOKENS, 768))
    tiles = grad[:WIDE].T.astype(BF16)
    parts = jnp.concatenate([grad[WIDE:, :384], grad[WIDE:, 384:]], axis=0).T.astype(BF16)
    first = place_ref[4] == 0
    for w in range(2):
        sides = []
        for h in range(2):
            at = [(v * 2 + w) * ROWS for v in range(2)]
            lanes = slice(h * NARROW, (h + 1) * NARROW)
            narrow = jnp.concatenate([parts[k : k + ROWS, lanes] for k in at], axis=1)
            sides.append([tiles[h * 384 + k : h * 384 + k + ROWS] for k in at] + [narrow])
        for n, (low, high) in enumerate(zip(*sides, strict=True)):
            keep_ref[w, n * ROWS : (n + 1) * ROWS, :] = jnp.where(first, low, high)
            send_ref[w, n * ROWS : (n + 1) * ROWS, :] = jnp.where(first, high, low)


def sum_kernel(place_ref, got_ref, keep_ref, send_ref):
    v = place_ref[0]
    for n in range(2):
        rows = slice(n * GEN_ROWS, (n + 1) * GEN_ROWS)
        total = got_ref[0, rows].astype(F32)
        for k in range(1, CHUNKS):
            total = total + got_ref[k, rows].astype(F32)
        low = jnp.concatenate([total[:ROWS], total[2 * ROWS :, :NARROW]], axis=1)
        high = jnp.concatenate([total[ROWS : 2 * ROWS], total[2 * ROWS :, NARROW:]], axis=1)
        keep_ref[n] = jnp.where(v == 0, low, high)
        send_ref[n] = jnp.where(v == 0, high, low)


def place_kernel(place_ref, keep_ref, other_ref, fake_ref, gen_ref):
    for n, ref in enumerate((fake_ref, gen_ref)):
        low, high = in_order(place_ref[0], keep_ref[n], other_ref[n])
        ref[:, :128] = low[:, :WIDE]
        ref[:, 128:256] = jnp.concatenate([low[:, WIDE:], high[:, WIDE:]], axis=1)
        ref[:, 256:] = high[:, :WIDE]


def in_hbm(*arrays):
    return [pltpu.with_memory_space_constraint(a, pltpu.HBM) for a in arrays]


def exchange(value, axes):
    return lax.all_to_all(value, axes, 0, 0)


def shards(
    gen_noise,
    score_noise,
    gen_steps,
    score_steps,
    gen_embed,
    gen_modulation,
    gen_proj,
    gen_final,
    teacher_embed,
    teacher_modulation,
    teacher_proj,
    teacher_final,
    fake_embed,
    fake_modulation,
    fake_proj,
    fake_final,
):
    v, s = lax.axis_index("v"), lax.axis_index("s")
    start = lax.axis_index(("g", "h")) * 384
    member = lax.axis_index(("h", "g"))
    place = jnp.stack([v, start + 256 * v, start + 128, member * OWNED, s]).astype(jnp.int32)
    gen_final, teacher_final, fake_final = gen_final.T, teacher_final.T, fake_final.T

    times, conds = time_features(jnp.concatenate([gen_steps, score_steps]), gen_modulation.shape[0])
    gen_time, score_time = times[:3], times[3:]
    halves = jax.ShapeDtypeStruct((SENT_ROWS, 128), BF16)
    mine, other = pl.pallas_call(
        split_kernel,
        grid=(1,),
        in_specs=[smem(), whole((6, 256))] + [whole((IMAGES, C, HALF))] * 2 + [whole((ROWS, 384))] * 3
        + [whole((480, 256))] * 3,
        out_specs=[whole((SENT_ROWS, 128))] * 2,
        out_shape=[halves, halves],
        compiler_params=params(60),
        name="split",
    )(place, conds, gen_noise.transpose(0, 2, 1), score_noise.transpose(0, 2, 1), gen_proj, teacher_proj, fake_proj,
      gen_modulation.T, teacher_modulation.T, fake_modulation.T)
    mine = lax.ppermute(mine, PLACES, SWAP)
    other = lax.ppermute(other, PLACES, SWAP_TURNED)

    g_packed, packed = pl.pallas_call(
        pack_kernel,
        grid=(1,),
        in_specs=[smem()] + [whole((SENT_ROWS, 128))] * 2,
        out_specs=[whole((CHUNKS, GEN_CHUNK, 128)), whole((CHUNKS, SCORE_ROWS, 128))],
        out_shape=[
            jax.ShapeDtypeStruct((CHUNKS, GEN_CHUNK, 128), BF16),
            jax.ShapeDtypeStruct((CHUNKS, SCORE_ROWS, 128), BF16),
        ],
        compiler_params=params(6),
        name="pack",
    )(place, mine, other)
    g_packed = exchange(g_packed, GATHER)
    g_other = lax.ppermute(g_packed, "s", SIBLING)
    packed, g_packed, g_other = lax.optimization_barrier((packed, g_packed, g_other))
    packed = exchange(packed, GATHER)
    low, high = (a[:, GEN_ROWS : GEN_ROWS + 2 * MODS_ROWS] for a in in_order(s, g_packed, g_other))
    mods = jnp.stack([low, high]).reshape(2, 4, 2, 2, 4, 9, 128).transpose(5, 1, 0, 3, 2, 4, 6)
    mods = mods.reshape(9, 32, 512)[:, :, :480].reshape(9, 5, D).astype(F32)
    mods = jnp.pad(mods, ((0, 0), (0, 3), (0, 0)))

    by_image = lambda *shape: pl.BlockSpec((1, *shape), lambda i: (i,) + (0,) * len(shape))
    noise_rows = pl.BlockSpec((HALF, 128), lambda i: (i, 0))
    mods_of = lambda net: pl.BlockSpec((1, 8, D), lambda i: (3 * net + i, 0, 0))
    local = pltpu.HBM((IMAGES, TOKENS, COLS), F32)
    wide = pltpu.HBM((IMAGES, TOKENS, D), BF16)
    gen_embed, teacher_embed, fake_embed = in_hbm(gen_embed, teacher_embed, fake_embed)
    gen_final, teacher_final, fake_final = in_hbm(gen_final, teacher_final, fake_final)

    part, g_shaped, g_pre, g_res = pl.pallas_call(
        generator_kernel,
        grid=(IMAGES,),
        in_specs=[
            smem(), noise_rows, noise_rows, whole((C, D)), mods_of(0), whole((C, D)),
            *([whole((CHUNKS, GEN_CHUNK, 128))] * 2),
        ],
        out_specs=[whole((OWNERS, 32, 128)), by_image(TOKENS, D), by_image(TOKENS, COLS), by_image(TOKENS, COLS)],
        out_shape=[jax.ShapeDtypeStruct((OWNERS, 32, 128), F32), wide, local, local],
        scratch_shapes=[pltpu.VMEM((D, COLS), BF16), pltpu.VMEM((TOKENS, D), F32)],
        compiler_params=params(16),
        cost_estimate=pl.CostEstimate(flops=12 * 10**9, bytes_accessed=30 * 10**6, transcendentals=0),
        name="generator",
    )(place, mine, other, gen_embed, mods, gen_final, g_packed, g_other)
    packed, part = lax.optimization_barrier((packed, part))
    other_packed = lax.ppermute(packed, "s", SIBLING)
    part = exchange(part, COMBINE)

    net_mods = lambda net: pl.BlockSpec((IMAGES, 8, D), lambda *_: (net, 0, 0))
    pack1, keep, sums = pl.pallas_call(
        samples_kernel,
        grid=(1,),
        in_specs=[
            smem(), smem(), whole((OWNERS, 32, 128)), whole((NOISE_ROWS, 128)), net_mods(0), whole((C, D)),
        ],
        out_specs=[whole((OWNERS, 24, 128)), whole((4, 48, C)), whole((8, C))],
        out_shape=[
            jax.ShapeDtypeStruct((OWNERS, 24, 128), F32),
            jax.ShapeDtypeStruct((4, 48, C), F32),
            jax.ShapeDtypeStruct((8, C), F32),
        ],
        compiler_params=params(5),
        name="samples",
    )(place, gen_time, part, mine, mods, gen_final)
    pack1 = exchange(pack1, COMBINE)

    part2, samples, f_shaped, f_pre, f_res = pl.pallas_call(
        score_kernel,
        grid=(IMAGES,),
        in_specs=[
            smem(), smem(), whole((OWNERS, 24, 128)), noise_rows, noise_rows,
            whole((C, D)), whole((C, D)), mods_of(1), mods_of(2), whole((C, D)), whole((C, D)),
            *([whole((CHUNKS, SCORE_ROWS, 128))] * 2),
        ],
        out_specs=[
            whole((OWNERS, 56, 128)), by_image(C, HALF), by_image(TOKENS, D), by_image(TOKENS, COLS),
            by_image(TOKENS, COLS),
        ],
        out_shape=[
            jax.ShapeDtypeStruct((OWNERS, 56, 128), F32),
            jax.ShapeDtypeStruct((IMAGES, C, HALF), F32),
            wide, local, local,
        ],
        scratch_shapes=[
            pltpu.VMEM((D, COLS), BF16), pltpu.VMEM((D, COLS), BF16), pltpu.VMEM((TOKENS, D), F32),
            pltpu.VMEM((TOKENS, D), BF16),
        ],
        compiler_params=params(22),
        cost_estimate=pl.CostEstimate(flops=24 * 10**9, bytes_accessed=50 * 10**6, transcendentals=0),
        name="score",
    )(place, score_time, pack1, mine, other, teacher_embed, fake_embed, mods, mods,
      teacher_final, fake_final, packed, other_packed)
    samples = lax.ppermute(samples, PLACES, SWAP).transpose(0, 2, 1)
    part2 = exchange(part2, COMBINE)

    pack2 = pl.pallas_call(
        cotangent_kernel,
        grid=(1,),
        in_specs=[
            smem(), smem(), smem(), whole((OWNERS, 56, 128)), whole((NOISE_ROWS, 128)), whole((4, 48, C)),
            whole((8, C)), net_mods(1), net_mods(2), whole((C, D)), whole((C, D)),
        ],
        out_specs=whole((OWNERS, 64, 128)),
        out_shape=jax.ShapeDtypeStruct((OWNERS, 64, 128), BF16),
        compiler_params=params(6),
        name="cotangents",
    )(place, gen_time, score_time, part2, mine, keep, sums, mods, mods, teacher_final, fake_final)
    pack2 = exchange(pack2, COMBINE)

    gap = jnp.sum(pack2[:, 48:57, 96].astype(F32).reshape(OWNERS, 3, 3), axis=(0, 2))
    gap = jnp.broadcast_to(jnp.pad(gap, (0, 5))[None, :, None], (16, 8, 128))
    gap = exchange(gap, TOKEN_AXES)

    by_columns = pl.BlockSpec((IMAGES, TOKENS, 768), lambda x: (0, 0, x))
    partial = jax.ShapeDtypeStruct((CHUNKS, GEN_ROWS, 128), BF16)
    partial_spec = pl.BlockSpec((2, GEN_ROWS, 128), lambda x: (x, 0, 0))

    def gradient(net, gaps, mods_net, final, pre, res, shaped):
        kept, sent = pl.pallas_call(
            functools.partial(gradient_kernel, net),
            grid=(4,),
            in_specs=[
                smem(), whole((OWNERS, 64, 128)), *([whole((16, 8, 128))] * len(gaps)), net_mods(mods_net),
                whole((C, D)), *([whole((IMAGES, TOKENS, COLS))] * 2), by_columns,
            ],
            out_specs=[partial_spec, partial_spec],
            out_shape=[partial, partial],
            scratch_shapes=[pltpu.VMEM((COLS, IMAGES * TOKENS), BF16)],
            compiler_params=params(13),
            cost_estimate=pl.CostEstimate(flops=7 * 10**9, bytes_accessed=20 * 10**6, transcendentals=0),
        name="gradient",
        )(place, pack2, *gaps, mods, final, *in_hbm(pre, res, shaped))
        return kept, lax.ppermute(sent, "s", SIBLING)

    pieces = gradient(0, (), 2, fake_final, f_pre, f_res, f_shaped)
    pieces += gradient(1, (gap,), 0, gen_final, g_pre, g_res, g_shaped)
    both = jnp.concatenate(
        [(pieces[n].astype(F32) + pieces[n + 1].astype(F32)).astype(BF16) for n in (0, 2)], axis=1
    )
    tiles = jax.ShapeDtypeStruct((2, ROWS, COLS), F32)
    kept, sent = pl.pallas_call(
        sum_kernel,
        grid=(1,),
        in_specs=[smem(), whole((CHUNKS, 2 * GEN_ROWS, 128))],
        out_specs=[whole((2, ROWS, COLS))] * 2,
        out_shape=[tiles, tiles],
        compiler_params=params(8),
        name="sum",
    )(place, exchange(both, GATHER))
    kept = lax.ppermute(kept, PLACES, SWAP)
    sent = lax.ppermute(sent, PLACES, SWAP_TURNED)
    fake_grad, gen_grad = pl.pallas_call(
        place_kernel,
        grid=(1,),
        in_specs=[smem(), whole((2, ROWS, COLS)), whole((2, ROWS, COLS))],
        out_specs=[whole((ROWS, 384))] * 2,
        out_shape=[jax.ShapeDtypeStruct((ROWS, 384), F32)] * 2,
        compiler_params=params(4),
        name="place",
    )(place, kept, sent)
    return (samples, gen_grad, fake_grad)


def solution(mesh):
    split = Mesh(mesh.devices.reshape(4, 4, 2, 2, 2, 2), ("g", "x", "h", "v", "w", "s"))
    tokens = P(None, ROW_AXES, None)
    columns = P(None, ROW_AXES)
    block = P(ROW_AXES, ("g", "s"))
    net = (P(), columns, block, P())
    return jax.shard_map(
        shards,
        mesh=split,
        in_specs=(tokens, tokens, P(), P(), *net, *net, *net),
        out_specs=(tokens, block, block),
        check_vma=False,
    )
```

```python
import functools
import math

import jax
import jax.numpy as jnp
from jax import lax
from jax.experimental import pallas as pl
from jax.experimental.pallas import tpu as pltpu
from jax.sharding import Mesh
from jax.sharding import PartitionSpec as P

S = 4096
STEPS = 1000
D = 3072
C = 64
IMAGES = 3

norm_epsilon = 1e-06
gap_epsilon = 1e-05

F32 = jnp.float32
BF16 = jnp.bfloat16

GATHER = ("x", "w")
ROW_AXES = ("x", "h", "v", "w")
COMBINE = ("v", "h", "g")
TOKEN_AXES = ("x", "w", "s")
OWNERS = 16
TOKENS = 256
HALF = 128
OWNED = 16
ROWS = 96
WIDE = 128
NARROW = 64
COLS = WIDE + NARROW
GEN_ROWS = 288
NOISE_ROWS = 384
MODS_AT = 864
MODS_ROWS = 36
SENT_ROWS = 912
GEN_CHUNK = 368
SCORE_ROWS = 576
CHUNKS = 8
BLOCK = 512

PLACES = ("h", "v", "s")
SWAP = [(h * 4 + v * 2 + s, s * 4 + v * 2 + h) for h in range(2) for v in range(2) for s in range(2)]
SWAP_TURNED = [(h * 4 + v * 2 + s, s * 4 + (1 - v) * 2 + h) for h in range(2) for v in range(2) for s in range(2)]
SIBLING = [(0, 1), (1, 0)]


def params(mib):
    return pltpu.CompilerParams(vmem_limit_bytes=mib * 1024 * 1024)


def smem():
    return pl.BlockSpec(memory_space=pltpu.SMEM)


def whole(shape):
    zeros = (0,) * len(shape)
    return pl.BlockSpec(shape, lambda *_: zeros)


def dot(a, b):
    return jnp.dot(a, b, preferred_element_type=F32)


def dot_turned(a, b):
    return lax.dot_general(a, b, (((1,), (1,)), ((), ())), preferred_element_type=F32)


def time_features(steps, embed_width):
    times = (steps.astype(F32) + 1.0) / (STEPS + 1.0)
    half = embed_width // 2
    frequency = jnp.exp(-jnp.log(10000.0) * jnp.arange(half, dtype=F32) / half)
    angles = 1000.0 * times[:, None] * frequency[None, :]
    embedding = jnp.concatenate([jnp.cos(angles), jnp.sin(angles)], axis=1)
    return (times, jax.nn.silu(embedding).astype(BF16))


def to_row(numbers):
    shape = (numbers[0].shape[0], OWNED, 128)
    lane = lax.broadcasted_iota(jnp.int32, shape, 2)
    token = lax.broadcasted_iota(jnp.int32, shape, 1)
    total = jnp.zeros(shape, F32)
    for k, number in enumerate(numbers):
        total = jnp.where(lane == token + OWNED * k, number, total)
    return jnp.sum(total, axis=1, keepdims=True)


def from_row(row, k):
    shape = (row.shape[0], OWNED, 128)
    lane = lax.broadcasted_iota(jnp.int32, shape, 2)
    token = lax.broadcasted_iota(jnp.int32, shape, 1)
    return jnp.sum(jnp.where(lane == token + OWNED * k, row, 0.0), axis=2, keepdims=True)


def local_lanes(load, place_ref):
    tile = load(pl.ds(pl.multiple_of(place_ref[1], 128), 128))
    middle = load(pl.ds(pl.multiple_of(place_ref[2], 128), 128))
    part = jnp.where(place_ref[0] == 0, middle[:, :NARROW], middle[:, NARROW:])
    return jnp.concatenate([tile, part], axis=1)


def unpack_weights(place_ref, own_ref, other_ref, net, w_ref):
    s = place_ref[4]
    for packed_ref, side in ((own_ref, s), (other_ref, 1 - s)):
        for chunk in range(CHUNKS):
            x, w = chunk // 2, chunk % 2
            for v in range(2):
                k = pl.multiple_of((x * 8 + v * 2 + w) * ROWS + side * (4 * ROWS), 32)
                first = max(net - 1, 0) * 192 + v * ROWS
                w_ref[pl.ds(k, ROWS), :WIDE] = packed_ref[chunk, first : first + ROWS, :]
                if net == 0:
                    part = packed_ref[chunk, 192:288, v * NARROW : (v + 1) * NARROW]
                else:
                    part = packed_ref[chunk, 384 + v * ROWS : 384 + (v + 1) * ROWS, (net - 1) * NARROW : net * NARROW]
                w_ref[pl.ds(k, ROWS), WIDE:] = part


def split_bits(value, count):
    pieces = []
    for _ in range(count):
        piece = value.astype(BF16)
        pieces.append(piece)
        value = value - piece.astype(F32)
    return pieces


def embed_moments(embed_ref, gram_ref, mean_ref):
    embed = embed_ref[...]
    ones = jnp.ones((8, D), BF16)
    column = dot_turned(embed, ones)[:, 0:1] / D
    row = dot_turned(ones, embed)[0:1] / D
    gram = dot_turned(embed, embed) / D - column * row
    gram_ref[...] = jnp.concatenate(split_bits(gram, 3), axis=1)
    mean_ref[...] = jnp.broadcast_to(column, mean_ref.shape)


def forward(x, embed_ref, mods_ref, final_ref, w_ref, gram_ref, mean_ref, shaped_ref, place_ref):
    turned = dot(x, gram_ref[...])
    turned = turned[:, :C] + turned[:, C : 2 * C] + turned[:, 2 * C :]
    inverse = lax.rsqrt(jnp.sum(turned * x.astype(F32), axis=1, keepdims=True) + norm_epsilon)
    inverse = jnp.broadcast_to(inverse, (TOKENS, BLOCK))
    twice = jnp.concatenate([x, x], axis=1)
    mean = mean_ref[:, 0:1]
    preactivation = jnp.zeros((TOKENS, COLS), F32)
    for b in range(D // BLOCK):
        cut = slice(b * BLOCK, (b + 1) * BLOCK)
        scaled = (embed_ref[:, cut].astype(F32) - mean) * (1.0 + mods_ref[0, 1:2, cut])
        scaled = jnp.concatenate(split_bits(scaled, 2), axis=0)
        shaped = (dot(twice, scaled) * inverse + mods_ref[0, 0:1, cut]).astype(BF16)
        shaped_ref[:, cut] = shaped
        preactivation = preactivation + dot(shaped, w_ref[cut, :])
    activated = jax.nn.gelu(preactivation, approximate=True).astype(BF16).astype(F32)
    own_hidden = dot(x, local_lanes(lambda at: embed_ref[:, at], place_ref))
    gate = local_lanes(lambda at: mods_ref[0, 2:3, at], place_ref)
    scale = local_lanes(lambda at: mods_ref[0, 4:5, at], place_ref)
    residual = own_hidden + gate * activated
    total = jnp.sum(residual, axis=1, keepdims=True)
    total_square = jnp.sum(residual * residual, axis=1, keepdims=True)
    own_mean = total / COLS
    final = local_lanes(lambda at: final_ref[:, at], place_ref)
    centred = ((residual - own_mean) * (1.0 + scale)).astype(BF16)
    ones = jnp.ones((8, COLS), BF16)
    column = dot_turned(jnp.concatenate([ones, jnp.broadcast_to(scale, (8, COLS)).astype(BF16)], axis=0), final)
    column = column[0:1] + column[8:9]
    partial = dot_turned(centred, final) + own_mean * column
    return preactivation, residual, partial, total, total_square


def owned(value):
    return value.reshape(OWNERS, OWNED, value.shape[-1])


def final_sums(mods_ref, final_ref):
    scales = [mods_ref[i, 4:5, :] for i in range(IMAGES)]
    shifts = [mods_ref[i, 3:4, :] for i in range(IMAGES)]
    left = jnp.concatenate(scales + shifts + [jnp.ones((2, D), F32)], axis=0).astype(BF16)
    sums = dot_turned(left, final_ref[...])
    return [sums[i : i + 1] + sums[6:7] for i in range(IMAGES)], [sums[3 + i : 4 + i] for i in range(IMAGES)]


def split_kernel(place_ref, cond_ref, gen_noise_ref, score_noise_ref, gen_ref, teacher_ref, fake_ref,
                 gen_mod_ref, teacher_mod_ref, fake_mod_ref, mine_ref, other_ref):
    for i in range(IMAGES):
        noise = jnp.concatenate([gen_noise_ref[i], score_noise_ref[i]], axis=0).astype(F32).T.astype(BF16)
        mine_ref[i * HALF : (i + 1) * HALF] = noise
        other_ref[i * HALF : (i + 1) * HALF] = noise
    cond = cond_ref[...]
    mods = [dot_turned(cond, ref[...]) for ref in (gen_mod_ref, teacher_mod_ref, fake_mod_ref)]
    mods = jnp.concatenate([mods[0][0:3], mods[1][3:6], mods[2][3:6]], axis=0)
    mods = jnp.concatenate([mods, jnp.zeros((9, 32), F32)], axis=1)
    mods = jnp.concatenate([mods[:, 128 * p : 128 * (p + 1)] for p in range(4)] + [jnp.zeros((12, 128), F32)], axis=0)
    mine_ref[MODS_AT:] = mods.astype(BF16)
    other_ref[MODS_AT:] = mods.astype(BF16)
    first = place_ref[0] == 0
    mine, other = [], []
    for n, ref in enumerate((gen_ref, teacher_ref, fake_ref)):
        rows = slice(NOISE_ROWS + n * ROWS, NOISE_ROWS + (n + 1) * ROWS)
        low, high = ref[:, :128], ref[:, 256:]
        mine_ref[rows] = jnp.where(first, low, high)
        other_ref[rows] = jnp.where(first, high, low)
        low, high = ref[:, 128:192], ref[:, 192:256]
        mine.append(jnp.where(first, low, high))
        other.append(jnp.where(first, high, low))
    for ref, parts in ((mine_ref, mine), (other_ref, other)):
        ref[NOISE_ROWS + 3 * ROWS : NOISE_ROWS + 4 * ROWS] = jnp.concatenate(parts[1:], axis=1)
        ref[NOISE_ROWS + 4 * ROWS : MODS_AT] = jnp.concatenate([parts[0], parts[0]], axis=1)


def in_order(v, mine, other):
    return jnp.where(v == 0, mine, other), jnp.where(v == 0, other, mine)


def pack_kernel(place_ref, mine_ref, other_ref, gen_ref, score_ref):
    v = place_ref[0]
    cuts = [slice(NOISE_ROWS + n * ROWS, NOISE_ROWS + (n + 1) * ROWS) for n in range(5)]
    ordered = [in_order(v, mine_ref[rows], other_ref[rows]) for rows in cuts]
    parts = jnp.concatenate([ordered[4][0][:, :NARROW], ordered[4][1][:, :NARROW]], axis=1)
    mods = in_order(v, mine_ref[MODS_AT:].astype(F32), other_ref[MODS_AT:].astype(F32))
    mods = jnp.concatenate([mods[0][:MODS_ROWS], mods[1][:MODS_ROWS], jnp.zeros((8, 128), F32)], axis=0)
    gen = jnp.concatenate([*ordered[0], parts, mods.astype(BF16)], axis=0)
    score = jnp.concatenate([*ordered[1], *ordered[2], *ordered[3]], axis=0)
    for k in range(CHUNKS):
        gen_ref[k] = gen
        score_ref[k] = score


def generator_kernel(place_ref, own_ref, other_ref, embed_ref, mods_ref, final_ref, own_w_ref, other_w_ref,
                     part_ref, shaped_ref, pre_ref, res_ref, w_ref, gram_ref, mean_ref):
    i = pl.program_id(0)
    v = place_ref[0]

    @pl.when(i == 0)
    def _():
        embed_moments(embed_ref, gram_ref, mean_ref)
        unpack_weights(place_ref, own_w_ref, other_w_ref, 0, w_ref)
        part_ref[:, 24:32, :] = jnp.zeros((OWNERS, 8, 128), F32)

    x = jnp.concatenate(in_order(v, own_ref[:, :C], other_ref[:, :C]), axis=0)
    pre, res, partial, total, square = forward(
        x, embed_ref, mods_ref, final_ref, w_ref, gram_ref, mean_ref, shaped_ref.at[0], place_ref
    )
    pre_ref[0] = pre
    res_ref[0] = res
    pieces = owned(partial)
    part_ref[:, pl.ds(pl.multiple_of(i * 8, 8), 8), :] = jnp.concatenate([pieces[:, :8], pieces[:, 8:]], axis=2)
    part_ref[:, pl.ds(24 + i, 1), :] = to_row([owned(total), owned(square)])


def samples_kernel(place_ref, time_ref, got_ref, noise_ref, mods_ref, final_ref,
                   out_ref, keep_ref, sums_ref):
    total = jnp.sum(got_ref[...], axis=0)
    scales, shifts = final_sums(mods_ref, final_ref)
    packed = []
    for i in range(IMAGES):
        block = total[8 * i : 8 * i + 8]
        partial = jnp.concatenate([block[:, :C], block[:, C:]], axis=0)
        row = total[24 + i : 25 + i][None]
        average = from_row(row, 0)[0] / D
        square = from_row(row, 1)[0] / D
        inverse = lax.rsqrt(square - average * average + norm_epsilon)
        inner = inverse * (partial - average * scales[i])
        velocity = inner + shifts[i]
        noise = noise_ref[pl.ds(pl.multiple_of(place_ref[3] + i * HALF, 16), OWNED), :][:, :C].astype(F32)
        samples = noise - time_ref[i] * velocity
        packed.append(jnp.concatenate([samples[:8], samples[8:]], axis=1))
        at = slice(i * OWNED, (i + 1) * OWNED)
        keep_ref[0, at, :] = samples
        keep_ref[1, at, :] = inner
        keep_ref[2, at, :] = jnp.broadcast_to(average, (OWNED, C))
        keep_ref[3, at, :] = jnp.broadcast_to(inverse, (OWNED, C))
    sums_ref[...] = jnp.concatenate(scales + [jnp.zeros((5, C), F32)], axis=0)
    out_ref[...] = jnp.broadcast_to(jnp.concatenate(packed, axis=0)[None], out_ref.shape)


def mix(samples, noise, t):
    return ((1.0 - t) * samples + t * noise).astype(BF16)


def score_kernel(place_ref, time_ref, got_ref, own_ref, other_ref,
                 t_embed_ref, f_embed_ref, t_mods_ref, f_mods_ref, t_final_ref, f_final_ref, own_w_ref, other_w_ref,
                 part_ref, samples_ref, shaped_ref, pre_ref, res_ref,
                 t_w_ref, f_w_ref, t_gram_ref, f_gram_ref, t_mean_ref, f_mean_ref, t_shaped_ref):
    i = pl.program_id(0)
    v = place_ref[0]

    @pl.when(i == 0)
    def _():
        embed_moments(t_embed_ref, t_gram_ref, t_mean_ref)
        embed_moments(f_embed_ref, f_gram_ref, f_mean_ref)
        unpack_weights(place_ref, own_w_ref, other_w_ref, 1, t_w_ref)
        unpack_weights(place_ref, own_w_ref, other_w_ref, 2, f_w_ref)
        part_ref[:, 48:56, :] = jnp.zeros((OWNERS, 8, 128), F32)

    got = got_ref[:, pl.ds(pl.multiple_of(i * 8, 8), 8), :]
    samples = jnp.concatenate([got[:, :, :C], got[:, :, C:]], axis=1).reshape(TOKENS, C)
    turned = jnp.concatenate([samples[:HALF], samples[HALF:]], axis=1).T
    samples_ref[0] = jnp.where(v == 0, turned[:C], turned[C:])
    own, other = own_ref[:, C:].astype(F32), other_ref[:, C:].astype(F32)
    noise = jnp.concatenate(in_order(v, own, other), axis=0)
    noised = mix(samples, noise, time_ref[i])
    _, _, t_partial, t_total, t_square = forward(
        noised, t_embed_ref, t_mods_ref, t_final_ref, t_w_ref, t_gram_ref, t_mean_ref, t_shaped_ref, place_ref
    )
    pre, res, f_partial, f_total, f_square = forward(
        noised, f_embed_ref, f_mods_ref, f_final_ref, f_w_ref, f_gram_ref, f_mean_ref, shaped_ref.at[0], place_ref
    )
    pre_ref[0] = pre
    res_ref[0] = res
    part_ref[:, pl.ds(pl.multiple_of(i * 16, 16), 16), :] = owned(jnp.concatenate([t_partial, f_partial], axis=1))
    part_ref[:, pl.ds(48 + i, 1), :] = to_row([owned(v) for v in (t_total, t_square, f_total, f_square)])


def cotangent_kernel(place_ref, gen_time_ref, time_ref, got_ref, noise_ref, keep_ref, sums_ref,
                     t_mods_ref, f_mods_ref, t_final_ref, f_final_ref, out_ref):
    loss_scale = 1.0 / math.sqrt(IMAGES * S)
    total = jnp.sum(got_ref[...], axis=0)
    t_scales, t_shifts = final_sums(t_mods_ref, t_final_ref)
    f_scales, f_shifts = final_sums(f_mods_ref, f_final_ref)
    lane = lax.broadcasted_iota(jnp.int32, (1, 128), 1)
    cots, rows = [], []
    for i in range(IMAGES):
        block = total[16 * i : 16 * i + 16]
        row = total[48 + i : 49 + i][None]

        def inner(partial, k, scale):
            average = from_row(row, k)[0] / D
            square = from_row(row, k + 1)[0] / D
            inverse = lax.rsqrt(square - average * average + norm_epsilon)
            return inverse * (partial - average * scale), average, inverse

        t_inner, _, _ = inner(block[:, :C], 0, t_scales[i])
        f_inner, f_average, f_inverse = inner(block[:, C:], 2, f_scales[i])
        teacher, fake = t_inner + t_shifts[i], f_inner + f_shifts[i]
        at = slice(i * OWNED, (i + 1) * OWNED)
        samples, g_inner = keep_ref[0, at, :], keep_ref[1, at, :]
        g_average, g_inverse = keep_ref[2, at, 0:1], keep_ref[3, at, 0:1]
        noise = noise_ref[pl.ds(pl.multiple_of(place_ref[3] + i * HALF, 16), OWNED), :][:, C:].astype(F32)
        t = time_ref[i]
        noised = mix(samples, noise, t).astype(F32)
        distance = jnp.sum(jnp.abs(samples - noised + t * teacher))
        gen_cot = (-(gen_time_ref[i] * t * loss_scale) * (teacher - fake)).astype(BF16).astype(F32)
        fake_cot = (loss_scale * (fake - noise + samples)).astype(BF16).astype(F32)
        numbers = []
        for cot, column, value, average, inverse in (
            (fake_cot, f_scales[i], f_inner, f_average, f_inverse),
            (gen_cot, sums_ref[i : i + 1, :], g_inner, g_average, g_inverse),
        ):
            first = jnp.sum(cot * column, axis=1, keepdims=True) / D
            second = jnp.sum(cot * value, axis=1, keepdims=True) / D
            slope = inverse * inverse * second
            numbers += [inverse, slope, average * slope - inverse * first]
        cots.append(jnp.concatenate([fake_cot, gen_cot], axis=1))
        numbers_row = to_row([number[None] for number in numbers])[0]
        numbers_row = jnp.where(lane == 96, distance, numbers_row)
        for _ in range(3):
            rounded = numbers_row.astype(BF16).astype(F32)
            rows.append(rounded)
            numbers_row = numbers_row - rounded
    rows.append(jnp.zeros((7, 128), F32))
    packed = jnp.concatenate(cots + rows, axis=0).astype(BF16)
    out_ref[...] = jnp.broadcast_to(packed[None], out_ref.shape)


def gelu_slope(v):
    a, b = math.sqrt(2.0 / math.pi), 0.044715
    t = jnp.tanh(a * (v + b * (v * v * v)))
    return 0.5 * (1.0 + t) + 0.5 * v * (1.0 - t * t) * (a * (1.0 + 3.0 * b * (v * v)))


def gradient_kernel(net, place_ref, got_ref, *refs):
    gap_ref, refs = (refs[0], refs[1:]) if net == 1 else (None, refs)
    mods_ref, final_ref, pre_ref, res_ref, shaped_ref, keep_ref, send_ref, left_ref = refs

    @pl.when(pl.program_id(0) == 0)
    def _():
        final = local_lanes(lambda at: final_ref[:, at], place_ref)
        if net == 1:
            gaps = jnp.sum(gap_ref[...], axis=0)
        for i in range(IMAGES):
            row = got_ref[:, 48:64, :].astype(F32)
            row = row[:, 3 * i : 3 * i + 1] + row[:, 3 * i + 1 : 3 * i + 2] + row[:, 3 * i + 2 : 3 * i + 3]
            inverse, slope, offset = [from_row(row, 3 * net + k).reshape(TOKENS, 1) for k in range(3)]
            cot = got_ref[:, 16 * i : 16 * i + 16, :].reshape(TOKENS, 128)[:, net * C : (net + 1) * C]
            out_grad = dot(cot, final)
            scale = local_lanes(lambda at: mods_ref[i, 4:5, at], place_ref)
            gate = local_lanes(lambda at: mods_ref[i, 2:3, at], place_ref)
            res_grad = inverse * (out_grad * (1.0 + scale)) - slope * res_ref[i] + offset
            act_grad = res_grad * gate
            if net == 1:
                inverse_gap = 1.0 / (gaps[i : i + 1, :] / (S * C) + gap_epsilon)
                act_grad = act_grad * jnp.concatenate([inverse_gap, inverse_gap[:, :NARROW]], axis=1)
            grad = act_grad * gelu_slope(pre_ref[i])
            turned = jnp.concatenate([grad, jnp.zeros((TOKENS, NARROW), F32)], axis=1).T
            left_ref[:, i * TOKENS : (i + 1) * TOKENS] = turned[:COLS].astype(BF16)

    grad = dot(left_ref[...], shaped_ref[...].reshape(IMAGES * TOKENS, 768))
    tiles = grad[:WIDE].T.astype(BF16)
    parts = jnp.concatenate([grad[WIDE:, :384], grad[WIDE:, 384:]], axis=0).T.astype(BF16)
    first = place_ref[4] == 0
    for w in range(2):
        sides = []
        for h in range(2):
            at = [(v * 2 + w) * ROWS for v in range(2)]
            lanes = slice(h * NARROW, (h + 1) * NARROW)
            narrow = jnp.concatenate([parts[k : k + ROWS, lanes] for k in at], axis=1)
            sides.append([tiles[h * 384 + k : h * 384 + k + ROWS] for k in at] + [narrow])
        for n, (low, high) in enumerate(zip(*sides, strict=True)):
            keep_ref[w, n * ROWS : (n + 1) * ROWS, :] = jnp.where(first, low, high)
            send_ref[w, n * ROWS : (n + 1) * ROWS, :] = jnp.where(first, high, low)


def sum_kernel(place_ref, got_ref, keep_ref, send_ref):
    v = place_ref[0]
    for n in range(2):
        rows = slice(n * GEN_ROWS, (n + 1) * GEN_ROWS)
        total = got_ref[0, rows].astype(F32)
        for k in range(1, CHUNKS):
            total = total + got_ref[k, rows].astype(F32)
        def folded(rows, part):
            return jnp.concatenate([rows, jnp.concatenate([part[:48], part[48:]], axis=1)], axis=0)

        low = folded(total[:ROWS], total[2 * ROWS :, :NARROW])
        high = folded(total[ROWS : 2 * ROWS], total[2 * ROWS :, NARROW:])
        keep_ref[n] = jnp.where(v == 0, low, high)
        send_ref[n] = jnp.where(v == 0, high, low)


def place_kernel(place_ref, keep_ref, other_ref, fake_ref, gen_ref):
    for n, ref in enumerate((fake_ref, gen_ref)):
        low, high = in_order(place_ref[0], keep_ref[n], other_ref[n])
        ref[:, :128] = low[:ROWS]
        ref[:48, 128:256] = jnp.concatenate([low[ROWS:, :NARROW], high[ROWS:, :NARROW]], axis=1)
        ref[48:, 128:256] = jnp.concatenate([low[ROWS:, NARROW:], high[ROWS:, NARROW:]], axis=1)
        ref[:, 256:] = high[:ROWS]


def in_hbm(*arrays):
    return [pltpu.with_memory_space_constraint(a, pltpu.HBM) for a in arrays]


def exchange(value, axes):
    return lax.all_to_all(value, axes, 0, 0)


def shards(
    gen_noise,
    score_noise,
    gen_steps,
    score_steps,
    gen_embed,
    gen_modulation,
    gen_proj,
    gen_final,
    teacher_embed,
    teacher_modulation,
    teacher_proj,
    teacher_final,
    fake_embed,
    fake_modulation,
    fake_proj,
    fake_final,
):
    v, s = lax.axis_index("v"), lax.axis_index("s")
    start = lax.axis_index(("g", "h")) * 384
    member = lax.axis_index(("h", "g"))
    place = jnp.stack([v, start + 256 * v, start + 128, member * OWNED, s]).astype(jnp.int32)
    gen_final, teacher_final, fake_final = gen_final.T, teacher_final.T, fake_final.T

    times, conds = time_features(jnp.concatenate([gen_steps, score_steps]), gen_modulation.shape[0])
    gen_time, score_time = times[:3], times[3:]
    halves = jax.ShapeDtypeStruct((SENT_ROWS, 128), BF16)
    mine, other = pl.pallas_call(
        split_kernel,
        grid=(1,),
        in_specs=[smem(), whole((6, 256))] + [whole((IMAGES, C, HALF))] * 2 + [whole((ROWS, 384))] * 3
        + [whole((480, 256))] * 3,
        out_specs=[whole((SENT_ROWS, 128))] * 2,
        out_shape=[halves, halves],
        compiler_params=params(60),
        name="split",
    )(place, conds, gen_noise.transpose(0, 2, 1), score_noise.transpose(0, 2, 1), gen_proj, teacher_proj, fake_proj,
      gen_modulation.T, teacher_modulation.T, fake_modulation.T)
    mine = lax.ppermute(mine, PLACES, SWAP)
    other = lax.ppermute(other, PLACES, SWAP_TURNED)

    g_packed, packed = pl.pallas_call(
        pack_kernel,
        grid=(1,),
        in_specs=[smem()] + [whole((SENT_ROWS, 128))] * 2,
        out_specs=[whole((CHUNKS, GEN_CHUNK, 128)), whole((CHUNKS, SCORE_ROWS, 128))],
        out_shape=[
            jax.ShapeDtypeStruct((CHUNKS, GEN_CHUNK, 128), BF16),
            jax.ShapeDtypeStruct((CHUNKS, SCORE_ROWS, 128), BF16),
        ],
        compiler_params=params(6),
        name="pack",
    )(place, mine, other)
    g_packed = exchange(g_packed, GATHER)
    g_other = lax.ppermute(g_packed, "s", SIBLING)
    packed, g_packed, g_other = lax.optimization_barrier((packed, g_packed, g_other))
    packed = exchange(packed, GATHER)
    low, high = (a[:, GEN_ROWS : GEN_ROWS + 2 * MODS_ROWS] for a in in_order(s, g_packed, g_other))
    mods = jnp.stack([low, high]).reshape(2, 4, 2, 2, 4, 9, 128).transpose(5, 1, 0, 3, 2, 4, 6)
    mods = mods.reshape(9, 32, 512)[:, :, :480].reshape(9, 5, D).astype(F32)
    mods = jnp.pad(mods, ((0, 0), (0, 3), (0, 0)))

    by_image = lambda *shape: pl.BlockSpec((1, *shape), lambda i: (i,) + (0,) * len(shape))
    noise_rows = pl.BlockSpec((HALF, 128), lambda i: (i, 0))
    mods_of = lambda net: pl.BlockSpec((1, 8, D), lambda i: (3 * net + i, 0, 0))
    local = pltpu.HBM((IMAGES, TOKENS, COLS), F32)
    wide = pltpu.HBM((IMAGES, TOKENS, D), BF16)
    gen_embed, teacher_embed, fake_embed = in_hbm(gen_embed, teacher_embed, fake_embed)
    gen_final, teacher_final, fake_final = in_hbm(gen_final, teacher_final, fake_final)

    part, g_shaped, g_pre, g_res = pl.pallas_call(
        generator_kernel,
        grid=(IMAGES,),
        in_specs=[
            smem(), noise_rows, noise_rows, whole((C, D)), mods_of(0), whole((C, D)),
            *([whole((CHUNKS, GEN_CHUNK, 128))] * 2),
        ],
        out_specs=[whole((OWNERS, 32, 128)), by_image(TOKENS, D), by_image(TOKENS, COLS), by_image(TOKENS, COLS)],
        out_shape=[jax.ShapeDtypeStruct((OWNERS, 32, 128), F32), wide, local, local],
        scratch_shapes=[pltpu.VMEM((D, COLS), BF16), pltpu.VMEM((C, 3 * C), BF16), pltpu.VMEM((C, 128), F32)],
        compiler_params=params(16),
        cost_estimate=pl.CostEstimate(flops=12 * 10**9, bytes_accessed=30 * 10**6, transcendentals=0),
        name="generator",
    )(place, mine, other, gen_embed, mods, gen_final, g_packed, g_other)
    packed, part = lax.optimization_barrier((packed, part))
    part = exchange(part, COMBINE)

    net_mods = lambda net: pl.BlockSpec((IMAGES, 8, D), lambda *_: (net, 0, 0))
    pack1, keep, sums = pl.pallas_call(
        samples_kernel,
        grid=(1,),
        in_specs=[
            smem(), smem(), whole((OWNERS, 32, 128)), whole((NOISE_ROWS, 128)), net_mods(0), whole((C, D)),
        ],
        out_specs=[whole((OWNERS, 24, 128)), whole((4, 48, C)), whole((8, C))],
        out_shape=[
            jax.ShapeDtypeStruct((OWNERS, 24, 128), F32),
            jax.ShapeDtypeStruct((4, 48, C), F32),
            jax.ShapeDtypeStruct((8, C), F32),
        ],
        compiler_params=params(5),
        name="samples",
    )(place, gen_time, part, mine, mods, gen_final)
    packed, pack1 = lax.optimization_barrier((packed, pack1))
    pack1 = exchange(pack1, COMBINE)
    other_packed = lax.ppermute(packed, "s", SIBLING)

    part2, samples, f_shaped, f_pre, f_res = pl.pallas_call(
        score_kernel,
        grid=(IMAGES,),
        in_specs=[
            smem(), smem(), whole((OWNERS, 24, 128)), noise_rows, noise_rows,
            whole((C, D)), whole((C, D)), mods_of(1), mods_of(2), whole((C, D)), whole((C, D)),
            *([whole((CHUNKS, SCORE_ROWS, 128))] * 2),
        ],
        out_specs=[
            whole((OWNERS, 56, 128)), by_image(C, HALF), by_image(TOKENS, D), by_image(TOKENS, COLS),
            by_image(TOKENS, COLS),
        ],
        out_shape=[
            jax.ShapeDtypeStruct((OWNERS, 56, 128), F32),
            jax.ShapeDtypeStruct((IMAGES, C, HALF), F32),
            wide, local, local,
        ],
        scratch_shapes=[
            *([pltpu.VMEM((D, COLS), BF16)] * 2), *([pltpu.VMEM((C, 3 * C), BF16)] * 2),
            *([pltpu.VMEM((C, 128), F32)] * 2), pltpu.VMEM((TOKENS, D), BF16),
        ],
        compiler_params=params(22),
        cost_estimate=pl.CostEstimate(flops=24 * 10**9, bytes_accessed=50 * 10**6, transcendentals=0),
        name="score",
    )(place, score_time, pack1, mine, other, teacher_embed, fake_embed, mods, mods,
      teacher_final, fake_final, packed, other_packed)
    part2 = exchange(part2, COMBINE)

    pack2 = pl.pallas_call(
        cotangent_kernel,
        grid=(1,),
        in_specs=[
            smem(), smem(), smem(), whole((OWNERS, 56, 128)), whole((NOISE_ROWS, 128)), whole((4, 48, C)),
            whole((8, C)), net_mods(1), net_mods(2), whole((C, D)), whole((C, D)),
        ],
        out_specs=whole((OWNERS, 64, 128)),
        out_shape=jax.ShapeDtypeStruct((OWNERS, 64, 128), BF16),
        compiler_params=params(6),
        name="cotangents",
    )(place, gen_time, score_time, part2, mine, keep, sums, mods, mods, teacher_final, fake_final)
    pack2 = exchange(pack2, COMBINE)
    samples, pack2 = lax.optimization_barrier((samples, pack2))
    samples = lax.ppermute(samples, PLACES, SWAP)

    gap = jnp.sum(pack2[:, 48:57, 96].astype(F32).reshape(OWNERS, 3, 3), axis=(0, 2))
    gap = jnp.broadcast_to(jnp.pad(gap, (0, 5))[None, :, None], (16, 8, 128))
    gap = exchange(gap, TOKEN_AXES)

    by_columns = pl.BlockSpec((IMAGES, TOKENS, 768), lambda x: (0, 0, x))
    partial = jax.ShapeDtypeStruct((CHUNKS, GEN_ROWS, 128), BF16)
    partial_spec = pl.BlockSpec((2, GEN_ROWS, 128), lambda x: (x, 0, 0))

    def gradient(net, gaps, mods_net, final, pre, res, shaped):
        kept, sent = pl.pallas_call(
            functools.partial(gradient_kernel, net),
            grid=(4,),
            in_specs=[
                smem(), whole((OWNERS, 64, 128)), *([whole((16, 8, 128))] * len(gaps)), net_mods(mods_net),
                whole((C, D)), *([whole((IMAGES, TOKENS, COLS))] * 2), by_columns,
            ],
            out_specs=[partial_spec, partial_spec],
            out_shape=[partial, partial],
            scratch_shapes=[pltpu.VMEM((COLS, IMAGES * TOKENS), BF16)],
            compiler_params=params(13),
            cost_estimate=pl.CostEstimate(flops=7 * 10**9, bytes_accessed=20 * 10**6, transcendentals=0),
        name="gradient",
        )(place, pack2, *gaps, mods, final, *in_hbm(pre, res, shaped))
        return kept, lax.ppermute(sent, "s", SIBLING)

    pieces = gradient(0, (), 2, fake_final, f_pre, f_res, f_shaped)
    pieces += gradient(1, (gap,), 0, gen_final, g_pre, g_res, g_shaped)
    both = jnp.concatenate(
        [(pieces[n].astype(F32) + pieces[n + 1].astype(F32)).astype(BF16) for n in (0, 2)], axis=1
    )
    samples, both = lax.optimization_barrier((samples, both))
    samples = samples.transpose(0, 2, 1)
    tiles = jax.ShapeDtypeStruct((2, 144, 128), F32)
    kept, sent = pl.pallas_call(
        sum_kernel,
        grid=(1,),
        in_specs=[smem(), whole((CHUNKS, 2 * GEN_ROWS, 128))],
        out_specs=[whole((2, 144, 128))] * 2,
        out_shape=[tiles, tiles],
        compiler_params=params(8),
        name="sum",
    )(place, exchange(both, GATHER))
    kept = lax.ppermute(kept, PLACES, SWAP)
    sent = lax.ppermute(sent, PLACES, SWAP_TURNED)
    fake_grad, gen_grad = pl.pallas_call(
        place_kernel,
        grid=(1,),
        in_specs=[smem(), whole((2, 144, 128)), whole((2, 144, 128))],
        out_specs=[whole((ROWS, 384))] * 2,
        out_shape=[jax.ShapeDtypeStruct((ROWS, 384), F32)] * 2,
        compiler_params=params(4),
        name="place",
    )(place, kept, sent)
    return (samples, gen_grad, fake_grad)


def solution(mesh):
    split = Mesh(mesh.devices.reshape(4, 4, 2, 2, 2, 2), ("g", "x", "h", "v", "w", "s"))
    tokens = P(None, ROW_AXES, None)
    columns = P(None, ROW_AXES)
    block = P(ROW_AXES, ("g", "s"))
    net = (P(), columns, block, P())
    return jax.shard_map(
        shards,
        mesh=split,
        in_specs=(tokens, tokens, P(), P(), *net, *net, *net),
        out_specs=(tokens, block, block),
        check_vma=False,
    )
```

```python
import functools
import math

import jax
import jax.numpy as jnp
from jax import lax
from jax.experimental import pallas as pl
from jax.experimental.pallas import tpu as pltpu
from jax.sharding import Mesh
from jax.sharding import PartitionSpec as P

S = 4096
STEPS = 1000
D = 3072
C = 64
IMAGES = 3

norm_epsilon = 1e-06
gap_epsilon = 1e-05

F32 = jnp.float32
BF16 = jnp.bfloat16

GATHER = ("x", "w")
ROW_AXES = ("x", "h", "v", "w")
COMBINE = ("v", "h", "g")
TOKEN_AXES = ("x", "w", "s")
OWNERS = 16
TOKENS = 256
HALF = 128
OWNED = 16
ROWS = 96
WIDE = 128
NARROW = 64
COLS = WIDE + NARROW
GEN_ROWS = 288
NOISE_ROWS = 384
MODS_AT = 864
MODS_ROWS = 36
SENT_ROWS = 912
GEN_CHUNK = 368
SCORE_ROWS = 576
CHUNKS = 8
BLOCK = 512

PLACES = ("h", "v", "s")
SWAP = [(h * 4 + v * 2 + s, s * 4 + v * 2 + h) for h in range(2) for v in range(2) for s in range(2)]
SWAP_TURNED = [(h * 4 + v * 2 + s, s * 4 + (1 - v) * 2 + h) for h in range(2) for v in range(2) for s in range(2)]
SIBLING = [(0, 1), (1, 0)]


def params(mib):
    return pltpu.CompilerParams(vmem_limit_bytes=mib * 1024 * 1024)


def smem():
    return pl.BlockSpec(memory_space=pltpu.SMEM)


def whole(shape):
    zeros = (0,) * len(shape)
    return pl.BlockSpec(shape, lambda *_: zeros)


def dot(a, b):
    return jnp.dot(a, b, preferred_element_type=F32)


def dot_turned(a, b):
    return lax.dot_general(a, b, (((1,), (1,)), ((), ())), preferred_element_type=F32)


def time_features(steps, embed_width):
    times = (steps.astype(F32) + 1.0) / (STEPS + 1.0)
    half = embed_width // 2
    frequency = jnp.exp(-jnp.log(10000.0) * jnp.arange(half, dtype=F32) / half)
    angles = 1000.0 * times[:, None] * frequency[None, :]
    embedding = jnp.concatenate([jnp.cos(angles), jnp.sin(angles)], axis=1)
    return (times, jax.nn.silu(embedding).astype(BF16))


def to_row(numbers):
    shape = (numbers[0].shape[0], OWNED, 128)
    lane = lax.broadcasted_iota(jnp.int32, shape, 2)
    token = lax.broadcasted_iota(jnp.int32, shape, 1)
    total = jnp.zeros(shape, F32)
    for k, number in enumerate(numbers):
        total = jnp.where(lane == token + OWNED * k, number, total)
    return jnp.sum(total, axis=1, keepdims=True)


def row_pieces(numbers, stride):
    row = to_row(numbers)
    per_row = 128 // stride
    rows = [row.astype(BF16).astype(F32)]
    row = row - rows[0]
    rows.append(row.astype(BF16).astype(F32))
    rows.append((row - rows[1]).astype(BF16).astype(F32))
    packed = [jnp.concatenate([r[:, :, :stride] for r in rows[:per_row]], axis=2)]
    if len(rows) > per_row:
        packed.append(jnp.concatenate([rows[per_row][:, :, :stride], jnp.zeros_like(row)[:, :, : 128 - stride]], axis=2))
    else:
        packed[0] = jnp.concatenate([packed[0], jnp.zeros_like(row)[:, :, : 128 - 3 * stride]], axis=2)
    return packed


def from_row(row, k):
    shape = (row.shape[0], OWNED, 128)
    lane = lax.broadcasted_iota(jnp.int32, shape, 2)
    token = lax.broadcasted_iota(jnp.int32, shape, 1)
    return jnp.sum(jnp.where(lane == token + OWNED * k, row, 0.0), axis=2, keepdims=True)


def local_lanes(load, place_ref):
    tile = load(pl.ds(pl.multiple_of(place_ref[1], 128), 128))
    middle = load(pl.ds(pl.multiple_of(place_ref[2], 128), 128))
    part = jnp.where(place_ref[0] == 0, middle[:, :NARROW], middle[:, NARROW:])
    return jnp.concatenate([tile, part], axis=1)


def unpack_weights(place_ref, own_ref, other_ref, net, w_ref):
    s = place_ref[4]
    for packed_ref, side in ((own_ref, s), (other_ref, 1 - s)):
        for chunk in range(CHUNKS):
            x, w = chunk // 2, chunk % 2
            for v in range(2):
                k = pl.multiple_of((x * 8 + v * 2 + w) * ROWS + side * (4 * ROWS), 32)
                first = max(net - 1, 0) * 192 + v * ROWS
                w_ref[pl.ds(k, ROWS), :WIDE] = packed_ref[chunk, first : first + ROWS, :]
                if net == 0:
                    part = packed_ref[chunk, 192:288, v * NARROW : (v + 1) * NARROW]
                else:
                    part = packed_ref[chunk, 384 + v * ROWS : 384 + (v + 1) * ROWS, (net - 1) * NARROW : net * NARROW]
                w_ref[pl.ds(k, ROWS), WIDE:] = part


def split_bits(value, count):
    pieces = []
    for _ in range(count):
        piece = value.astype(BF16)
        pieces.append(piece)
        value = value - piece.astype(F32)
    return pieces


def embed_moments(embed_ref, gram_ref, mean_ref):
    embed = embed_ref[...]
    ones = jnp.ones((8, D), BF16)
    column = dot_turned(embed, ones)[:, 0:1] / D
    row = dot_turned(ones, embed)[0:1] / D
    gram = dot_turned(embed, embed) / D - column * row
    gram_ref[...] = jnp.concatenate(split_bits(gram, 3), axis=1)
    mean_ref[...] = jnp.broadcast_to(column, mean_ref.shape)


def forward(x, embed_ref, mods_ref, final_ref, w_ref, gram_ref, mean_ref, shaped_ref, place_ref):
    turned = dot(x, gram_ref[...])
    turned = turned[:, :C] + turned[:, C : 2 * C] + turned[:, 2 * C :]
    inverse = lax.rsqrt(jnp.sum(turned * x.astype(F32), axis=1, keepdims=True) + norm_epsilon)
    inverse = jnp.broadcast_to(inverse, (TOKENS, BLOCK))
    twice = jnp.concatenate([x, x], axis=1)
    mean = mean_ref[:, 0:1]
    preactivation = jnp.zeros((TOKENS, COLS), F32)
    for b in range(D // BLOCK):
        cut = slice(b * BLOCK, (b + 1) * BLOCK)
        scaled = (embed_ref[:, cut].astype(F32) - mean) * (1.0 + mods_ref[0, 1:2, cut])
        scaled = jnp.concatenate(split_bits(scaled, 2), axis=0)
        shaped = (dot(twice, scaled) * inverse + mods_ref[0, 0:1, cut]).astype(BF16)
        shaped_ref[:, cut] = shaped
        preactivation = preactivation + dot(shaped, w_ref[cut, :])
    activated = jax.nn.gelu(preactivation, approximate=True).astype(BF16).astype(F32)
    own_hidden = dot(x, local_lanes(lambda at: embed_ref[:, at], place_ref))
    gate = local_lanes(lambda at: mods_ref[0, 2:3, at], place_ref)
    scale = local_lanes(lambda at: mods_ref[0, 4:5, at], place_ref)
    residual = own_hidden + gate * activated
    total = jnp.sum(residual, axis=1, keepdims=True)
    total_square = jnp.sum(residual * residual, axis=1, keepdims=True)
    own_mean = total / COLS
    final = local_lanes(lambda at: final_ref[:, at], place_ref)
    centred = ((residual - own_mean) * (1.0 + scale)).astype(BF16)
    partial = dot_turned(centred, final)
    return preactivation, residual, partial, total, total_square


def owned(value):
    return value.reshape(OWNERS, OWNED, value.shape[-1])


def final_sums(mods_ref, final_ref):
    scales = [mods_ref[i, 4:5, :] for i in range(IMAGES)]
    shifts = [mods_ref[i, 3:4, :] for i in range(IMAGES)]
    run = lax.broadcasted_iota(jnp.int32, (OWNERS, D), 1) // COLS
    own = run == lax.broadcasted_iota(jnp.int32, (OWNERS, D), 0)
    left = [jnp.where(own, row, 0.0) for row in scales + [jnp.ones((1, D), F32)]]
    sums = dot_turned(jnp.concatenate(left + shifts + [jnp.zeros((5, D), F32)], axis=0).astype(BF16), final_ref[...])
    ones = sums[3 * OWNERS : 4 * OWNERS]
    runs = [sums[i * OWNERS : (i + 1) * OWNERS] + ones for i in range(IMAGES)]
    return runs, [jnp.sum(r, axis=0, keepdims=True) for r in runs], [sums[64 + i : 65 + i] for i in range(IMAGES)]


def add_up(partials, totals, squares, runs):
    means = totals * (1.0 / COLS)
    ordered = jnp.concatenate(
        [runs[(g * 2 + h) * 2 + v][None, None] for v in range(2) for h in range(2) for g in range(4)], axis=0
    )
    partial = jnp.sum(partials + means * ordered, axis=0)
    average = jnp.sum(totals, axis=0) / D
    inverse = lax.rsqrt(jnp.sum(squares, axis=0) / D - average * average + norm_epsilon)
    return partial, average, inverse


def split_kernel(place_ref, cond_ref, gen_noise_ref, score_noise_ref, gen_ref, teacher_ref, fake_ref,
                 gen_mod_ref, teacher_mod_ref, fake_mod_ref, mine_ref, other_ref):
    for i in range(IMAGES):
        noise = jnp.concatenate([gen_noise_ref[i], score_noise_ref[i]], axis=0).astype(F32).T.astype(BF16)
        mine_ref[i * HALF : (i + 1) * HALF] = noise
        other_ref[i * HALF : (i + 1) * HALF] = noise
    cond = cond_ref[...]
    mods = [dot_turned(cond, ref[...]) for ref in (gen_mod_ref, teacher_mod_ref, fake_mod_ref)]
    mods = jnp.concatenate([mods[0][0:3], mods[1][3:6], mods[2][3:6]], axis=0)
    mods = jnp.concatenate([mods, jnp.zeros((9, 32), F32)], axis=1)
    mods = jnp.concatenate([mods[:, 128 * p : 128 * (p + 1)] for p in range(4)] + [jnp.zeros((12, 128), F32)], axis=0)
    mine_ref[MODS_AT:] = mods.astype(BF16)
    other_ref[MODS_AT:] = mods.astype(BF16)
    first = place_ref[0] == 0
    mine, other = [], []
    for n, ref in enumerate((gen_ref, teacher_ref, fake_ref)):
        rows = slice(NOISE_ROWS + n * ROWS, NOISE_ROWS + (n + 1) * ROWS)
        low, high = ref[:, :128], ref[:, 256:]
        mine_ref[rows] = jnp.where(first, low, high)
        other_ref[rows] = jnp.where(first, high, low)
        low, high = ref[:, 128:192], ref[:, 192:256]
        mine.append(jnp.where(first, low, high))
        other.append(jnp.where(first, high, low))
    for ref, parts in ((mine_ref, mine), (other_ref, other)):
        ref[NOISE_ROWS + 3 * ROWS : NOISE_ROWS + 4 * ROWS] = jnp.concatenate(parts[1:], axis=1)
        ref[NOISE_ROWS + 4 * ROWS : MODS_AT] = jnp.concatenate([parts[0], parts[0]], axis=1)


def in_order(v, mine, other):
    return jnp.where(v == 0, mine, other), jnp.where(v == 0, other, mine)


def pack_kernel(place_ref, mine_ref, other_ref, gen_ref, score_ref):
    v = place_ref[0]
    cuts = [slice(NOISE_ROWS + n * ROWS, NOISE_ROWS + (n + 1) * ROWS) for n in range(5)]
    ordered = [in_order(v, mine_ref[rows], other_ref[rows]) for rows in cuts]
    parts = jnp.concatenate([ordered[4][0][:, :NARROW], ordered[4][1][:, :NARROW]], axis=1)
    mods = in_order(v, mine_ref[MODS_AT:].astype(F32), other_ref[MODS_AT:].astype(F32))
    mods = jnp.concatenate([mods[0][:MODS_ROWS], mods[1][:MODS_ROWS], jnp.zeros((8, 128), F32)], axis=0)
    gen = jnp.concatenate([*ordered[0], parts, mods.astype(BF16)], axis=0)
    score = jnp.concatenate([*ordered[1], *ordered[2], *ordered[3]], axis=0)
    for k in range(CHUNKS):
        gen_ref[k] = gen
        score_ref[k] = score


def generator_kernel(place_ref, own_ref, other_ref, embed_ref, mods_ref, final_ref, own_w_ref, other_w_ref,
                     part_ref, shaped_ref, pre_ref, res_ref, w_ref, gram_ref, mean_ref, sum_ref):
    i = pl.program_id(0)
    v = place_ref[0]

    @pl.when(i == 0)
    def _():
        embed_moments(embed_ref, gram_ref, mean_ref)
        unpack_weights(place_ref, own_w_ref, other_w_ref, 0, w_ref)
        sum_ref[:, 24:, :] = jnp.zeros((OWNERS, 8, 128), F32)

    x = jnp.concatenate(in_order(v, own_ref[:, :C], other_ref[:, :C]), axis=0)
    pre, res, partial, total, square = forward(
        x, embed_ref, mods_ref, final_ref, w_ref, gram_ref, mean_ref, shaped_ref.at[0], place_ref
    )
    pre_ref[0] = pre
    res_ref[0] = res
    pieces = owned(partial)
    pieces = jnp.concatenate([pieces[:, :8], pieces[:, 8:]], axis=2)
    rows = row_pieces([owned(total), owned(square)], 32)
    sum_ref[:, pl.ds(pl.multiple_of(i * 8, 8), 8), :] = pieces
    sum_ref[:, pl.ds(24 + i, 1), :] = rows[0]

    @pl.when(i == IMAGES - 1)
    def _():
        part_ref[...] = sum_ref[...].astype(BF16)


def samples_kernel(place_ref, time_ref, got_ref, noise_ref, mods_ref, final_ref,
                   out_ref, keep_ref, sums_ref):
    runs, scales, shifts = final_sums(mods_ref, final_ref)
    got = got_ref[...].astype(F32)
    packed = []
    for i in range(IMAGES):
        block = got[:, 8 * i : 8 * i + 8]
        partials = jnp.concatenate([block[:, :, :C], block[:, :, C:]], axis=1)
        row = got[:, 24 + i : 25 + i]
        row = row[:, :, :32] + row[:, :, 32:64] + row[:, :, 64:96]
        row = jnp.concatenate([row, jnp.zeros((OWNERS, 1, 96), F32)], axis=2)
        partial, average, inverse = add_up(partials, from_row(row, 0), from_row(row, 1), runs[i])
        inner = inverse * (partial - average * scales[i])
        velocity = inner + shifts[i]
        noise = noise_ref[pl.ds(pl.multiple_of(place_ref[3] + i * HALF, 16), OWNED), :][:, :C].astype(F32)
        samples = noise - time_ref[i] * velocity
        packed.append(jnp.concatenate([samples[:8], samples[8:]], axis=1))
        at = slice(i * OWNED, (i + 1) * OWNED)
        keep_ref[0, at, :] = samples
        keep_ref[1, at, :] = inner
        keep_ref[2, at, :] = jnp.broadcast_to(average, (OWNED, C))
        keep_ref[3, at, :] = jnp.broadcast_to(inverse, (OWNED, C))
    sums_ref[...] = jnp.concatenate(scales + [jnp.zeros((5, C), F32)], axis=0)
    out_ref[...] = jnp.broadcast_to(jnp.concatenate(packed, axis=0)[None], out_ref.shape)


def mix(samples, noise, t):
    return ((1.0 - t) * samples + t * noise).astype(BF16)


def score_kernel(place_ref, time_ref, got_ref, own_ref, other_ref,
                 t_embed_ref, f_embed_ref, t_mods_ref, f_mods_ref, t_final_ref, f_final_ref, own_w_ref, other_w_ref,
                 part_ref, samples_ref, shaped_ref, pre_ref, res_ref,
                 t_w_ref, f_w_ref, t_gram_ref, f_gram_ref, t_mean_ref, f_mean_ref, t_shaped_ref, sum_ref):
    i = pl.program_id(0)
    v = place_ref[0]

    @pl.when(i == 0)
    def _():
        embed_moments(t_embed_ref, t_gram_ref, t_mean_ref)
        embed_moments(f_embed_ref, f_gram_ref, f_mean_ref)
        unpack_weights(place_ref, own_w_ref, other_w_ref, 1, t_w_ref)
        unpack_weights(place_ref, own_w_ref, other_w_ref, 2, f_w_ref)
        sum_ref[:, 48:, :] = jnp.zeros((OWNERS, 16, 128), F32)
    got = got_ref[:, pl.ds(pl.multiple_of(i * 8, 8), 8), :]
    samples = jnp.concatenate([got[:, :, :C], got[:, :, C:]], axis=1).reshape(TOKENS, C)
    turned = jnp.concatenate([samples[:HALF], samples[HALF:]], axis=1).T
    samples_ref[0] = jnp.where(v == 0, turned[:C], turned[C:])
    own, other = own_ref[:, C:].astype(F32), other_ref[:, C:].astype(F32)
    noise = jnp.concatenate(in_order(v, own, other), axis=0)
    noised = mix(samples, noise, time_ref[i])
    _, _, t_partial, t_total, t_square = forward(
        noised, t_embed_ref, t_mods_ref, t_final_ref, t_w_ref, t_gram_ref, t_mean_ref, t_shaped_ref, place_ref
    )
    pre, res, f_partial, f_total, f_square = forward(
        noised, f_embed_ref, f_mods_ref, f_final_ref, f_w_ref, f_gram_ref, f_mean_ref, shaped_ref.at[0], place_ref
    )
    pre_ref[0] = pre
    res_ref[0] = res
    rows = row_pieces([owned(v) for v in (t_total, t_square, f_total, f_square)], 64)
    sum_ref[:, pl.ds(pl.multiple_of(i * 16, 16), 16), :] = owned(jnp.concatenate([t_partial, f_partial], axis=1))
    for n in range(2):
        sum_ref[:, pl.ds(48 + 2 * i + n, 1), :] = rows[n]

    @pl.when(i == IMAGES - 1)
    def _():
        part_ref[...] = sum_ref[...].astype(BF16)


def cotangent_kernel(place_ref, gen_time_ref, time_ref, got_ref, noise_ref, keep_ref, sums_ref,
                     t_mods_ref, f_mods_ref, t_final_ref, f_final_ref, out_ref):
    loss_scale = 1.0 / math.sqrt(IMAGES * S)
    t_runs, t_scales, t_shifts = final_sums(t_mods_ref, t_final_ref)
    f_runs, f_scales, f_shifts = final_sums(f_mods_ref, f_final_ref)
    got = got_ref[...].astype(F32)
    lane = lax.broadcasted_iota(jnp.int32, (1, 128), 1)
    cots, rows = [], []
    for i in range(IMAGES):
        block = got[:, 16 * i : 16 * i + 16]
        row = got[:, 48 + 2 * i : 50 + 2 * i]
        row = row[:, :1, :64] + row[:, :1, 64:] + row[:, 1:, :64]
        row = jnp.concatenate([row, jnp.zeros((OWNERS, 1, 64), F32)], axis=2)

        def inner(partials, k, runs, scale):
            partial, average, inverse = add_up(partials, from_row(row, k), from_row(row, k + 1), runs)
            return inverse * (partial - average * scale), average, inverse

        t_inner, _, _ = inner(block[:, :, :C], 0, t_runs[i], t_scales[i])
        f_inner, f_average, f_inverse = inner(block[:, :, C:], 2, f_runs[i], f_scales[i])
        teacher, fake = t_inner + t_shifts[i], f_inner + f_shifts[i]
        at = slice(i * OWNED, (i + 1) * OWNED)
        samples, g_inner = keep_ref[0, at, :], keep_ref[1, at, :]
        g_average, g_inverse = keep_ref[2, at, 0:1], keep_ref[3, at, 0:1]
        noise = noise_ref[pl.ds(pl.multiple_of(place_ref[3] + i * HALF, 16), OWNED), :][:, C:].astype(F32)
        t = time_ref[i]
        noised = mix(samples, noise, t).astype(F32)
        distance = jnp.sum(jnp.abs(samples - noised + t * teacher))
        gen_cot = (-(gen_time_ref[i] * t * loss_scale) * (teacher - fake)).astype(BF16).astype(F32)
        fake_cot = (loss_scale * (fake - noise + samples)).astype(BF16).astype(F32)
        numbers = []
        for cot, column, value, average, inverse in (
            (fake_cot, f_scales[i], f_inner, f_average, f_inverse),
            (gen_cot, sums_ref[i : i + 1, :], g_inner, g_average, g_inverse),
        ):
            first = jnp.sum(cot * column, axis=1, keepdims=True) / D
            second = jnp.sum(cot * value, axis=1, keepdims=True) / D
            slope = inverse * inverse * second
            numbers += [inverse, slope, average * slope - inverse * first]
        cots.append(jnp.concatenate([fake_cot, gen_cot], axis=1))
        numbers_row = to_row([number[None] for number in numbers])[0]
        numbers_row = jnp.where(lane == 96, distance, numbers_row)
        for _ in range(3):
            rounded = numbers_row.astype(BF16).astype(F32)
            rows.append(rounded)
            numbers_row = numbers_row - rounded
    rows.append(jnp.zeros((7, 128), F32))
    packed = jnp.concatenate(cots + rows, axis=0).astype(BF16)
    out_ref[...] = jnp.broadcast_to(packed[None], out_ref.shape)


def gelu_slope(v):
    a, b = math.sqrt(2.0 / math.pi), 0.044715
    t = jnp.tanh(a * (v + b * (v * v * v)))
    return 0.5 * (1.0 + t) + 0.5 * v * (1.0 - t * t) * (a * (1.0 + 3.0 * b * (v * v)))


def gradient_kernel(net, place_ref, got_ref, *refs):
    gap_ref, refs = (refs[0], refs[1:]) if net == 1 else (None, refs)
    mods_ref, final_ref, pre_ref, res_ref, shaped_ref, keep_ref, send_ref, left_ref = refs

    @pl.when(pl.program_id(0) == 0)
    def _():
        final = local_lanes(lambda at: final_ref[:, at], place_ref)
        if net == 1:
            gaps = jnp.sum(gap_ref[...], axis=0)
        for i in range(IMAGES):
            row = got_ref[:, 48:64, :].astype(F32)
            row = row[:, 3 * i : 3 * i + 1] + row[:, 3 * i + 1 : 3 * i + 2] + row[:, 3 * i + 2 : 3 * i + 3]
            inverse, slope, offset = [from_row(row, 3 * net + k).reshape(TOKENS, 1) for k in range(3)]
            cot = got_ref[:, 16 * i : 16 * i + 16, :].reshape(TOKENS, 128)[:, net * C : (net + 1) * C]
            out_grad = dot(cot, final)
            scale = local_lanes(lambda at: mods_ref[i, 4:5, at], place_ref)
            gate = local_lanes(lambda at: mods_ref[i, 2:3, at], place_ref)
            res_grad = inverse * (out_grad * (1.0 + scale)) - slope * res_ref[i] + offset
            act_grad = res_grad * gate
            if net == 1:
                inverse_gap = 1.0 / (gaps[i : i + 1, :] / (S * C) + gap_epsilon)
                act_grad = act_grad * jnp.concatenate([inverse_gap, inverse_gap[:, :NARROW]], axis=1)
            grad = act_grad * gelu_slope(pre_ref[i])
            turned = jnp.concatenate([grad, jnp.zeros((TOKENS, NARROW), F32)], axis=1).T
            left_ref[:, i * TOKENS : (i + 1) * TOKENS] = turned[:COLS].astype(BF16)

    grad = dot(left_ref[...], shaped_ref[...].reshape(IMAGES * TOKENS, 768))
    tiles = grad[:WIDE].T.astype(BF16)
    parts = jnp.concatenate([grad[WIDE:, :384], grad[WIDE:, 384:]], axis=0).T.astype(BF16)
    first = place_ref[4] == 0
    for w in range(2):
        sides = []
        for h in range(2):
            at = [(v * 2 + w) * ROWS for v in range(2)]
            lanes = slice(h * NARROW, (h + 1) * NARROW)
            narrow = jnp.concatenate([parts[k : k + ROWS, lanes] for k in at], axis=1)
            sides.append([tiles[h * 384 + k : h * 384 + k + ROWS] for k in at] + [narrow])
        for n, (low, high) in enumerate(zip(*sides, strict=True)):
            keep_ref[w, n * ROWS : (n + 1) * ROWS, :] = jnp.where(first, low, high)
            send_ref[w, n * ROWS : (n + 1) * ROWS, :] = jnp.where(first, high, low)


def sum_kernel(place_ref, got_ref, keep_ref, send_ref):
    v = place_ref[0]
    for n in range(2):
        rows = slice(n * GEN_ROWS, (n + 1) * GEN_ROWS)
        total = got_ref[0, rows].astype(F32)
        for k in range(1, CHUNKS):
            total = total + got_ref[k, rows].astype(F32)
        def folded(rows, part):
            return jnp.concatenate([rows, jnp.concatenate([part[:48], part[48:]], axis=1)], axis=0)

        low = folded(total[:ROWS], total[2 * ROWS :, :NARROW])
        high = folded(total[ROWS : 2 * ROWS], total[2 * ROWS :, NARROW:])
        keep_ref[n] = jnp.where(v == 0, low, high)
        send_ref[n] = jnp.where(v == 0, high, low)


def place_kernel(place_ref, keep_ref, other_ref, fake_ref, gen_ref):
    for n, ref in enumerate((fake_ref, gen_ref)):
        low, high = in_order(place_ref[0], keep_ref[n], other_ref[n])
        ref[:, :128] = low[:ROWS]
        ref[:48, 128:256] = jnp.concatenate([low[ROWS:, :NARROW], high[ROWS:, :NARROW]], axis=1)
        ref[48:, 128:256] = jnp.concatenate([low[ROWS:, NARROW:], high[ROWS:, NARROW:]], axis=1)
        ref[:, 256:] = high[:ROWS]


def in_hbm(*arrays):
    return [pltpu.with_memory_space_constraint(a, pltpu.HBM) for a in arrays]


def exchange(value, axes):
    return lax.all_to_all(value, axes, 0, 0)


def shards(
    gen_noise,
    score_noise,
    gen_steps,
    score_steps,
    gen_embed,
    gen_modulation,
    gen_proj,
    gen_final,
    teacher_embed,
    teacher_modulation,
    teacher_proj,
    teacher_final,
    fake_embed,
    fake_modulation,
    fake_proj,
    fake_final,
):
    v, s = lax.axis_index("v"), lax.axis_index("s")
    start = lax.axis_index(("g", "h")) * 384
    member = lax.axis_index(("h", "g"))
    place = jnp.stack([v, start + 256 * v, start + 128, member * OWNED, s]).astype(jnp.int32)
    gen_final, teacher_final, fake_final = gen_final.T, teacher_final.T, fake_final.T

    times, conds = time_features(jnp.concatenate([gen_steps, score_steps]), gen_modulation.shape[0])
    gen_time, score_time = times[:3], times[3:]
    halves = jax.ShapeDtypeStruct((SENT_ROWS, 128), BF16)
    mine, other = pl.pallas_call(
        split_kernel,
        grid=(1,),
        in_specs=[smem(), whole((6, 256))] + [whole((IMAGES, C, HALF))] * 2 + [whole((ROWS, 384))] * 3
        + [whole((480, 256))] * 3,
        out_specs=[whole((SENT_ROWS, 128))] * 2,
        out_shape=[halves, halves],
        compiler_params=params(60),
        name="split",
    )(place, conds, gen_noise.transpose(0, 2, 1), score_noise.transpose(0, 2, 1), gen_proj, teacher_proj, fake_proj,
      gen_modulation.T, teacher_modulation.T, fake_modulation.T)
    mine = lax.ppermute(mine, PLACES, SWAP)
    other = lax.ppermute(other, PLACES, SWAP_TURNED)

    g_packed, packed = pl.pallas_call(
        pack_kernel,
        grid=(1,),
        in_specs=[smem()] + [whole((SENT_ROWS, 128))] * 2,
        out_specs=[whole((CHUNKS, GEN_CHUNK, 128)), whole((CHUNKS, SCORE_ROWS, 128))],
        out_shape=[
            jax.ShapeDtypeStruct((CHUNKS, GEN_CHUNK, 128), BF16),
            jax.ShapeDtypeStruct((CHUNKS, SCORE_ROWS, 128), BF16),
        ],
        compiler_params=params(6),
        name="pack",
    )(place, mine, other)
    g_packed = exchange(g_packed, GATHER)
    g_other = lax.ppermute(g_packed, "s", SIBLING)
    packed, g_packed, g_other = lax.optimization_barrier((packed, g_packed, g_other))
    packed = exchange(packed, GATHER)
    low, high = (a[:, GEN_ROWS : GEN_ROWS + 2 * MODS_ROWS] for a in in_order(s, g_packed, g_other))
    mods = jnp.stack([low, high]).reshape(2, 4, 2, 2, 4, 9, 128).transpose(5, 1, 0, 3, 2, 4, 6)
    mods = mods.reshape(9, 32, 512)[:, :, :480].reshape(9, 5, D).astype(F32)
    mods = jnp.pad(mods, ((0, 0), (0, 3), (0, 0)))

    by_image = lambda *shape: pl.BlockSpec((1, *shape), lambda i: (i,) + (0,) * len(shape))
    noise_rows = pl.BlockSpec((HALF, 128), lambda i: (i, 0))
    mods_of = lambda net: pl.BlockSpec((1, 8, D), lambda i: (3 * net + i, 0, 0))
    local = pltpu.HBM((IMAGES, TOKENS, COLS), F32)
    wide = pltpu.HBM((IMAGES, TOKENS, D), BF16)
    gen_embed, teacher_embed, fake_embed = in_hbm(gen_embed, teacher_embed, fake_embed)
    gen_final, teacher_final, fake_final = in_hbm(gen_final, teacher_final, fake_final)

    part, g_shaped, g_pre, g_res = pl.pallas_call(
        generator_kernel,
        grid=(IMAGES,),
        in_specs=[
            smem(), noise_rows, noise_rows, whole((C, D)), mods_of(0), whole((C, D)),
            *([whole((CHUNKS, GEN_CHUNK, 128))] * 2),
        ],
        out_specs=[whole((OWNERS, 32, 128)), by_image(TOKENS, D), by_image(TOKENS, COLS), by_image(TOKENS, COLS)],
        out_shape=[jax.ShapeDtypeStruct((OWNERS, 32, 128), BF16), wide, local, local],
        scratch_shapes=[pltpu.VMEM((D, COLS), BF16), pltpu.VMEM((C, 3 * C), BF16), pltpu.VMEM((C, 128), F32),
                        pltpu.VMEM((OWNERS, 32, 128), F32)],
        compiler_params=params(16),
        cost_estimate=pl.CostEstimate(flops=12 * 10**9, bytes_accessed=30 * 10**6, transcendentals=0),
        name="generator",
    )(place, mine, other, gen_embed, mods, gen_final, g_packed, g_other)
    packed, part = lax.optimization_barrier((packed, part))
    part = exchange(part, COMBINE)

    net_mods = lambda net: pl.BlockSpec((IMAGES, 8, D), lambda *_: (net, 0, 0))
    pack1, keep, sums = pl.pallas_call(
        samples_kernel,
        grid=(1,),
        in_specs=[
            smem(), smem(), whole((OWNERS, 32, 128)), whole((NOISE_ROWS, 128)), net_mods(0), whole((C, D)),
        ],
        out_specs=[whole((OWNERS, 24, 128)), whole((4, 48, C)), whole((8, C))],
        out_shape=[
            jax.ShapeDtypeStruct((OWNERS, 24, 128), F32),
            jax.ShapeDtypeStruct((4, 48, C), F32),
            jax.ShapeDtypeStruct((8, C), F32),
        ],
        compiler_params=params(5),
        name="samples",
    )(place, gen_time, part, mine, mods, gen_final)
    packed, pack1 = lax.optimization_barrier((packed, pack1))
    pack1 = exchange(pack1, COMBINE)
    other_packed = lax.ppermute(packed, "s", SIBLING)

    part2, samples, f_shaped, f_pre, f_res = pl.pallas_call(
        score_kernel,
        grid=(IMAGES,),
        in_specs=[
            smem(), smem(), whole((OWNERS, 24, 128)), noise_rows, noise_rows,
            whole((C, D)), whole((C, D)), mods_of(1), mods_of(2), whole((C, D)), whole((C, D)),
            *([whole((CHUNKS, SCORE_ROWS, 128))] * 2),
        ],
        out_specs=[
            whole((OWNERS, 64, 128)), by_image(C, HALF), by_image(TOKENS, D), by_image(TOKENS, COLS),
            by_image(TOKENS, COLS),
        ],
        out_shape=[
            jax.ShapeDtypeStruct((OWNERS, 64, 128), BF16),
            jax.ShapeDtypeStruct((IMAGES, C, HALF), F32),
            wide, local, local,
        ],
        scratch_shapes=[
            *([pltpu.VMEM((D, COLS), BF16)] * 2), *([pltpu.VMEM((C, 3 * C), BF16)] * 2),
            *([pltpu.VMEM((C, 128), F32)] * 2), pltpu.VMEM((TOKENS, D), BF16),
            pltpu.VMEM((OWNERS, 64, 128), F32),
        ],
        compiler_params=params(22),
        cost_estimate=pl.CostEstimate(flops=24 * 10**9, bytes_accessed=50 * 10**6, transcendentals=0),
        name="score",
    )(place, score_time, pack1, mine, other, teacher_embed, fake_embed, mods, mods,
      teacher_final, fake_final, packed, other_packed)
    part2 = exchange(part2, COMBINE)

    pack2 = pl.pallas_call(
        cotangent_kernel,
        grid=(1,),
        in_specs=[
            smem(), smem(), smem(), whole((OWNERS, 64, 128)), whole((NOISE_ROWS, 128)), whole((4, 48, C)),
            whole((8, C)), net_mods(1), net_mods(2), whole((C, D)), whole((C, D)),
        ],
        out_specs=whole((OWNERS, 64, 128)),
        out_shape=jax.ShapeDtypeStruct((OWNERS, 64, 128), BF16),
        compiler_params=params(6),
        name="cotangents",
    )(place, gen_time, score_time, part2, mine, keep, sums, mods, mods, teacher_final, fake_final)
    pack2 = exchange(pack2, COMBINE)
    samples, pack2 = lax.optimization_barrier((samples, pack2))
    samples = lax.ppermute(samples, PLACES, SWAP)

    gap = jnp.sum(pack2[:, 48:57, 96].astype(F32).reshape(OWNERS, 3, 3), axis=(0, 2))
    gap = jnp.broadcast_to(jnp.pad(gap, (0, 5))[None, :, None], (16, 8, 128))
    gap = exchange(gap, TOKEN_AXES)

    by_columns = pl.BlockSpec((IMAGES, TOKENS, 768), lambda x: (0, 0, x))
    partial = jax.ShapeDtypeStruct((CHUNKS, GEN_ROWS, 128), BF16)
    partial_spec = pl.BlockSpec((2, GEN_ROWS, 128), lambda x: (x, 0, 0))

    def gradient(net, gaps, mods_net, final, pre, res, shaped):
        kept, sent = pl.pallas_call(
            functools.partial(gradient_kernel, net),
            grid=(4,),
            in_specs=[
                smem(), whole((OWNERS, 64, 128)), *([whole((16, 8, 128))] * len(gaps)), net_mods(mods_net),
                whole((C, D)), *([whole((IMAGES, TOKENS, COLS))] * 2), by_columns,
            ],
            out_specs=[partial_spec, partial_spec],
            out_shape=[partial, partial],
            scratch_shapes=[pltpu.VMEM((COLS, IMAGES * TOKENS), BF16)],
            compiler_params=params(13),
            cost_estimate=pl.CostEstimate(flops=7 * 10**9, bytes_accessed=20 * 10**6, transcendentals=0),
        name="gradient",
        )(place, pack2, *gaps, mods, final, *in_hbm(pre, res, shaped))
        return kept, lax.ppermute(sent, "s", SIBLING)

    pieces = gradient(0, (), 2, fake_final, f_pre, f_res, f_shaped)
    pieces += gradient(1, (gap,), 0, gen_final, g_pre, g_res, g_shaped)
    both = jnp.concatenate(
        [(pieces[n].astype(F32) + pieces[n + 1].astype(F32)).astype(BF16) for n in (0, 2)], axis=1
    )
    samples, both = lax.optimization_barrier((samples, both))
    samples = samples.transpose(0, 2, 1)
    tiles = jax.ShapeDtypeStruct((2, 144, 128), F32)
    kept, sent = pl.pallas_call(
        sum_kernel,
        grid=(1,),
        in_specs=[smem(), whole((CHUNKS, 2 * GEN_ROWS, 128))],
        out_specs=[whole((2, 144, 128))] * 2,
        out_shape=[tiles, tiles],
        compiler_params=params(8),
        name="sum",
    )(place, exchange(both, GATHER))
    kept = lax.ppermute(kept, PLACES, SWAP)
    sent = lax.ppermute(sent, PLACES, SWAP_TURNED)
    fake_grad, gen_grad = pl.pallas_call(
        place_kernel,
        grid=(1,),
        in_specs=[smem(), whole((2, 144, 128)), whole((2, 144, 128))],
        out_specs=[whole((ROWS, 384))] * 2,
        out_shape=[jax.ShapeDtypeStruct((ROWS, 384), F32)] * 2,
        compiler_params=params(4),
        name="place",
    )(place, kept, sent)
    return (samples, gen_grad, fake_grad)


def solution(mesh):
    split = Mesh(mesh.devices.reshape(4, 4, 2, 2, 2, 2), ("g", "x", "h", "v", "w", "s"))
    tokens = P(None, ROW_AXES, None)
    columns = P(None, ROW_AXES)
    block = P(ROW_AXES, ("g", "s"))
    net = (P(), columns, block, P())
    return jax.shard_map(
        shards,
        mesh=split,
        in_specs=(tokens, tokens, P(), P(), *net, *net, *net),
        out_specs=(tokens, block, block),
        check_vma=False,
    )
```

```python
import functools
import math

import jax
import jax.numpy as jnp
from jax import lax
from jax.experimental import pallas as pl
from jax.experimental.pallas import tpu as pltpu
from jax.sharding import Mesh
from jax.sharding import PartitionSpec as P

S = 4096
STEPS = 1000
D = 3072
C = 64
IMAGES = 3

norm_epsilon = 1e-06
gap_epsilon = 1e-05

F32 = jnp.float32
BF16 = jnp.bfloat16

GATHER = ("x", "w")
ROW_AXES = ("x", "h", "w", "v")
COMBINE = ("v", "h", "g")
TOKEN_AXES = ("x", "w", "s")
OWNERS = 16
TOKENS = 256
HALF = 128
OWNED = 16
ROWS = 96
WIDE = 128
NARROW = 64
COLS = WIDE + NARROW
GEN_ROWS = 288
NOISE_ROWS = 384
MODS_AT = 480
MODS_ROWS = 36
SENT_ROWS = 528
GEN_CHUNK = 368
SCORE_ROWS = 576
CHUNKS = 8
BLOCK = 512

PLACES = ("g", "h", "v", "s")


def number(g, h, v, s):
    return g * 8 + h * 4 + v * 2 + s


EVERY = [(g, h, v, s) for g in range(4) for h in range(2) for v in range(2) for s in range(2)]
SWAP, SWAP_TURNED = [
    [(number(g, h, v, s), number((g + 2) % 4, s, v ^ turn, h)) for g, h, v, s in EVERY] for turn in range(2)
]
NEAR, NEAR_TURNED = [
    [(number(g, h, v, s), number(g if h == s else 3 - g, s, v ^ turn, h)) for g, h, v, s in EVERY] for turn in range(2)
]
SIBLING = [(0, 1), (1, 0)]


def params(mib):
    return pltpu.CompilerParams(vmem_limit_bytes=mib * 1024 * 1024)


def smem():
    return pl.BlockSpec(memory_space=pltpu.SMEM)


def whole(shape):
    zeros = (0,) * len(shape)
    return pl.BlockSpec(shape, lambda *_: zeros)


def dot(a, b):
    return jnp.dot(a, b, preferred_element_type=F32)


def dot_turned(a, b):
    return lax.dot_general(a, b, (((1,), (1,)), ((), ())), preferred_element_type=F32)


def time_features(steps, embed_width):
    times = (steps.astype(F32) + 1.0) / (STEPS + 1.0)
    half = embed_width // 2
    frequency = jnp.exp(-jnp.log(10000.0) * jnp.arange(half, dtype=F32) / half)
    angles = 1000.0 * times[:, None] * frequency[None, :]
    embedding = jnp.concatenate([jnp.cos(angles), jnp.sin(angles)], axis=1)
    return (times, jax.nn.silu(embedding).astype(BF16))


def to_row(numbers):
    shape = (numbers[0].shape[0], OWNED, 128)
    lane = lax.broadcasted_iota(jnp.int32, shape, 2)
    token = lax.broadcasted_iota(jnp.int32, shape, 1)
    total = jnp.zeros(shape, F32)
    for k, number in enumerate(numbers):
        total = jnp.where(lane == token + OWNED * k, number, total)
    return jnp.sum(total, axis=1, keepdims=True)


def row_pieces(numbers, stride):
    row = to_row(numbers)
    per_row = 128 // stride
    rows = [row.astype(BF16).astype(F32)]
    row = row - rows[0]
    rows.append(row.astype(BF16).astype(F32))
    rows.append((row - rows[1]).astype(BF16).astype(F32))
    packed = [jnp.concatenate([r[:, :, :stride] for r in rows[:per_row]], axis=2)]
    if len(rows) > per_row:
        packed.append(jnp.concatenate([rows[per_row][:, :, :stride], jnp.zeros_like(row)[:, :, : 128 - stride]], axis=2))
    else:
        packed[0] = jnp.concatenate([packed[0], jnp.zeros_like(row)[:, :, : 128 - 3 * stride]], axis=2)
    return packed


def from_row(row, k):
    shape = (row.shape[0], OWNED, 128)
    lane = lax.broadcasted_iota(jnp.int32, shape, 2)
    token = lax.broadcasted_iota(jnp.int32, shape, 1)
    return jnp.sum(jnp.where(lane == token + OWNED * k, row, 0.0), axis=2, keepdims=True)


def local_lanes(load, place_ref):
    tile = load(pl.ds(pl.multiple_of(place_ref[1], 128), 128))
    middle = load(pl.ds(pl.multiple_of(place_ref[2], 128), 128))
    part = jnp.where(place_ref[0] == 0, middle[:, :NARROW], middle[:, NARROW:])
    return jnp.concatenate([tile, part], axis=1)


def unpack_weights(place_ref, own_ref, other_ref, net, w_ref):
    s = place_ref[4]
    for packed_ref, side in ((own_ref, s), (other_ref, 1 - s)):
        for chunk in range(CHUNKS):
            x, w = chunk // 2, chunk % 2
            for v in range(2):
                k = pl.multiple_of((x * 8 + w * 2 + v) * ROWS + side * (4 * ROWS), 32)
                first = max(net - 1, 0) * 192 + v * ROWS
                w_ref[pl.ds(k, ROWS), :WIDE] = packed_ref[chunk, first : first + ROWS, :]
                if net == 0:
                    part = packed_ref[chunk, 192:288, v * NARROW : (v + 1) * NARROW]
                else:
                    part = packed_ref[chunk, 384 + v * ROWS : 384 + (v + 1) * ROWS, (net - 1) * NARROW : net * NARROW]
                w_ref[pl.ds(k, ROWS), WIDE:] = part


def split_bits(value, count):
    pieces = []
    for _ in range(count):
        piece = value.astype(BF16)
        pieces.append(piece)
        value = value - piece.astype(F32)
    return pieces


def embed_moments(embed_ref, gram_ref, mean_ref):
    embed = embed_ref[...]
    ones = jnp.ones((8, D), BF16)
    column = dot_turned(embed, ones)[:, 0:1] / D
    row = dot_turned(ones, embed)[0:1] / D
    gram = dot_turned(embed, embed) / D - column * row
    gram_ref[...] = jnp.concatenate(split_bits(gram, 3), axis=1)
    mean_ref[...] = jnp.broadcast_to(column, mean_ref.shape)


def forward(x, embed_ref, mods_ref, final_ref, w_ref, gram_ref, mean_ref, shaped_ref, place_ref):
    turned = dot(x, gram_ref[...])
    turned = turned[:, :C] + turned[:, C : 2 * C] + turned[:, 2 * C :]
    inverse = lax.rsqrt(jnp.sum(turned * x.astype(F32), axis=1, keepdims=True) + norm_epsilon)
    inverse = jnp.broadcast_to(inverse, (TOKENS, BLOCK))
    twice = jnp.concatenate([x, x], axis=1)
    mean = mean_ref[:, 0:1]
    preactivation = jnp.zeros((TOKENS, COLS), F32)
    for b in range(D // BLOCK):
        cut = slice(b * BLOCK, (b + 1) * BLOCK)
        scaled = (embed_ref[:, cut].astype(F32) - mean) * (1.0 + mods_ref[0, 1:2, cut])
        scaled = jnp.concatenate(split_bits(scaled, 2), axis=0)
        shaped = (dot(twice, scaled) * inverse + mods_ref[0, 0:1, cut]).astype(BF16)
        shaped_ref[:, cut] = shaped
        preactivation = preactivation + dot(shaped, w_ref[cut, :])
    activated = jax.nn.gelu(preactivation, approximate=True).astype(BF16).astype(F32)
    own_hidden = dot(x, local_lanes(lambda at: embed_ref[:, at], place_ref))
    gate = local_lanes(lambda at: mods_ref[0, 2:3, at], place_ref)
    scale = local_lanes(lambda at: mods_ref[0, 4:5, at], place_ref)
    residual = own_hidden + gate * activated
    total = jnp.sum(residual, axis=1, keepdims=True)
    total_square = jnp.sum(residual * residual, axis=1, keepdims=True)
    own_mean = total / COLS
    final = local_lanes(lambda at: final_ref[:, at], place_ref)
    centred = ((residual - own_mean) * (1.0 + scale)).astype(BF16)
    partial = dot_turned(centred, final)
    return preactivation, residual, partial, total, total_square


def owned(value):
    return value.reshape(OWNERS, OWNED, value.shape[-1])


def sums_kernel(g_final_ref, t_final_ref, f_final_ref, mods_ref, out_ref):
    run = lax.broadcasted_iota(jnp.int32, (OWNERS, D), 1) // COLS
    own = run == lax.broadcasted_iota(jnp.int32, (OWNERS, D), 0)
    for net, final_ref in enumerate((g_final_ref, t_final_ref, f_final_ref)):
        scales = [mods_ref[3 * net + i, 4:5, :] for i in range(IMAGES)]
        shifts = [mods_ref[3 * net + i, 3:4, :] for i in range(IMAGES)]
        left = [jnp.where(own, row, 0.0) for row in scales + [jnp.ones((1, D), F32)]]
        left = jnp.concatenate(left + shifts + [jnp.zeros((5, D), F32)], axis=0).astype(BF16)
        sums = dot_turned(left, final_ref[...])
        ones = sums[3 * OWNERS : 4 * OWNERS]
        runs = [sums[i * OWNERS : (i + 1) * OWNERS] + ones for i in range(IMAGES)]
        totals = [jnp.sum(r, axis=0, keepdims=True) for r in runs]
        out_ref[net] = jnp.concatenate(runs + totals + [sums[64:67], jnp.zeros((2, C), F32)], axis=0)


def read_sums(sums_ref, net):
    runs = [sums_ref[net, i * OWNERS : (i + 1) * OWNERS] for i in range(IMAGES)]
    return runs, [sums_ref[net, 48 + i : 49 + i] for i in range(IMAGES)], [sums_ref[net, 51 + i : 52 + i] for i in range(IMAGES)]


def add_up(partials, totals, squares, runs):
    means = totals * (1.0 / COLS)
    ordered = [((g + 2) % 4 * 2 + h) * 2 + v for v in range(2) for h in range(2) for g in range(4)]
    ordered = jnp.concatenate([runs[run : run + 1][None] for run in ordered], axis=0)
    partial = jnp.sum(partials + means * ordered, axis=0)
    average = jnp.sum(totals, axis=0) / D
    inverse = lax.rsqrt(jnp.sum(squares, axis=0) / D - average * average + norm_epsilon)
    return partial, average, inverse


def split_kernel(place_ref, cond_ref, gen_noise_ref, score_noise_ref, gen_ref, teacher_ref, fake_ref,
                 gen_mod_ref, teacher_mod_ref, fake_mod_ref, mine_ref, other_ref, noise_ref):
    for i in range(IMAGES):
        noise = jnp.concatenate([gen_noise_ref[i], score_noise_ref[i]], axis=0).astype(F32).T.astype(BF16)
        noise_ref[i * HALF : (i + 1) * HALF] = noise
    cond = cond_ref[...]
    mods = [dot_turned(cond, ref[...]) for ref in (gen_mod_ref, teacher_mod_ref, fake_mod_ref)]
    mods = jnp.concatenate([mods[0][0:3], mods[1][3:6], mods[2][3:6]], axis=0)
    mods = jnp.concatenate([mods, jnp.zeros((9, 32), F32)], axis=1)
    mods = jnp.concatenate([mods[:, 128 * p : 128 * (p + 1)] for p in range(4)] + [jnp.zeros((12, 128), F32)], axis=0)
    mine_ref[MODS_AT:] = mods.astype(BF16)
    other_ref[MODS_AT:] = mods.astype(BF16)
    first = place_ref[0] == 0
    mine, other = [], []
    for n, ref in enumerate((gen_ref, teacher_ref, fake_ref)):
        rows = slice(n * ROWS, (n + 1) * ROWS)
        low, high = ref[:, :128], ref[:, 256:]
        mine_ref[rows] = jnp.where(first, low, high)
        other_ref[rows] = jnp.where(first, high, low)
        low, high = ref[:, 128:192], ref[:, 192:256]
        mine.append(jnp.where(first, low, high))
        other.append(jnp.where(first, high, low))
    for ref, parts in ((mine_ref, mine), (other_ref, other)):
        ref[3 * ROWS : 4 * ROWS] = jnp.concatenate(parts[1:], axis=1)
        ref[4 * ROWS : MODS_AT] = jnp.concatenate([parts[0], parts[0]], axis=1)


def in_order(v, mine, other):
    return jnp.where(v == 0, mine, other), jnp.where(v == 0, other, mine)


def pack_kernel(place_ref, mine_ref, other_ref, gen_ref, score_ref):
    v = place_ref[0]
    cuts = [slice(n * ROWS, (n + 1) * ROWS) for n in range(5)]
    ordered = [in_order(v, mine_ref[rows], other_ref[rows]) for rows in cuts]
    parts = jnp.concatenate([ordered[4][0][:, :NARROW], ordered[4][1][:, :NARROW]], axis=1)
    mods = in_order(v, mine_ref[MODS_AT:].astype(F32), other_ref[MODS_AT:].astype(F32))
    mods = jnp.concatenate([mods[0][:MODS_ROWS], mods[1][:MODS_ROWS], jnp.zeros((8, 128), F32)], axis=0)
    gen = jnp.concatenate([*ordered[0], parts, mods.astype(BF16)], axis=0)
    score = jnp.concatenate([*ordered[1], *ordered[2], *ordered[3]], axis=0)
    for k in range(CHUNKS):
        gen_ref[k] = gen
        score_ref[k] = score


def generator_kernel(place_ref, own_ref, other_ref, embed_ref, mods_ref, final_ref, own_w_ref, other_w_ref,
                     part_ref, shaped_ref, pre_ref, res_ref, w_ref, gram_ref, mean_ref, sum_ref):
    i = pl.program_id(0)
    v = place_ref[0]

    @pl.when(i == 0)
    def _():
        embed_moments(embed_ref, gram_ref, mean_ref)
        unpack_weights(place_ref, own_w_ref, other_w_ref, 0, w_ref)
        sum_ref[:, 24:, :] = jnp.zeros((OWNERS, 8, 128), F32)

    x = jnp.concatenate(in_order(v, own_ref[:, :C], other_ref[:, :C]), axis=0)
    pre, res, partial, total, square = forward(
        x, embed_ref, mods_ref, final_ref, w_ref, gram_ref, mean_ref, shaped_ref.at[0], place_ref
    )
    pre_ref[0] = pre
    res_ref[0] = res
    pieces = owned(partial)
    pieces = jnp.concatenate([pieces[:, :8], pieces[:, 8:]], axis=2)
    rows = row_pieces([owned(total), owned(square)], 32)
    sum_ref[:, pl.ds(pl.multiple_of(i * 8, 8), 8), :] = pieces
    sum_ref[:, pl.ds(24 + i, 1), :] = rows[0]

    @pl.when(i == IMAGES - 1)
    def _():
        part_ref[...] = sum_ref[...].astype(BF16)


def samples_kernel(place_ref, time_ref, got_ref, noise_ref, sums_ref, out_ref, keep_ref):
    runs, scales, shifts = read_sums(sums_ref, 0)
    got = got_ref[...].astype(F32)
    packed = []
    for i in range(IMAGES):
        block = got[:, 8 * i : 8 * i + 8]
        partials = jnp.concatenate([block[:, :, :C], block[:, :, C:]], axis=1)
        row = got[:, 24 + i : 25 + i]
        row = row[:, :, :32] + row[:, :, 32:64] + row[:, :, 64:96]
        row = jnp.concatenate([row, jnp.zeros((OWNERS, 1, 96), F32)], axis=2)
        partial, average, inverse = add_up(partials, from_row(row, 0), from_row(row, 1), runs[i])
        inner = inverse * (partial - average * scales[i])
        velocity = inner + shifts[i]
        noise = noise_ref[pl.ds(pl.multiple_of(place_ref[3] + i * HALF, 16), OWNED), :][:, :C].astype(F32)
        samples = noise - time_ref[i] * velocity
        packed.append(jnp.concatenate([samples[:8], samples[8:]], axis=1))
        at = slice(i * OWNED, (i + 1) * OWNED)
        keep_ref[0, at, :] = samples
        keep_ref[1, at, :] = inner
        keep_ref[2, at, :] = jnp.broadcast_to(average, (OWNED, C))
        keep_ref[3, at, :] = jnp.broadcast_to(inverse, (OWNED, C))
    out_ref[...] = jnp.broadcast_to(jnp.concatenate(packed, axis=0)[None], out_ref.shape)


def mix(samples, noise, t):
    return ((1.0 - t) * samples + t * noise).astype(BF16)


def score_kernel(place_ref, time_ref, got_ref, own_ref, other_ref,
                 t_embed_ref, f_embed_ref, t_mods_ref, f_mods_ref, t_final_ref, f_final_ref, own_w_ref, other_w_ref,
                 part_ref, samples_ref, shaped_ref, pre_ref, res_ref,
                 t_w_ref, f_w_ref, t_gram_ref, f_gram_ref, t_mean_ref, f_mean_ref, t_shaped_ref, sum_ref):
    i = pl.program_id(0)
    v = place_ref[0]

    @pl.when(i == 0)
    def _():
        embed_moments(t_embed_ref, t_gram_ref, t_mean_ref)
        embed_moments(f_embed_ref, f_gram_ref, f_mean_ref)
        unpack_weights(place_ref, own_w_ref, other_w_ref, 1, t_w_ref)
        unpack_weights(place_ref, own_w_ref, other_w_ref, 2, f_w_ref)
        sum_ref[:, 48:, :] = jnp.zeros((OWNERS, 16, 128), F32)
    got = got_ref[:, pl.ds(pl.multiple_of(i * 8, 8), 8), :]
    samples = jnp.concatenate([got[:, :, :C], got[:, :, C:]], axis=1).reshape(TOKENS, C)
    turned = jnp.concatenate([samples[:HALF], samples[HALF:]], axis=1).T
    samples_ref[0] = jnp.where(v == 0, turned[:C], turned[C:])
    own, other = own_ref[:, C:].astype(F32), other_ref[:, C:].astype(F32)
    noise = jnp.concatenate(in_order(v, own, other), axis=0)
    noised = mix(samples, noise, time_ref[i])
    _, _, t_partial, t_total, t_square = forward(
        noised, t_embed_ref, t_mods_ref, t_final_ref, t_w_ref, t_gram_ref, t_mean_ref, t_shaped_ref, place_ref
    )
    pre, res, f_partial, f_total, f_square = forward(
        noised, f_embed_ref, f_mods_ref, f_final_ref, f_w_ref, f_gram_ref, f_mean_ref, shaped_ref.at[0], place_ref
    )
    pre_ref[0] = pre
    res_ref[0] = res
    rows = row_pieces([owned(v) for v in (t_total, t_square, f_total, f_square)], 64)
    sum_ref[:, pl.ds(pl.multiple_of(i * 16, 16), 16), :] = owned(jnp.concatenate([t_partial, f_partial], axis=1))
    for n in range(2):
        sum_ref[:, pl.ds(48 + 2 * i + n, 1), :] = rows[n]

    @pl.when(i == IMAGES - 1)
    def _():
        part_ref[...] = sum_ref[...].astype(BF16)


def cotangent_kernel(place_ref, gen_time_ref, time_ref, got_ref, noise_ref, keep_ref, sums_ref, out_ref):
    loss_scale = 1.0 / math.sqrt(IMAGES * S)
    t_runs, t_scales, t_shifts = read_sums(sums_ref, 1)
    f_runs, f_scales, f_shifts = read_sums(sums_ref, 2)
    got = got_ref[...].astype(F32)
    lane = lax.broadcasted_iota(jnp.int32, (1, 128), 1)
    cots, rows = [], []
    for i in range(IMAGES):
        block = got[:, 16 * i : 16 * i + 16]
        row = got[:, 48 + 2 * i : 50 + 2 * i]
        row = row[:, :1, :64] + row[:, :1, 64:] + row[:, 1:, :64]
        row = jnp.concatenate([row, jnp.zeros((OWNERS, 1, 64), F32)], axis=2)

        def inner(partials, k, runs, scale):
            partial, average, inverse = add_up(partials, from_row(row, k), from_row(row, k + 1), runs)
            return inverse * (partial - average * scale), average, inverse

        t_inner, _, _ = inner(block[:, :, :C], 0, t_runs[i], t_scales[i])
        f_inner, f_average, f_inverse = inner(block[:, :, C:], 2, f_runs[i], f_scales[i])
        teacher, fake = t_inner + t_shifts[i], f_inner + f_shifts[i]
        at = slice(i * OWNED, (i + 1) * OWNED)
        samples, g_inner = keep_ref[0, at, :], keep_ref[1, at, :]
        g_average, g_inverse = keep_ref[2, at, 0:1], keep_ref[3, at, 0:1]
        noise = noise_ref[pl.ds(pl.multiple_of(place_ref[3] + i * HALF, 16), OWNED), :][:, C:].astype(F32)
        t = time_ref[i]
        noised = mix(samples, noise, t).astype(F32)
        distance = jnp.sum(jnp.abs(samples - noised + t * teacher))
        gen_cot = (-(gen_time_ref[i] * t * loss_scale) * (teacher - fake)).astype(BF16).astype(F32)
        fake_cot = (loss_scale * (fake - noise + samples)).astype(BF16).astype(F32)
        numbers = []
        for cot, column, value, average, inverse in (
            (fake_cot, f_scales[i], f_inner, f_average, f_inverse),
            (gen_cot, sums_ref[0, 48 + i : 49 + i], g_inner, g_average, g_inverse),
        ):
            first = jnp.sum(cot * column, axis=1, keepdims=True) / D
            second = jnp.sum(cot * value, axis=1, keepdims=True) / D
            slope = inverse * inverse * second
            numbers += [inverse, slope, average * slope - inverse * first]
        cots.append(jnp.concatenate([fake_cot, gen_cot], axis=1))
        numbers_row = to_row([number[None] for number in numbers])[0]
        numbers_row = jnp.where(lane == 96, distance, numbers_row)
        for _ in range(3):
            rounded = numbers_row.astype(BF16).astype(F32)
            rows.append(rounded)
            numbers_row = numbers_row - rounded
    rows.append(jnp.zeros((7, 128), F32))
    packed = jnp.concatenate(cots + rows, axis=0).astype(BF16)
    out_ref[...] = jnp.broadcast_to(packed[None], out_ref.shape)


def gelu_slope(v):
    a, b = math.sqrt(2.0 / math.pi), 0.044715
    t = jnp.tanh(a * (v + b * (v * v * v)))
    return 0.5 * (1.0 + t) + 0.5 * v * (1.0 - t * t) * (a * (1.0 + 3.0 * b * (v * v)))


def gradient_kernel(net, place_ref, got_ref, *refs):
    gap_ref, refs = (refs[0], refs[1:]) if net == 1 else (None, refs)
    mods_ref, final_ref, pre_ref, res_ref, shaped_ref, keep_ref, send_ref, left_ref = refs

    @pl.when(pl.program_id(0) == 0)
    def _():
        final = local_lanes(lambda at: final_ref[:, at], place_ref)
        if net == 1:
            gaps = jnp.sum(gap_ref[...], axis=0)
        for i in range(IMAGES):
            row = got_ref[:, 48:64, :].astype(F32)
            row = row[:, 3 * i : 3 * i + 1] + row[:, 3 * i + 1 : 3 * i + 2] + row[:, 3 * i + 2 : 3 * i + 3]
            inverse, slope, offset = [from_row(row, 3 * net + k).reshape(TOKENS, 1) for k in range(3)]
            cot = got_ref[:, 16 * i : 16 * i + 16, :].reshape(TOKENS, 128)[:, net * C : (net + 1) * C]
            out_grad = dot(cot, final)
            scale = local_lanes(lambda at: mods_ref[i, 4:5, at], place_ref)
            gate = local_lanes(lambda at: mods_ref[i, 2:3, at], place_ref)
            res_grad = inverse * (out_grad * (1.0 + scale)) - slope * res_ref[i] + offset
            act_grad = res_grad * gate
            if net == 1:
                inverse_gap = 1.0 / (gaps[i : i + 1, :] / (S * C) + gap_epsilon)
                act_grad = act_grad * jnp.concatenate([inverse_gap, inverse_gap[:, :NARROW]], axis=1)
            grad = act_grad * gelu_slope(pre_ref[i])
            turned = jnp.concatenate([grad, jnp.zeros((TOKENS, NARROW), F32)], axis=1).T
            left_ref[:, i * TOKENS : (i + 1) * TOKENS] = turned[:COLS].astype(BF16)

    grad = dot(left_ref[...], shaped_ref[...].reshape(IMAGES * TOKENS, 768))
    tiles = grad[:WIDE].T.astype(BF16)
    parts = jnp.concatenate([grad[WIDE:, :384], grad[WIDE:, 384:]], axis=0).T.astype(BF16)
    first = place_ref[4] == 0
    for w in range(2):
        sides = []
        for h in range(2):
            at = [(w * 2 + v) * ROWS for v in range(2)]
            lanes = slice(h * NARROW, (h + 1) * NARROW)
            narrow = jnp.concatenate([parts[k : k + ROWS, lanes] for k in at], axis=1)
            sides.append([tiles[h * 384 + k : h * 384 + k + ROWS] for k in at] + [narrow])
        for n, (low, high) in enumerate(zip(*sides, strict=True)):
            keep_ref[w, n * ROWS : (n + 1) * ROWS, :] = jnp.where(first, low, high)
            send_ref[w, n * ROWS : (n + 1) * ROWS, :] = jnp.where(first, high, low)


def sum_kernel(place_ref, got_ref, keep_ref, send_ref):
    v = place_ref[0]
    for n in range(2):
        rows = slice(n * GEN_ROWS, (n + 1) * GEN_ROWS)
        total = got_ref[0, rows].astype(F32)
        for k in range(1, CHUNKS):
            total = total + got_ref[k, rows].astype(F32)
        def folded(rows, part):
            return jnp.concatenate([rows, jnp.concatenate([part[:48], part[48:]], axis=1)], axis=0)

        low = folded(total[:ROWS], total[2 * ROWS :, :NARROW])
        high = folded(total[ROWS : 2 * ROWS], total[2 * ROWS :, NARROW:])
        keep_ref[n] = jnp.where(v == 0, low, high).astype(BF16)
        send_ref[n] = jnp.where(v == 0, high, low).astype(BF16)


def place_kernel(place_ref, keep_ref, other_ref, fake_ref, gen_ref):
    for n, ref in enumerate((fake_ref, gen_ref)):
        low, high = in_order(place_ref[0], keep_ref[n].astype(F32), other_ref[n].astype(F32))
        ref[:, :128] = low[:ROWS]
        ref[:48, 128:256] = jnp.concatenate([low[ROWS:, :NARROW], high[ROWS:, :NARROW]], axis=1)
        ref[48:, 128:256] = jnp.concatenate([low[ROWS:, NARROW:], high[ROWS:, NARROW:]], axis=1)
        ref[:, 256:] = high[:ROWS]


def in_hbm(*arrays):
    return [pltpu.with_memory_space_constraint(a, pltpu.HBM) for a in arrays]


def exchange(value, axes):
    return lax.all_to_all(value, axes, 0, 0)


def shards(
    gen_noise,
    score_noise,
    gen_steps,
    score_steps,
    gen_embed,
    gen_modulation,
    gen_proj,
    gen_final,
    teacher_embed,
    teacher_modulation,
    teacher_proj,
    teacher_final,
    fake_embed,
    fake_modulation,
    fake_proj,
    fake_final,
):
    v, s = lax.axis_index("v"), lax.axis_index("s")
    start = (lax.rem(lax.axis_index("g") + 2, 4) * 2 + lax.axis_index("h")) * 384
    member = lax.axis_index(("h", "g"))
    place = jnp.stack([v, start + 256 * v, start + 128, member * OWNED, s]).astype(jnp.int32)
    gen_final, teacher_final, fake_final = gen_final.T, teacher_final.T, fake_final.T

    times, conds = time_features(jnp.concatenate([gen_steps, score_steps]), gen_modulation.shape[0])
    gen_time, score_time = times[:3], times[3:]
    halves = jax.ShapeDtypeStruct((SENT_ROWS, 128), BF16)
    mine, other, noise = pl.pallas_call(
        split_kernel,
        grid=(1,),
        in_specs=[smem(), whole((6, 256))] + [whole((IMAGES, C, HALF))] * 2 + [whole((ROWS, 384))] * 3
        + [whole((480, 256))] * 3,
        out_specs=[whole((SENT_ROWS, 128))] * 2 + [whole((NOISE_ROWS, 128))],
        out_shape=[halves, halves, jax.ShapeDtypeStruct((NOISE_ROWS, 128), BF16)],
        compiler_params=params(60),
        name="split",
    )(place, conds, gen_noise.transpose(0, 2, 1), score_noise.transpose(0, 2, 1), gen_proj, teacher_proj, fake_proj,
      gen_modulation.T, teacher_modulation.T, fake_modulation.T)
    mine = lax.ppermute(mine, PLACES, SWAP)
    other = lax.ppermute(other, PLACES, SWAP_TURNED)
    mine, other, noise = lax.optimization_barrier((mine, other, noise))
    own_noise = lax.ppermute(noise, PLACES, NEAR)
    other_noise = lax.ppermute(noise, PLACES, NEAR_TURNED)

    g_packed, packed = pl.pallas_call(
        pack_kernel,
        grid=(1,),
        in_specs=[smem()] + [whole((SENT_ROWS, 128))] * 2,
        out_specs=[whole((CHUNKS, GEN_CHUNK, 128)), whole((CHUNKS, SCORE_ROWS, 128))],
        out_shape=[
            jax.ShapeDtypeStruct((CHUNKS, GEN_CHUNK, 128), BF16),
            jax.ShapeDtypeStruct((CHUNKS, SCORE_ROWS, 128), BF16),
        ],
        compiler_params=params(6),
        name="pack",
    )(place, mine, other)
    g_packed = exchange(g_packed, GATHER)
    g_packed, own_noise, other_noise = lax.optimization_barrier((g_packed, own_noise, other_noise))
    g_other = lax.ppermute(g_packed, "s", SIBLING)
    packed, g_packed, g_other = lax.optimization_barrier((packed, g_packed, g_other))
    packed = exchange(packed, GATHER)
    low, high = (a[:, GEN_ROWS : GEN_ROWS + 2 * MODS_ROWS] for a in in_order(s, g_packed, g_other))
    mods = jnp.stack([low, high]).reshape(2, 4, 2, 2, 4, 9, 128).transpose(5, 1, 0, 2, 3, 4, 6)
    mods = mods.reshape(9, 32, 512)[:, :, :480].reshape(9, 5, D).astype(F32)
    mods = jnp.pad(mods, ((0, 0), (0, 3), (0, 0)))

    by_image = lambda *shape: pl.BlockSpec((1, *shape), lambda i: (i,) + (0,) * len(shape))
    noise_rows = pl.BlockSpec((HALF, 128), lambda i: (i, 0))
    mods_of = lambda net: pl.BlockSpec((1, 8, D), lambda i: (3 * net + i, 0, 0))
    local = pltpu.HBM((IMAGES, TOKENS, COLS), F32)
    wide = pltpu.HBM((IMAGES, TOKENS, D), BF16)
    gen_embed, teacher_embed, fake_embed = in_hbm(gen_embed, teacher_embed, fake_embed)
    gen_final, teacher_final, fake_final = in_hbm(gen_final, teacher_final, fake_final)

    sums = pl.pallas_call(
        sums_kernel,
        grid=(1,),
        in_specs=[whole((C, D))] * 3 + [whole((9, 8, D))],
        out_specs=whole((3, 56, C)),
        out_shape=jax.ShapeDtypeStruct((3, 56, C), F32),
        compiler_params=params(16),
        name="sums",
    )(gen_final, teacher_final, fake_final, mods)

    part, g_shaped, g_pre, g_res = pl.pallas_call(
        generator_kernel,
        grid=(IMAGES,),
        in_specs=[
            smem(), noise_rows, noise_rows, whole((C, D)), mods_of(0), whole((C, D)),
            *([whole((CHUNKS, GEN_CHUNK, 128))] * 2),
        ],
        out_specs=[whole((OWNERS, 32, 128)), by_image(TOKENS, D), by_image(TOKENS, COLS), by_image(TOKENS, COLS)],
        out_shape=[jax.ShapeDtypeStruct((OWNERS, 32, 128), BF16), wide, local, local],
        scratch_shapes=[pltpu.VMEM((D, COLS), BF16), pltpu.VMEM((C, 3 * C), BF16), pltpu.VMEM((C, 128), F32),
                        pltpu.VMEM((OWNERS, 32, 128), F32)],
        compiler_params=params(16),
        cost_estimate=pl.CostEstimate(flops=12 * 10**9, bytes_accessed=30 * 10**6, transcendentals=0),
        name="generator",
    )(place, own_noise, other_noise, gen_embed, mods, gen_final, g_packed, g_other)
    packed, part, sums = lax.optimization_barrier((packed, part, sums))
    part = exchange(part, COMBINE)

    net_mods = lambda net: pl.BlockSpec((IMAGES, 8, D), lambda *_: (net, 0, 0))
    pack1, keep = pl.pallas_call(
        samples_kernel,
        grid=(1,),
        in_specs=[
            smem(), smem(), whole((OWNERS, 32, 128)), whole((NOISE_ROWS, 128)), whole((3, 56, C)),
        ],
        out_specs=[whole((OWNERS, 24, 128)), whole((4, 48, C))],
        out_shape=[
            jax.ShapeDtypeStruct((OWNERS, 24, 128), F32),
            jax.ShapeDtypeStruct((4, 48, C), F32),
        ],
        compiler_params=params(5),
        name="samples",
    )(place, gen_time, part, own_noise, sums)
    packed, pack1 = lax.optimization_barrier((packed, pack1))
    pack1 = exchange(pack1, COMBINE)
    other_packed = lax.ppermute(packed, "s", SIBLING)

    part2, samples, f_shaped, f_pre, f_res = pl.pallas_call(
        score_kernel,
        grid=(IMAGES,),
        in_specs=[
            smem(), smem(), whole((OWNERS, 24, 128)), noise_rows, noise_rows,
            whole((C, D)), whole((C, D)), mods_of(1), mods_of(2), whole((C, D)), whole((C, D)),
            *([whole((CHUNKS, SCORE_ROWS, 128))] * 2),
        ],
        out_specs=[
            whole((OWNERS, 64, 128)), by_image(C, HALF), by_image(TOKENS, D), by_image(TOKENS, COLS),
            by_image(TOKENS, COLS),
        ],
        out_shape=[
            jax.ShapeDtypeStruct((OWNERS, 64, 128), BF16),
            jax.ShapeDtypeStruct((IMAGES, C, HALF), F32),
            wide, local, local,
        ],
        scratch_shapes=[
            *([pltpu.VMEM((D, COLS), BF16)] * 2), *([pltpu.VMEM((C, 3 * C), BF16)] * 2),
            *([pltpu.VMEM((C, 128), F32)] * 2), pltpu.VMEM((TOKENS, D), BF16),
            pltpu.VMEM((OWNERS, 64, 128), F32),
        ],
        compiler_params=params(22),
        cost_estimate=pl.CostEstimate(flops=24 * 10**9, bytes_accessed=50 * 10**6, transcendentals=0),
        name="score",
    )(place, score_time, pack1, own_noise, other_noise, teacher_embed, fake_embed, mods, mods,
      teacher_final, fake_final, packed, other_packed)
    part2 = exchange(part2, COMBINE)

    pack2 = pl.pallas_call(
        cotangent_kernel,
        grid=(1,),
        in_specs=[
            smem(), smem(), smem(), whole((OWNERS, 64, 128)), whole((NOISE_ROWS, 128)), whole((4, 48, C)),
            whole((3, 56, C)),
        ],
        out_specs=whole((OWNERS, 64, 128)),
        out_shape=jax.ShapeDtypeStruct((OWNERS, 64, 128), BF16),
        compiler_params=params(6),
        name="cotangents",
    )(place, gen_time, score_time, part2, own_noise, keep, sums)
    pack2 = exchange(pack2, COMBINE)
    samples, pack2 = lax.optimization_barrier((samples, pack2))
    own_samples = samples
    samples = lax.ppermute(samples, "s", SIBLING)

    gap = jnp.sum(pack2[:, 48:57, 96].astype(F32).reshape(OWNERS, 3, 3), axis=(0, 2))
    gap = jnp.broadcast_to(jnp.pad(gap, (0, 5))[None, :, None], (16, 8, 128))
    gap = exchange(gap, TOKEN_AXES)
    samples, gap = lax.optimization_barrier((samples, gap))
    samples = jnp.where(lax.axis_index("h") == s, own_samples, samples).transpose(0, 2, 1)

    by_columns = pl.BlockSpec((IMAGES, TOKENS, 768), lambda x: (0, 0, x))
    partial = jax.ShapeDtypeStruct((CHUNKS, GEN_ROWS, 128), BF16)
    partial_spec = pl.BlockSpec((2, GEN_ROWS, 128), lambda x: (x, 0, 0))

    def gradient(net, gaps, mods_net, final, pre, res, shaped):
        kept, sent = pl.pallas_call(
            functools.partial(gradient_kernel, net),
            grid=(4,),
            in_specs=[
                smem(), whole((OWNERS, 64, 128)), *([whole((16, 8, 128))] * len(gaps)), net_mods(mods_net),
                whole((C, D)), *([whole((IMAGES, TOKENS, COLS))] * 2), by_columns,
            ],
            out_specs=[partial_spec, partial_spec],
            out_shape=[partial, partial],
            scratch_shapes=[pltpu.VMEM((COLS, IMAGES * TOKENS), BF16)],
            compiler_params=params(13),
            cost_estimate=pl.CostEstimate(flops=7 * 10**9, bytes_accessed=20 * 10**6, transcendentals=0),
        name="gradient",
        )(place, pack2, *gaps, mods, final, *in_hbm(pre, res, shaped))
        return kept, lax.ppermute(sent, "s", SIBLING)

    pieces = gradient(0, (), 2, fake_final, f_pre, f_res, f_shaped)
    pieces += gradient(1, (gap,), 0, gen_final, g_pre, g_res, g_shaped)
    both = jnp.concatenate(
        [(pieces[n].astype(F32) + pieces[n + 1].astype(F32)).astype(BF16) for n in (0, 2)], axis=1
    )
    tiles = jax.ShapeDtypeStruct((2, 144, 128), BF16)
    kept, sent = pl.pallas_call(
        sum_kernel,
        grid=(1,),
        in_specs=[smem(), whole((CHUNKS, 2 * GEN_ROWS, 128))],
        out_specs=[whole((2, 144, 128))] * 2,
        out_shape=[tiles, tiles],
        compiler_params=params(8),
        name="sum",
    )(place, exchange(both, GATHER))
    kept = lax.ppermute(kept, PLACES, SWAP)
    sent = lax.ppermute(sent, PLACES, SWAP_TURNED)
    fake_grad, gen_grad = pl.pallas_call(
        place_kernel,
        grid=(1,),
        in_specs=[smem(), whole((2, 144, 128)), whole((2, 144, 128))],
        out_specs=[whole((ROWS, 384))] * 2,
        out_shape=[jax.ShapeDtypeStruct((ROWS, 384), F32)] * 2,
        compiler_params=params(4),
        name="place",
    )(place, kept, sent)
    return (samples, gen_grad, fake_grad)


def solution(mesh):
    split = Mesh(mesh.devices.reshape(4, 4, 2, 2, 2, 2), ("g", "x", "h", "w", "v", "s"))
    tokens = P(None, ROW_AXES, None)
    columns = P(None, ROW_AXES)
    block = P(ROW_AXES, ("g", "s"))
    net = (P(), columns, block, P())
    return jax.shard_map(
        shards,
        mesh=split,
        in_specs=(tokens, tokens, P(), P(), *net, *net, *net),
        out_specs=(tokens, block, block),
        check_vma=False,
    )
```

```python
import functools
import math

import jax
import jax.numpy as jnp
from jax import lax
from jax.experimental import pallas as pl
from jax.experimental.pallas import tpu as pltpu
from jax.sharding import Mesh
from jax.sharding import PartitionSpec as P

S = 4096
STEPS = 1000
D = 3072
C = 64
IMAGES = 3

norm_epsilon = 1e-06
gap_epsilon = 1e-05

F32 = jnp.float32
BF16 = jnp.bfloat16

GATHER = ("x", "w")
ROW_AXES = ("x", "h", "w", "v")
COMBINE = ("v", "h", "g")
TOKEN_AXES = ("x", "w", "s")
OWNERS = 16
TOKENS = 256
HALF = 128
OWNED = 16
ROWS = 96
WIDE = 128
NARROW = 64
COLS = WIDE + NARROW
GEN_ROWS = 288
NOISE_ROWS = 384
MODS_AT = 480
MODS_ROWS = 36
SENT_ROWS = 528
GEN_CHUNK = 368
SCORE_ROWS = 576
CHUNKS = 8
BLOCK = 512

PLACES = ("g", "h", "v", "s")


def number(g, h, v, s):
    return g * 8 + h * 4 + v * 2 + s


EVERY = [(g, h, v, s) for g in range(4) for h in range(2) for v in range(2) for s in range(2)]
SWAP, SWAP_TURNED = [
    [(number(g, h, v, s), number((g + 2) % 4, s, v ^ turn, h)) for g, h, v, s in EVERY] for turn in range(2)
]
NEAR, NEAR_TURNED = [
    [(number(g, h, v, s), number(g if h == s else 3 - g, s, v ^ turn, h)) for g, h, v, s in EVERY] for turn in range(2)
]
SIBLING = [(0, 1), (1, 0)]


def params(mib):
    return pltpu.CompilerParams(vmem_limit_bytes=mib * 1024 * 1024)


def smem():
    return pl.BlockSpec(memory_space=pltpu.SMEM)


def whole(shape):
    zeros = (0,) * len(shape)
    return pl.BlockSpec(shape, lambda *_: zeros)


def dot(a, b):
    return jnp.dot(a, b, preferred_element_type=F32)


def dot_turned(a, b):
    return lax.dot_general(a, b, (((1,), (1,)), ((), ())), preferred_element_type=F32)


def time_features(steps, embed_width):
    times = (steps.astype(F32) + 1.0) / (STEPS + 1.0)
    half = embed_width // 2
    frequency = jnp.exp(-jnp.log(10000.0) * jnp.arange(half, dtype=F32) / half)
    angles = 1000.0 * times[:, None] * frequency[None, :]
    embedding = jnp.concatenate([jnp.cos(angles), jnp.sin(angles)], axis=1)
    return (times, jax.nn.silu(embedding).astype(BF16))


def to_row(numbers):
    shape = (numbers[0].shape[0], OWNED, 128)
    lane = lax.broadcasted_iota(jnp.int32, shape, 2)
    token = lax.broadcasted_iota(jnp.int32, shape, 1)
    total = jnp.zeros(shape, F32)
    for k, number in enumerate(numbers):
        total = jnp.where(lane == token + OWNED * k, number, total)
    return jnp.sum(total, axis=1, keepdims=True)


def row_pieces(numbers, stride):
    row = to_row(numbers)
    per_row = 128 // stride
    rows = [row.astype(BF16).astype(F32)]
    row = row - rows[0]
    rows.append(row.astype(BF16).astype(F32))
    rows.append((row - rows[1]).astype(BF16).astype(F32))
    packed = [jnp.concatenate([r[:, :, :stride] for r in rows[:per_row]], axis=2)]
    if len(rows) > per_row:
        packed.append(jnp.concatenate([rows[per_row][:, :, :stride], jnp.zeros_like(row)[:, :, : 128 - stride]], axis=2))
    else:
        packed[0] = jnp.concatenate([packed[0], jnp.zeros_like(row)[:, :, : 128 - 3 * stride]], axis=2)
    return packed


def from_row(row, k):
    shape = (row.shape[0], OWNED, 128)
    lane = lax.broadcasted_iota(jnp.int32, shape, 2)
    token = lax.broadcasted_iota(jnp.int32, shape, 1)
    return jnp.sum(jnp.where(lane == token + OWNED * k, row, 0.0), axis=2, keepdims=True)


def local_lanes(load, place_ref):
    tile = load(pl.ds(pl.multiple_of(place_ref[1], 128), 128))
    middle = load(pl.ds(pl.multiple_of(place_ref[2], 128), 128))
    part = jnp.where(place_ref[0] == 0, middle[:, :NARROW], middle[:, NARROW:])
    return jnp.concatenate([tile, part], axis=1)


def unpack_weights(place_ref, own_ref, other_ref, net, w_ref):
    s = place_ref[4]
    for packed_ref, side in ((own_ref, s), (other_ref, 1 - s)):
        for chunk in range(CHUNKS):
            x, w = chunk // 2, chunk % 2
            for v in range(2):
                k = pl.multiple_of((x * 8 + w * 2 + v) * ROWS + side * (4 * ROWS), 32)
                first = max(net - 1, 0) * 192 + v * ROWS
                w_ref[pl.ds(k, ROWS), :WIDE] = packed_ref[chunk, first : first + ROWS, :]
                if net == 0:
                    part = packed_ref[chunk, 192:288, v * NARROW : (v + 1) * NARROW]
                else:
                    part = packed_ref[chunk, 384 + v * ROWS : 384 + (v + 1) * ROWS, (net - 1) * NARROW : net * NARROW]
                w_ref[pl.ds(k, ROWS), WIDE:] = part


def split_bits(value, count):
    pieces = []
    for _ in range(count):
        piece = value.astype(BF16)
        pieces.append(piece)
        value = value - piece.astype(F32)
    return pieces


def embed_moments(embed_ref, gram_ref, mean_ref):
    embed = embed_ref[...]
    ones = jnp.ones((8, D), BF16)
    column = dot_turned(embed, ones)[:, 0:1] / D
    row = dot_turned(ones, embed)[0:1] / D
    gram = dot_turned(embed, embed) / D - column * row
    gram_ref[...] = jnp.concatenate(split_bits(gram, 3), axis=1)
    mean_ref[...] = jnp.broadcast_to(column, mean_ref.shape)


def shape_tokens(x, embed_ref, mods_ref, image, gram_ref, mean_ref, store):
    turned = dot(x, gram_ref[...])
    turned = turned[:, :C] + turned[:, C : 2 * C] + turned[:, 2 * C :]
    inverse = lax.rsqrt(jnp.sum(turned * x.astype(F32), axis=1, keepdims=True) + norm_epsilon)
    inverse = jnp.broadcast_to(inverse, (TOKENS, BLOCK))
    twice = jnp.concatenate([x, x], axis=1)
    mean = mean_ref[:, 0:1]
    for b in range(D // BLOCK):
        cut = slice(b * BLOCK, (b + 1) * BLOCK)
        scaled = (embed_ref[:, cut].astype(F32) - mean) * (1.0 + mods_ref[image, 1:2, cut])
        scaled = jnp.concatenate(split_bits(scaled, 2), axis=0)
        store(cut, (dot(twice, scaled) * inverse + mods_ref[image, 0:1, cut]).astype(BF16))


def finish(preactivation, x, embed_ref, mods_ref, image, final_ref, place_ref):
    activated = jax.nn.gelu(preactivation, approximate=True).astype(BF16).astype(F32)
    own_hidden = dot(x, local_lanes(lambda at: embed_ref[:, at], place_ref))
    gate = local_lanes(lambda at: mods_ref[image, 2:3, at], place_ref)
    scale = local_lanes(lambda at: mods_ref[image, 4:5, at], place_ref)
    residual = own_hidden + gate * activated
    total = jnp.sum(residual, axis=1, keepdims=True)
    total_square = jnp.sum(residual * residual, axis=1, keepdims=True)
    own_mean = total / COLS
    final = local_lanes(lambda at: final_ref[:, at], place_ref)
    centred = ((residual - own_mean) * (1.0 + scale)).astype(BF16)
    partial = dot_turned(centred, final)
    return residual, partial, total, total_square


def owned(value):
    return value.reshape(OWNERS, OWNED, value.shape[-1])


def sums_kernel(g_final_ref, t_final_ref, f_final_ref, mods_ref, out_ref):
    run = lax.broadcasted_iota(jnp.int32, (OWNERS, D), 1) // COLS
    own = run == lax.broadcasted_iota(jnp.int32, (OWNERS, D), 0)
    for net, final_ref in enumerate((g_final_ref, t_final_ref, f_final_ref)):
        scales = [mods_ref[3 * net + i, 4:5, :] for i in range(IMAGES)]
        shifts = [mods_ref[3 * net + i, 3:4, :] for i in range(IMAGES)]
        left = [jnp.where(own, row, 0.0) for row in scales + [jnp.ones((1, D), F32)]]
        left = jnp.concatenate(left + shifts + [jnp.zeros((5, D), F32)], axis=0).astype(BF16)
        sums = dot_turned(left, final_ref[...])
        ones = sums[3 * OWNERS : 4 * OWNERS]
        runs = [sums[i * OWNERS : (i + 1) * OWNERS] + ones for i in range(IMAGES)]
        totals = [jnp.sum(r, axis=0, keepdims=True) for r in runs]
        out_ref[net] = jnp.concatenate(runs + totals + [sums[64:67], jnp.zeros((2, C), F32)], axis=0)


def read_sums(sums_ref, net):
    runs = [sums_ref[net, i * OWNERS : (i + 1) * OWNERS] for i in range(IMAGES)]
    return runs, [sums_ref[net, 48 + i : 49 + i] for i in range(IMAGES)], [sums_ref[net, 51 + i : 52 + i] for i in range(IMAGES)]


def add_up(partials, totals, squares, runs):
    means = totals * (1.0 / COLS)
    ordered = [((g + 2) % 4 * 2 + h) * 2 + v for v in range(2) for h in range(2) for g in range(4)]
    ordered = jnp.concatenate([runs[run : run + 1][None] for run in ordered], axis=0)
    partial = jnp.sum(partials + means * ordered, axis=0)
    average = jnp.sum(totals, axis=0) / D
    inverse = lax.rsqrt(jnp.sum(squares, axis=0) / D - average * average + norm_epsilon)
    return partial, average, inverse


def split_kernel(place_ref, cond_ref, gen_noise_ref, score_noise_ref, gen_ref, teacher_ref, fake_ref,
                 gen_mod_ref, teacher_mod_ref, fake_mod_ref, mine_ref, other_ref, noise_ref):
    for i in range(IMAGES):
        noise = jnp.concatenate([gen_noise_ref[i], score_noise_ref[i]], axis=0).astype(F32).T.astype(BF16)
        noise_ref[i * HALF : (i + 1) * HALF] = noise
    cond = cond_ref[...]
    mods = [dot_turned(cond, ref[...]) for ref in (gen_mod_ref, teacher_mod_ref, fake_mod_ref)]
    mods = jnp.concatenate([mods[0][0:3], mods[1][3:6], mods[2][3:6]], axis=0)
    mods = jnp.concatenate([mods, jnp.zeros((9, 32), F32)], axis=1)
    mods = jnp.concatenate([mods[:, 128 * p : 128 * (p + 1)] for p in range(4)] + [jnp.zeros((12, 128), F32)], axis=0)
    mine_ref[MODS_AT:] = mods.astype(BF16)
    other_ref[MODS_AT:] = mods.astype(BF16)
    first = place_ref[0] == 0
    mine, other = [], []
    for n, ref in enumerate((gen_ref, teacher_ref, fake_ref)):
        rows = slice(n * ROWS, (n + 1) * ROWS)
        low, high = ref[:, :128], ref[:, 256:]
        mine_ref[rows] = jnp.where(first, low, high)
        other_ref[rows] = jnp.where(first, high, low)
        low, high = ref[:, 128:192], ref[:, 192:256]
        mine.append(jnp.where(first, low, high))
        other.append(jnp.where(first, high, low))
    for ref, parts in ((mine_ref, mine), (other_ref, other)):
        ref[3 * ROWS : 4 * ROWS] = jnp.concatenate(parts[1:], axis=1)
        ref[4 * ROWS : MODS_AT] = jnp.concatenate([parts[0], parts[0]], axis=1)


def in_order(v, mine, other):
    return jnp.where(v == 0, mine, other), jnp.where(v == 0, other, mine)


def pack_kernel(place_ref, mine_ref, other_ref, out_ref):
    v = place_ref[0]
    tiles = in_order(v, mine_ref[:ROWS], other_ref[:ROWS])
    parts = in_order(v, mine_ref[4 * ROWS : MODS_AT], other_ref[4 * ROWS : MODS_AT])
    parts = jnp.concatenate([part[:, :NARROW] for part in parts], axis=1)
    mods = in_order(v, mine_ref[MODS_AT:].astype(F32), other_ref[MODS_AT:].astype(F32))
    mods = jnp.concatenate([mods[0][:MODS_ROWS], mods[1][:MODS_ROWS], jnp.zeros((8, 128), F32)], axis=0)
    gen = jnp.concatenate([*tiles, parts, mods.astype(BF16)], axis=0)
    for k in range(CHUNKS):
        out_ref[k] = gen


def pack_score_kernel(place_ref, mine_ref, other_ref, out_ref):
    cuts = [slice(n * ROWS, (n + 1) * ROWS) for n in (1, 2, 3)]
    ordered = [in_order(place_ref[0], mine_ref[rows], other_ref[rows]) for rows in cuts]
    score = jnp.concatenate([block for pair in ordered for block in pair], axis=0)
    for k in range(CHUNKS):
        out_ref[k] = score


def generator_kernel(place_ref, own_ref, other_ref, embed_ref, mods_ref, final_ref, own_w_ref, other_w_ref,
                     part_ref, shaped_ref, pre_ref, res_ref, w_ref, gram_ref, mean_ref, sum_ref):
    i = pl.program_id(0)
    v = place_ref[0]

    @pl.when(i == 0)
    def _():
        embed_moments(embed_ref, gram_ref, mean_ref)
        unpack_weights(place_ref, own_w_ref, other_w_ref, 0, w_ref)
        sum_ref[:, 24:, :] = jnp.zeros((OWNERS, 8, 128), F32)

    x = jnp.concatenate(in_order(v, own_ref[:, :C], other_ref[:, :C]), axis=0)

    def store(cut, shaped):
        shaped_ref[0, :, cut] = shaped

    shape_tokens(x, embed_ref, mods_ref, 0, gram_ref, mean_ref, store)
    pre = dot(shaped_ref[0], w_ref[...])
    res, partial, total, square = finish(pre, x, embed_ref, mods_ref, 0, final_ref, place_ref)
    pre_ref[0] = pre
    res_ref[0] = res
    pieces = owned(partial)
    pieces = jnp.concatenate([pieces[:, :8], pieces[:, 8:]], axis=2)
    rows = row_pieces([owned(total), owned(square)], 32)
    sum_ref[:, pl.ds(pl.multiple_of(i * 8, 8), 8), :] = pieces
    sum_ref[:, pl.ds(24 + i, 1), :] = rows[0]

    @pl.when(i == IMAGES - 1)
    def _():
        part_ref[...] = sum_ref[...].astype(BF16)


def samples_kernel(place_ref, time_ref, got_ref, noise_ref, sums_ref, out_ref, keep_ref):
    runs, scales, shifts = read_sums(sums_ref, 0)
    got = got_ref[...].astype(F32)
    packed = []
    for i in range(IMAGES):
        block = got[:, 8 * i : 8 * i + 8]
        partials = jnp.concatenate([block[:, :, :C], block[:, :, C:]], axis=1)
        row = got[:, 24 + i : 25 + i]
        row = row[:, :, :32] + row[:, :, 32:64] + row[:, :, 64:96]
        row = jnp.concatenate([row, jnp.zeros((OWNERS, 1, 96), F32)], axis=2)
        partial, average, inverse = add_up(partials, from_row(row, 0), from_row(row, 1), runs[i])
        inner = inverse * (partial - average * scales[i])
        velocity = inner + shifts[i]
        noise = noise_ref[pl.ds(pl.multiple_of(place_ref[3] + i * HALF, 16), OWNED), :][:, :C].astype(F32)
        samples = noise - time_ref[i] * velocity
        packed.append(jnp.concatenate([samples[:8], samples[8:]], axis=1))
        at = slice(i * OWNED, (i + 1) * OWNED)
        keep_ref[0, at, :] = samples
        keep_ref[1, at, :] = inner
        keep_ref[2, at, :] = jnp.broadcast_to(average, (OWNED, C))
        keep_ref[3, at, :] = jnp.broadcast_to(inverse, (OWNED, C))
    out_ref[...] = jnp.broadcast_to(jnp.concatenate(packed, axis=0)[None], out_ref.shape)


def mix(samples, noise, t):
    return ((1.0 - t) * samples + t * noise).astype(BF16)


def score_kernel(place_ref, time_ref, got_ref, own_ref, other_ref,
                 t_embed_ref, f_embed_ref, t_mods_ref, f_mods_ref, t_final_ref, f_final_ref, own_w_ref, other_w_ref,
                 part_ref, samples_ref, shaped_ref, pre_ref, res_ref,
                 t_w_ref, f_w_ref, t_gram_ref, f_gram_ref, t_mean_ref, f_mean_ref, t_shaped_ref, f_shaped_ref, x_ref, sum_ref):
    i = pl.program_id(0)
    v = place_ref[0]

    @pl.when(i == 0)
    def _():
        embed_moments(t_embed_ref, t_gram_ref, t_mean_ref)
        embed_moments(f_embed_ref, f_gram_ref, f_mean_ref)
        unpack_weights(place_ref, own_w_ref, other_w_ref, 1, t_w_ref)
        unpack_weights(place_ref, own_w_ref, other_w_ref, 2, f_w_ref)
        sum_ref[:, 48:, :] = jnp.zeros((OWNERS, 16, 128), F32)
    got = got_ref[:, pl.ds(pl.multiple_of(i * 8, 8), 8), :]
    samples = jnp.concatenate([got[:, :, :C], got[:, :, C:]], axis=1).reshape(TOKENS, C)
    turned = jnp.concatenate([samples[:HALF], samples[HALF:]], axis=1).T
    samples_ref[0] = jnp.where(v == 0, turned[:C], turned[C:])
    own, other = own_ref[:, C:].astype(F32), other_ref[:, C:].astype(F32)
    noise = jnp.concatenate(in_order(v, own, other), axis=0)
    noised = mix(samples, noise, time_ref[i])
    x_ref[i] = noised
    tokens = pl.ds(pl.multiple_of(i * TOKENS, TOKENS), TOKENS)

    def t_store(cut, shaped):
        t_shaped_ref[tokens, cut] = shaped

    def f_store(cut, shaped):
        f_shaped_ref[tokens, cut] = shaped
        shaped_ref[0, :, cut] = shaped

    shape_tokens(noised, t_embed_ref, t_mods_ref, i, t_gram_ref, t_mean_ref, t_store)
    shape_tokens(noised, f_embed_ref, f_mods_ref, i, f_gram_ref, f_mean_ref, f_store)

    @pl.when(i == IMAGES - 1)
    def _():
        t_pre = dot(t_shaped_ref[...], t_w_ref[...])
        f_pre = dot(f_shaped_ref[...], f_w_ref[...])
        for n in range(IMAGES):
            x = x_ref[n]
            rows = slice(n * TOKENS, (n + 1) * TOKENS)
            _, t_partial, t_total, t_square = finish(t_pre[rows], x, t_embed_ref, t_mods_ref, n, t_final_ref, place_ref)
            res, f_partial, f_total, f_square = finish(f_pre[rows], x, f_embed_ref, f_mods_ref, n, f_final_ref, place_ref)
            pre_ref[n] = f_pre[rows]
            res_ref[n] = res
            sum_ref[:, 16 * n : 16 * n + 16, :] = owned(jnp.concatenate([t_partial, f_partial], axis=1))
            pieces = row_pieces([owned(v) for v in (t_total, t_square, f_total, f_square)], 64)
            for k in range(2):
                sum_ref[:, 48 + 2 * n + k : 49 + 2 * n + k, :] = pieces[k]
        part_ref[...] = sum_ref[...].astype(BF16)


def cotangent_kernel(place_ref, gen_time_ref, time_ref, got_ref, noise_ref, keep_ref, sums_ref, out_ref):
    loss_scale = 1.0 / math.sqrt(IMAGES * S)
    t_runs, t_scales, t_shifts = read_sums(sums_ref, 1)
    f_runs, f_scales, f_shifts = read_sums(sums_ref, 2)
    got = got_ref[...].astype(F32)
    lane = lax.broadcasted_iota(jnp.int32, (1, 128), 1)
    cots, rows = [], []
    for i in range(IMAGES):
        block = got[:, 16 * i : 16 * i + 16]
        row = got[:, 48 + 2 * i : 50 + 2 * i]
        row = row[:, :1, :64] + row[:, :1, 64:] + row[:, 1:, :64]
        row = jnp.concatenate([row, jnp.zeros((OWNERS, 1, 64), F32)], axis=2)

        def inner(partials, k, runs, scale):
            partial, average, inverse = add_up(partials, from_row(row, k), from_row(row, k + 1), runs)
            return inverse * (partial - average * scale), average, inverse

        t_inner, _, _ = inner(block[:, :, :C], 0, t_runs[i], t_scales[i])
        f_inner, f_average, f_inverse = inner(block[:, :, C:], 2, f_runs[i], f_scales[i])
        teacher, fake = t_inner + t_shifts[i], f_inner + f_shifts[i]
        at = slice(i * OWNED, (i + 1) * OWNED)
        samples, g_inner = keep_ref[0, at, :], keep_ref[1, at, :]
        g_average, g_inverse = keep_ref[2, at, 0:1], keep_ref[3, at, 0:1]
        noise = noise_ref[pl.ds(pl.multiple_of(place_ref[3] + i * HALF, 16), OWNED), :][:, C:].astype(F32)
        t = time_ref[i]
        noised = mix(samples, noise, t).astype(F32)
        distance = jnp.sum(jnp.abs(samples - noised + t * teacher))
        gen_cot = (-(gen_time_ref[i] * t * loss_scale) * (teacher - fake)).astype(BF16).astype(F32)
        fake_cot = (loss_scale * (fake - noise + samples)).astype(BF16).astype(F32)
        numbers = []
        for cot, column, value, average, inverse in (
            (fake_cot, f_scales[i], f_inner, f_average, f_inverse),
            (gen_cot, sums_ref[0, 48 + i : 49 + i], g_inner, g_average, g_inverse),
        ):
            first = jnp.sum(cot * column, axis=1, keepdims=True) / D
            second = jnp.sum(cot * value, axis=1, keepdims=True) / D
            slope = inverse * inverse * second
            numbers += [inverse, slope, average * slope - inverse * first]
        cots.append(jnp.concatenate([fake_cot, gen_cot], axis=1))
        numbers_row = to_row([number[None] for number in numbers])[0]
        numbers_row = jnp.where(lane == 96, distance, numbers_row)
        for _ in range(3):
            rounded = numbers_row.astype(BF16).astype(F32)
            rows.append(rounded)
            numbers_row = numbers_row - rounded
    rows.append(jnp.zeros((7, 128), F32))
    packed = jnp.concatenate(cots + rows, axis=0).astype(BF16)
    out_ref[...] = jnp.broadcast_to(packed[None], out_ref.shape)


def gelu_slope(v):
    a, b = math.sqrt(2.0 / math.pi), 0.044715
    t = jnp.tanh(a * (v + b * (v * v * v)))
    return 0.5 * (1.0 + t) + 0.5 * v * (1.0 - t * t) * (a * (1.0 + 3.0 * b * (v * v)))


def gradient_kernel(net, place_ref, got_ref, *refs):
    gap_ref, refs = (refs[0], refs[1:]) if net == 1 else (None, refs)
    mods_ref, final_ref, pre_ref, res_ref, shaped_ref, keep_ref, send_ref, left_ref = refs

    @pl.when(pl.program_id(0) == 0)
    def _():
        final = local_lanes(lambda at: final_ref[:, at], place_ref)
        if net == 1:
            gaps = jnp.sum(gap_ref[...], axis=0)
        for i in range(IMAGES):
            row = got_ref[:, 48:64, :].astype(F32)
            row = row[:, 3 * i : 3 * i + 1] + row[:, 3 * i + 1 : 3 * i + 2] + row[:, 3 * i + 2 : 3 * i + 3]
            inverse, slope, offset = [from_row(row, 3 * net + k).reshape(TOKENS, 1) for k in range(3)]
            cot = got_ref[:, 16 * i : 16 * i + 16, :].reshape(TOKENS, 128)[:, net * C : (net + 1) * C]
            out_grad = dot(cot, final)
            scale = local_lanes(lambda at: mods_ref[i, 4:5, at], place_ref)
            gate = local_lanes(lambda at: mods_ref[i, 2:3, at], place_ref)
            res_grad = inverse * (out_grad * (1.0 + scale)) - slope * res_ref[i] + offset
            act_grad = res_grad * gate
            if net == 1:
                lane = lax.broadcasted_iota(jnp.int32, gaps.shape, 1)
                total = jnp.sum(jnp.where(lane == i, gaps, 0.0), axis=1, keepdims=True)
                act_grad = act_grad * (1.0 / (total / (S * C) + gap_epsilon))
            grad = act_grad * gelu_slope(pre_ref[i])
            turned = jnp.concatenate([grad, jnp.zeros((TOKENS, NARROW), F32)], axis=1).T
            left_ref[:, i * TOKENS : (i + 1) * TOKENS] = turned[:COLS].astype(BF16)

    grad = dot(left_ref[...], shaped_ref[...].reshape(IMAGES * TOKENS, 768))
    tiles = grad[:WIDE].T.astype(BF16)
    parts = jnp.concatenate([grad[WIDE:, :384], grad[WIDE:, 384:]], axis=0).T.astype(BF16)
    first = place_ref[4] == 0
    for w in range(2):
        sides = []
        for h in range(2):
            at = [(w * 2 + v) * ROWS for v in range(2)]
            lanes = slice(h * NARROW, (h + 1) * NARROW)
            narrow = jnp.concatenate([parts[k : k + ROWS, lanes] for k in at], axis=1)
            sides.append([tiles[h * 384 + k : h * 384 + k + ROWS] for k in at] + [narrow])
        for n, (low, high) in enumerate(zip(*sides, strict=True)):
            keep_ref[w, n * ROWS : (n + 1) * ROWS, :] = jnp.where(first, low, high)
            send_ref[w, n * ROWS : (n + 1) * ROWS, :] = jnp.where(first, high, low)


def add_kernel(f_keep_ref, f_got_ref, g_keep_ref, g_got_ref, out_ref):
    for n, (keep_ref, got_ref) in enumerate(((f_keep_ref, f_got_ref), (g_keep_ref, g_got_ref))):
        for k in range(CHUNKS):
            total = keep_ref[k].astype(F32) + got_ref[k].astype(F32)
            out_ref[k, n * GEN_ROWS : (n + 1) * GEN_ROWS] = total.astype(BF16)


def sum_kernel(place_ref, got_ref, keep_ref, send_ref):
    v = place_ref[0]
    for n in range(2):
        rows = slice(n * GEN_ROWS, (n + 1) * GEN_ROWS)
        total = got_ref[0, rows].astype(F32)
        for k in range(1, CHUNKS):
            total = total + got_ref[k, rows].astype(F32)
        def folded(rows, part):
            return jnp.concatenate([rows, jnp.concatenate([part[:48], part[48:]], axis=1)], axis=0)

        low = folded(total[:ROWS], total[2 * ROWS :, :NARROW])
        high = folded(total[ROWS : 2 * ROWS], total[2 * ROWS :, NARROW:])
        keep_ref[n] = jnp.where(v == 0, low, high).astype(BF16)
        send_ref[n] = jnp.where(v == 0, high, low).astype(BF16)


def place_kernel(place_ref, keep_ref, other_ref, fake_ref, gen_ref):
    for n, ref in enumerate((fake_ref, gen_ref)):
        low, high = in_order(place_ref[0], keep_ref[n].astype(F32), other_ref[n].astype(F32))
        ref[:, :128] = low[:ROWS]
        ref[:48, 128:256] = jnp.concatenate([low[ROWS:, :NARROW], high[ROWS:, :NARROW]], axis=1)
        ref[48:, 128:256] = jnp.concatenate([low[ROWS:, NARROW:], high[ROWS:, NARROW:]], axis=1)
        ref[:, 256:] = high[:ROWS]


def in_hbm(*arrays):
    return [pltpu.with_memory_space_constraint(a, pltpu.HBM) for a in arrays]


def exchange(value, axes):
    return lax.all_to_all(value, axes, 0, 0)


def shards(
    gen_noise,
    score_noise,
    gen_steps,
    score_steps,
    gen_embed,
    gen_modulation,
    gen_proj,
    gen_final,
    teacher_embed,
    teacher_modulation,
    teacher_proj,
    teacher_final,
    fake_embed,
    fake_modulation,
    fake_proj,
    fake_final,
):
    v, s = lax.axis_index("v"), lax.axis_index("s")
    start = (lax.rem(lax.axis_index("g") + 2, 4) * 2 + lax.axis_index("h")) * 384
    member = lax.axis_index(("h", "g"))
    place = jnp.stack([v, start + 256 * v, start + 128, member * OWNED, s]).astype(jnp.int32)
    gen_final, teacher_final, fake_final = gen_final.T, teacher_final.T, fake_final.T

    times, conds = time_features(jnp.concatenate([gen_steps, score_steps]), gen_modulation.shape[0])
    gen_time, score_time = times[:3], times[3:]
    halves = jax.ShapeDtypeStruct((SENT_ROWS, 128), BF16)
    mine, other, noise = pl.pallas_call(
        split_kernel,
        grid=(1,),
        in_specs=[smem(), whole((6, 256))] + [whole((IMAGES, C, HALF))] * 2 + [whole((ROWS, 384))] * 3
        + [whole((480, 256))] * 3,
        out_specs=[whole((SENT_ROWS, 128))] * 2 + [whole((NOISE_ROWS, 128))],
        out_shape=[halves, halves, jax.ShapeDtypeStruct((NOISE_ROWS, 128), BF16)],
        compiler_params=params(60),
        name="split",
    )(place, conds, gen_noise.transpose(0, 2, 1), score_noise.transpose(0, 2, 1), gen_proj, teacher_proj, fake_proj,
      gen_modulation.T, teacher_modulation.T, fake_modulation.T)
    mine = lax.ppermute(mine, PLACES, SWAP)
    other = lax.ppermute(other, PLACES, SWAP_TURNED)
    mine, other, noise = lax.optimization_barrier((mine, other, noise))
    own_noise = lax.ppermute(noise, PLACES, NEAR)
    other_noise = lax.ppermute(noise, PLACES, NEAR_TURNED)

    def pack(kernel, rows):
        return pl.pallas_call(
            kernel,
            grid=(1,),
            in_specs=[smem()] + [whole((SENT_ROWS, 128))] * 2,
            out_specs=whole((CHUNKS, rows, 128)),
            out_shape=jax.ShapeDtypeStruct((CHUNKS, rows, 128), BF16),
            compiler_params=params(6),
            name="pack",
        )(place, mine, other)

    g_packed = pack(pack_kernel, GEN_CHUNK)
    g_packed = exchange(g_packed, GATHER)
    mine, other, own_noise, other_noise = lax.optimization_barrier((mine, other, own_noise, other_noise))
    packed = pack(pack_score_kernel, SCORE_ROWS)
    g_packed, own_noise, other_noise = lax.optimization_barrier((g_packed, own_noise, other_noise))
    g_other = lax.ppermute(g_packed, "s", SIBLING)
    packed, g_packed, g_other = lax.optimization_barrier((packed, g_packed, g_other))
    packed = exchange(packed, GATHER)
    low, high = (a[:, GEN_ROWS : GEN_ROWS + 2 * MODS_ROWS] for a in in_order(s, g_packed, g_other))
    mods = jnp.stack([low, high]).reshape(2, 4, 2, 2, 4, 9, 128).transpose(5, 1, 0, 2, 3, 4, 6)
    mods = mods.reshape(9, 32, 512)[:, :, :480].reshape(9, 5, D).astype(F32)
    mods = jnp.pad(mods, ((0, 0), (0, 3), (0, 0)))

    by_image = lambda *shape: pl.BlockSpec((1, *shape), lambda i: (i,) + (0,) * len(shape))
    noise_rows = pl.BlockSpec((HALF, 128), lambda i: (i, 0))
    mods_of = lambda net: pl.BlockSpec((1, 8, D), lambda i: (3 * net + i, 0, 0))
    local = pltpu.HBM((IMAGES, TOKENS, COLS), F32)
    wide = pltpu.HBM((IMAGES, TOKENS, D), BF16)
    gen_embed, teacher_embed, fake_embed = in_hbm(gen_embed, teacher_embed, fake_embed)
    gen_final, teacher_final, fake_final = in_hbm(gen_final, teacher_final, fake_final)

    sums = pl.pallas_call(
        sums_kernel,
        grid=(1,),
        in_specs=[whole((C, D))] * 3 + [whole((9, 8, D))],
        out_specs=whole((3, 56, C)),
        out_shape=jax.ShapeDtypeStruct((3, 56, C), F32),
        compiler_params=params(16),
        name="sums",
    )(gen_final, teacher_final, fake_final, mods)

    part, g_shaped, g_pre, g_res = pl.pallas_call(
        generator_kernel,
        grid=(IMAGES,),
        in_specs=[
            smem(), noise_rows, noise_rows, whole((C, D)), mods_of(0), whole((C, D)),
            *([whole((CHUNKS, GEN_CHUNK, 128))] * 2),
        ],
        out_specs=[whole((OWNERS, 32, 128)), by_image(TOKENS, D), by_image(TOKENS, COLS), by_image(TOKENS, COLS)],
        out_shape=[jax.ShapeDtypeStruct((OWNERS, 32, 128), BF16), wide, local, local],
        scratch_shapes=[pltpu.VMEM((D, COLS), BF16), pltpu.VMEM((C, 3 * C), BF16), pltpu.VMEM((C, 128), F32),
                        pltpu.VMEM((OWNERS, 32, 128), F32)],
        compiler_params=params(16),
        cost_estimate=pl.CostEstimate(flops=12 * 10**9, bytes_accessed=30 * 10**6, transcendentals=0),
        name="generator",
    )(place, own_noise, other_noise, gen_embed, mods, gen_final, g_packed, g_other)
    packed, part = lax.optimization_barrier((packed, part))
    part = exchange(part, COMBINE)

    net_mods = lambda net: pl.BlockSpec((IMAGES, 8, D), lambda *_: (net, 0, 0))
    pack1, keep = pl.pallas_call(
        samples_kernel,
        grid=(1,),
        in_specs=[
            smem(), smem(), whole((OWNERS, 32, 128)), whole((NOISE_ROWS, 128)), whole((3, 56, C)),
        ],
        out_specs=[whole((OWNERS, 24, 128)), whole((4, 48, C))],
        out_shape=[
            jax.ShapeDtypeStruct((OWNERS, 24, 128), F32),
            jax.ShapeDtypeStruct((4, 48, C), F32),
        ],
        compiler_params=params(5),
        name="samples",
    )(place, gen_time, part, own_noise, sums)
    packed, pack1 = lax.optimization_barrier((packed, pack1))
    pack1 = exchange(pack1, COMBINE)
    other_packed = lax.ppermute(packed, "s", SIBLING)

    part2, samples, f_shaped, f_pre, f_res = pl.pallas_call(
        score_kernel,
        grid=(IMAGES,),
        in_specs=[
            smem(), smem(), whole((OWNERS, 24, 128)), noise_rows, noise_rows,
            whole((C, D)), whole((C, D)), net_mods(1), net_mods(2), whole((C, D)), whole((C, D)),
            *([whole((CHUNKS, SCORE_ROWS, 128))] * 2),
        ],
        out_specs=[
            whole((OWNERS, 64, 128)), by_image(C, HALF), by_image(TOKENS, D), whole((IMAGES, TOKENS, COLS)),
            whole((IMAGES, TOKENS, COLS)),
        ],
        out_shape=[
            jax.ShapeDtypeStruct((OWNERS, 64, 128), BF16),
            jax.ShapeDtypeStruct((IMAGES, C, HALF), F32),
            wide, local, local,
        ],
        scratch_shapes=[
            *([pltpu.VMEM((D, COLS), BF16)] * 2), *([pltpu.VMEM((C, 3 * C), BF16)] * 2),
            *([pltpu.VMEM((C, 128), F32)] * 2), *([pltpu.VMEM((IMAGES * TOKENS, D), BF16)] * 2),
            pltpu.VMEM((IMAGES, TOKENS, C), BF16),
            pltpu.VMEM((OWNERS, 64, 128), F32),
        ],
        compiler_params=params(34),
        cost_estimate=pl.CostEstimate(flops=24 * 10**9, bytes_accessed=50 * 10**6, transcendentals=0),
        name="score",
    )(place, score_time, pack1, own_noise, other_noise, teacher_embed, fake_embed, mods, mods,
      teacher_final, fake_final, packed, other_packed)
    part2 = exchange(part2, COMBINE)

    pack2 = pl.pallas_call(
        cotangent_kernel,
        grid=(1,),
        in_specs=[
            smem(), smem(), smem(), whole((OWNERS, 64, 128)), whole((NOISE_ROWS, 128)), whole((4, 48, C)),
            whole((3, 56, C)),
        ],
        out_specs=whole((OWNERS, 64, 128)),
        out_shape=jax.ShapeDtypeStruct((OWNERS, 64, 128), BF16),
        compiler_params=params(6),
        name="cotangents",
    )(place, gen_time, score_time, part2, own_noise, keep, sums)
    pack2 = exchange(pack2, COMBINE)
    samples, pack2 = lax.optimization_barrier((samples, pack2))
    own_samples = samples
    samples = lax.ppermute(samples, "s", SIBLING)

    gap = jnp.sum(pack2[:, 48:57, 96].astype(F32).reshape(OWNERS, 3, 3), axis=(0, 2))
    gap = jnp.broadcast_to(jnp.pad(gap, (0, 125)), (16, 1, 128))
    gap = exchange(gap, TOKEN_AXES)
    samples, gap = lax.optimization_barrier((samples, gap))
    samples = jnp.where(lax.axis_index("h") == s, own_samples, samples).transpose(0, 2, 1)

    by_columns = pl.BlockSpec((IMAGES, TOKENS, 768), lambda x: (0, 0, x))
    partial = jax.ShapeDtypeStruct((CHUNKS, GEN_ROWS, 128), BF16)
    partial_spec = pl.BlockSpec((2, GEN_ROWS, 128), lambda x: (x, 0, 0))

    def gradient(net, gaps, mods_net, final, pre, res, shaped):
        kept, sent = pl.pallas_call(
            functools.partial(gradient_kernel, net),
            grid=(4,),
            in_specs=[
                smem(), whole((OWNERS, 64, 128)), *([whole((16, 1, 128))] * len(gaps)), net_mods(mods_net),
                whole((C, D)), *([whole((IMAGES, TOKENS, COLS))] * 2), by_columns,
            ],
            out_specs=[partial_spec, partial_spec],
            out_shape=[partial, partial],
            scratch_shapes=[pltpu.VMEM((COLS, IMAGES * TOKENS), BF16)],
            compiler_params=params(13),
            cost_estimate=pl.CostEstimate(flops=7 * 10**9, bytes_accessed=20 * 10**6, transcendentals=0),
        name="gradient",
        )(place, pack2, *gaps, mods, final, *in_hbm(pre, res, shaped))
        return kept, lax.ppermute(sent, "s", SIBLING)

    pieces = gradient(0, (), 2, fake_final, f_pre, f_res, f_shaped)
    pieces += gradient(1, (gap,), 0, gen_final, g_pre, g_res, g_shaped)
    both = pl.pallas_call(
        add_kernel,
        grid=(1,),
        in_specs=[whole((CHUNKS, GEN_ROWS, 128))] * 4,
        out_specs=whole((CHUNKS, 2 * GEN_ROWS, 128)),
        out_shape=jax.ShapeDtypeStruct((CHUNKS, 2 * GEN_ROWS, 128), BF16),
        compiler_params=params(16),
        name="add",
    )(*pieces)
    tiles = jax.ShapeDtypeStruct((2, 144, 128), BF16)
    kept, sent = pl.pallas_call(
        sum_kernel,
        grid=(1,),
        in_specs=[smem(), whole((CHUNKS, 2 * GEN_ROWS, 128))],
        out_specs=[whole((2, 144, 128))] * 2,
        out_shape=[tiles, tiles],
        compiler_params=params(8),
        name="sum",
    )(place, exchange(both, GATHER))
    kept = lax.ppermute(kept, PLACES, SWAP)
    sent = lax.ppermute(sent, PLACES, SWAP_TURNED)
    fake_grad, gen_grad = pl.pallas_call(
        place_kernel,
        grid=(1,),
        in_specs=[smem(), whole((2, 144, 128)), whole((2, 144, 128))],
        out_specs=[whole((ROWS, 384))] * 2,
        out_shape=[jax.ShapeDtypeStruct((ROWS, 384), F32)] * 2,
        compiler_params=params(4),
        name="place",
    )(place, kept, sent)
    return (samples, gen_grad, fake_grad)


def solution(mesh):
    split = Mesh(mesh.devices.reshape(4, 4, 2, 2, 2, 2), ("g", "x", "h", "w", "v", "s"))
    tokens = P(None, ROW_AXES, None)
    columns = P(None, ROW_AXES)
    block = P(ROW_AXES, ("g", "s"))
    net = (P(), columns, block, P())
    return jax.shard_map(
        shards,
        mesh=split,
        in_specs=(tokens, tokens, P(), P(), *net, *net, *net),
        out_specs=(tokens, block, block),
        check_vma=False,
    )
```

```python
import functools
import math

import jax
import jax.numpy as jnp
from jax import lax
from jax.experimental import pallas as pl
from jax.experimental.pallas import tpu as pltpu
from jax.sharding import Mesh
from jax.sharding import PartitionSpec as P

S = 4096
STEPS = 1000
D = 3072
C = 64
IMAGES = 3

norm_epsilon = 1e-06
gap_epsilon = 1e-05

F32 = jnp.float32
BF16 = jnp.bfloat16

GATHER = ("x", "w")
ROW_AXES = ("x", "h", "w", "v")
COMBINE = ("v", "h", "g")
TOKEN_AXES = ("x", "w", "s")
OWNERS = 16
TOKENS = 256
HALF = 128
OWNED = 16
ROWS = 96
WIDE = 128
NARROW = 64
COLS = WIDE + NARROW
GEN_ROWS = 288
NOISE_ROWS = 384
MODS_AT = 480
MODS_ROWS = 36
SENT_ROWS = 528
GEN_CHUNK = 368
SCORE_ROWS = 576
CHUNKS = 8
BLOCK = 512

PLACES = ("g", "h", "v", "s")


def number(g, h, v, s):
    return g * 8 + h * 4 + v * 2 + s


EVERY = [(g, h, v, s) for g in range(4) for h in range(2) for v in range(2) for s in range(2)]
SWAP, SWAP_TURNED = [
    [(number(g, h, v, s), number((g + 2) % 4, s, v ^ turn, h)) for g, h, v, s in EVERY] for turn in range(2)
]
NEAR, NEAR_TURNED = [
    [(number(g, h, v, s), number(g if h == s else 3 - g, s, v ^ turn, h)) for g, h, v, s in EVERY] for turn in range(2)
]
SIBLING = [(0, 1), (1, 0)]


def params(mib):
    return pltpu.CompilerParams(vmem_limit_bytes=mib * 1024 * 1024)


def smem():
    return pl.BlockSpec(memory_space=pltpu.SMEM)


def whole(shape):
    zeros = (0,) * len(shape)
    return pl.BlockSpec(shape, lambda *_: zeros)


def dot(a, b):
    return jnp.dot(a, b, preferred_element_type=F32)


def dot_turned(a, b):
    return lax.dot_general(a, b, (((1,), (1,)), ((), ())), preferred_element_type=F32)


def time_features(steps, embed_width):
    times = (steps.astype(F32) + 1.0) / (STEPS + 1.0)
    half = embed_width // 2
    frequency = jnp.exp(-jnp.log(10000.0) * jnp.arange(half, dtype=F32) / half)
    angles = 1000.0 * times[:, None] * frequency[None, :]
    embedding = jnp.concatenate([jnp.cos(angles), jnp.sin(angles)], axis=1)
    return (times, jax.nn.silu(embedding).astype(BF16))


def to_row(numbers):
    shape = (numbers[0].shape[0], OWNED, 128)
    lane = lax.broadcasted_iota(jnp.int32, shape, 2)
    token = lax.broadcasted_iota(jnp.int32, shape, 1)
    total = jnp.zeros(shape, F32)
    for k, number in enumerate(numbers):
        total = jnp.where(lane == token + OWNED * k, number, total)
    return jnp.sum(total, axis=1, keepdims=True)


def row_pieces(numbers, stride):
    row = to_row(numbers)
    per_row = 128 // stride
    rows = [row.astype(BF16).astype(F32)]
    row = row - rows[0]
    rows.append(row.astype(BF16).astype(F32))
    rows.append((row - rows[1]).astype(BF16).astype(F32))
    packed = [jnp.concatenate([r[:, :, :stride] for r in rows[:per_row]], axis=2)]
    if len(rows) > per_row:
        packed.append(jnp.concatenate([rows[per_row][:, :, :stride], jnp.zeros_like(row)[:, :, : 128 - stride]], axis=2))
    else:
        packed[0] = jnp.concatenate([packed[0], jnp.zeros_like(row)[:, :, : 128 - 3 * stride]], axis=2)
    return packed


def from_row(row, k):
    shape = (row.shape[0], OWNED, 128)
    lane = lax.broadcasted_iota(jnp.int32, shape, 2)
    token = lax.broadcasted_iota(jnp.int32, shape, 1)
    return jnp.sum(jnp.where(lane == token + OWNED * k, row, 0.0), axis=2, keepdims=True)


def local_lanes(load, place_ref):
    tile = load(pl.ds(pl.multiple_of(place_ref[1], 128), 128))
    middle = load(pl.ds(pl.multiple_of(place_ref[2], 128), 128))
    part = jnp.where(place_ref[0] == 0, middle[:, :NARROW], middle[:, NARROW:])
    return jnp.concatenate([tile, part], axis=1)


def unpack_weights(place_ref, own_ref, other_ref, net, w_ref):
    s = place_ref[4]
    for packed_ref, side in ((own_ref, s), (other_ref, 1 - s)):
        for chunk in range(CHUNKS):
            x, w = chunk // 2, chunk % 2
            for v in range(2):
                k = pl.multiple_of((x * 8 + w * 2 + v) * ROWS + side * (4 * ROWS), 32)
                first = max(net - 1, 0) * 192 + v * ROWS
                w_ref[pl.ds(k, ROWS), :WIDE] = packed_ref[chunk, first : first + ROWS, :]
                if net == 0:
                    part = packed_ref[chunk, 192:288, v * NARROW : (v + 1) * NARROW]
                else:
                    part = packed_ref[chunk, 384 + v * ROWS : 384 + (v + 1) * ROWS, (net - 1) * NARROW : net * NARROW]
                w_ref[pl.ds(k, ROWS), WIDE:] = part


def split_bits(value, count):
    pieces = []
    for _ in range(count):
        piece = value.astype(BF16)
        pieces.append(piece)
        value = value - piece.astype(F32)
    return pieces


def embed_moments(embed_ref, gram_ref, mean_ref):
    embed = embed_ref[...]
    ones = jnp.ones((8, D), BF16)
    column = dot_turned(embed, ones)[:, 0:1] / D
    row = dot_turned(ones, embed)[0:1] / D
    gram = dot_turned(embed, embed) / D - column * row
    gram_ref[...] = jnp.concatenate(split_bits(gram, 3), axis=1)
    mean_ref[...] = jnp.broadcast_to(column, mean_ref.shape)


def shape_tokens(x, embed_ref, mods_ref, image, gram_ref, mean_ref, store):
    turned = dot(x, gram_ref[...])
    turned = turned[:, :C] + turned[:, C : 2 * C] + turned[:, 2 * C :]
    inverse = lax.rsqrt(jnp.sum(turned * x.astype(F32), axis=1, keepdims=True) + norm_epsilon)
    inverse = jnp.broadcast_to(inverse, (TOKENS, BLOCK))
    twice = jnp.concatenate([x, x], axis=1)
    mean = mean_ref[:, 0:1]
    for b in range(D // BLOCK):
        cut = slice(b * BLOCK, (b + 1) * BLOCK)
        scaled = (embed_ref[:, cut].astype(F32) - mean) * (1.0 + mods_ref[image, 1:2, cut])
        scaled = jnp.concatenate(split_bits(scaled, 2), axis=0)
        store(cut, (dot(twice, scaled) * inverse + mods_ref[image, 0:1, cut]).astype(BF16))


def finish(preactivation, x, embed_ref, mods_ref, image, final_ref, place_ref):
    activated = jax.nn.gelu(preactivation, approximate=True).astype(BF16).astype(F32)
    own_hidden = dot(x, local_lanes(lambda at: embed_ref[:, at], place_ref))
    gate = local_lanes(lambda at: mods_ref[image, 2:3, at], place_ref)
    scale = local_lanes(lambda at: mods_ref[image, 4:5, at], place_ref)
    residual = own_hidden + gate * activated
    total = jnp.sum(residual, axis=1, keepdims=True)
    total_square = jnp.sum(residual * residual, axis=1, keepdims=True)
    own_mean = total / COLS
    final = local_lanes(lambda at: final_ref[:, at], place_ref)
    centred = ((residual - own_mean) * (1.0 + scale)).astype(BF16)
    partial = dot_turned(centred, final)
    return residual, partial, total, total_square


def owned(value):
    return value.reshape(OWNERS, OWNED, value.shape[-1])


def sums_kernel(g_final_ref, t_final_ref, f_final_ref, mods_ref, out_ref):
    run = lax.broadcasted_iota(jnp.int32, (OWNERS, D), 1) // COLS
    own = run == lax.broadcasted_iota(jnp.int32, (OWNERS, D), 0)
    for net, final_ref in enumerate((g_final_ref, t_final_ref, f_final_ref)):
        scales = [mods_ref[3 * net + i, 4:5, :] for i in range(IMAGES)]
        shifts = [mods_ref[3 * net + i, 3:4, :] for i in range(IMAGES)]
        left = [jnp.where(own, row, 0.0) for row in scales + [jnp.ones((1, D), F32)]]
        left = jnp.concatenate(left + shifts + [jnp.zeros((5, D), F32)], axis=0).astype(BF16)
        sums = dot_turned(left, final_ref[...])
        ones = sums[3 * OWNERS : 4 * OWNERS]
        runs = [sums[i * OWNERS : (i + 1) * OWNERS] + ones for i in range(IMAGES)]
        totals = [jnp.sum(r, axis=0, keepdims=True) for r in runs]
        out_ref[net] = jnp.concatenate(runs + totals + [sums[64:67], jnp.zeros((2, C), F32)], axis=0)


def read_sums(sums_ref, net):
    runs = [sums_ref[net, i * OWNERS : (i + 1) * OWNERS] for i in range(IMAGES)]
    return runs, [sums_ref[net, 48 + i : 49 + i] for i in range(IMAGES)], [sums_ref[net, 51 + i : 52 + i] for i in range(IMAGES)]


def add_up(partials, totals, squares, runs):
    means = totals * (1.0 / COLS)
    ordered = [((g + 2) % 4 * 2 + h) * 2 + v for v in range(2) for h in range(2) for g in range(4)]
    ordered = jnp.concatenate([runs[run : run + 1][None] for run in ordered], axis=0)
    partial = jnp.sum(partials + means * ordered, axis=0)
    average = jnp.sum(totals, axis=0) / D
    inverse = lax.rsqrt(jnp.sum(squares, axis=0) / D - average * average + norm_epsilon)
    return partial, average, inverse


def split_kernel(place_ref, cond_ref, gen_noise_ref, score_noise_ref, gen_ref, teacher_ref, fake_ref,
                 gen_mod_ref, teacher_mod_ref, fake_mod_ref, mine_ref, other_ref, noise_ref):
    for i in range(IMAGES):
        noise = jnp.concatenate([gen_noise_ref[i], score_noise_ref[i]], axis=0).astype(F32).T.astype(BF16)
        noise_ref[i * HALF : (i + 1) * HALF] = noise
    cond = cond_ref[...]
    mods = [dot_turned(cond, ref[...]) for ref in (gen_mod_ref, teacher_mod_ref, fake_mod_ref)]
    mods = jnp.concatenate([mods[0][0:3], mods[1][3:6], mods[2][3:6]], axis=0)
    mods = jnp.concatenate([mods, jnp.zeros((9, 32), F32)], axis=1)
    mods = jnp.concatenate([mods[:, 128 * p : 128 * (p + 1)] for p in range(4)] + [jnp.zeros((12, 128), F32)], axis=0)
    mine_ref[MODS_AT:] = mods.astype(BF16)
    other_ref[MODS_AT:] = mods.astype(BF16)
    first = place_ref[0] == 0
    mine, other = [], []
    for n, ref in enumerate((gen_ref, teacher_ref, fake_ref)):
        rows = slice(n * ROWS, (n + 1) * ROWS)
        low, high = ref[:, :128], ref[:, 256:]
        mine_ref[rows] = jnp.where(first, low, high)
        other_ref[rows] = jnp.where(first, high, low)
        low, high = ref[:, 128:192], ref[:, 192:256]
        mine.append(jnp.where(first, low, high))
        other.append(jnp.where(first, high, low))
    for ref, parts in ((mine_ref, mine), (other_ref, other)):
        ref[3 * ROWS : 4 * ROWS] = jnp.concatenate(parts[1:], axis=1)
        ref[4 * ROWS : MODS_AT] = jnp.concatenate([parts[0], parts[0]], axis=1)


def in_order(v, mine, other):
    return jnp.where(v == 0, mine, other), jnp.where(v == 0, other, mine)


def pack_kernel(place_ref, mine_ref, other_ref, out_ref):
    v = place_ref[0]
    tiles = in_order(v, mine_ref[:ROWS], other_ref[:ROWS])
    parts = in_order(v, mine_ref[4 * ROWS : MODS_AT], other_ref[4 * ROWS : MODS_AT])
    parts = jnp.concatenate([part[:, :NARROW] for part in parts], axis=1)
    mods = in_order(v, mine_ref[MODS_AT:].astype(F32), other_ref[MODS_AT:].astype(F32))
    mods = jnp.concatenate([mods[0][:MODS_ROWS], mods[1][:MODS_ROWS], jnp.zeros((8, 128), F32)], axis=0)
    gen = jnp.concatenate([*tiles, parts, mods.astype(BF16)], axis=0)
    for k in range(CHUNKS):
        out_ref[k] = gen


def pack_score_kernel(place_ref, mine_ref, other_ref, out_ref):
    cuts = [slice(n * ROWS, (n + 1) * ROWS) for n in (1, 2, 3)]
    ordered = [in_order(place_ref[0], mine_ref[rows], other_ref[rows]) for rows in cuts]
    score = jnp.concatenate([block for pair in ordered for block in pair], axis=0)
    for k in range(CHUNKS):
        out_ref[k] = score


def generator_kernel(place_ref, own_ref, other_ref, embed_ref, mods_ref, final_ref, own_w_ref, other_w_ref,
                     part_ref, shaped_ref, pre_ref, res_ref, w_ref, gram_ref, mean_ref, sum_ref, all_ref, x_ref):
    i = pl.program_id(0)
    v = place_ref[0]

    @pl.when(i == 0)
    def _():
        embed_moments(embed_ref, gram_ref, mean_ref)
        unpack_weights(place_ref, own_w_ref, other_w_ref, 0, w_ref)
        sum_ref[:, 24:, :] = jnp.zeros((OWNERS, 8, 128), F32)

    x = jnp.concatenate(in_order(v, own_ref[:, :C], other_ref[:, :C]), axis=0)

    x_ref[i] = x
    tokens = pl.ds(pl.multiple_of(i * TOKENS, TOKENS), TOKENS)

    def store(cut, shaped):
        shaped_ref[0, :, cut] = shaped
        all_ref[tokens, cut] = shaped

    shape_tokens(x, embed_ref, mods_ref, i, gram_ref, mean_ref, store)

    @pl.when(i == IMAGES - 1)
    def _():
        every = dot(all_ref[...], w_ref[...])
        for n in range(IMAGES):
            pre = every[n * TOKENS : (n + 1) * TOKENS]
            res, partial, total, square = finish(pre, x_ref[n], embed_ref, mods_ref, n, final_ref, place_ref)
            pre_ref[n] = pre
            res_ref[n] = res
            pieces = owned(partial)
            sum_ref[:, 8 * n : 8 * n + 8, :] = jnp.concatenate([pieces[:, :8], pieces[:, 8:]], axis=2)
            sum_ref[:, 24 + n : 25 + n, :] = row_pieces([owned(total), owned(square)], 32)[0]
        part_ref[...] = sum_ref[...].astype(BF16)


def samples_kernel(place_ref, time_ref, got_ref, noise_ref, sums_ref, out_ref, keep_ref):
    runs, scales, shifts = read_sums(sums_ref, 0)
    got = got_ref[...].astype(F32)
    packed = []
    for i in range(IMAGES):
        block = got[:, 8 * i : 8 * i + 8]
        partials = jnp.concatenate([block[:, :, :C], block[:, :, C:]], axis=1)
        row = got[:, 24 + i : 25 + i]
        row = row[:, :, :32] + row[:, :, 32:64] + row[:, :, 64:96]
        row = jnp.concatenate([row, jnp.zeros((OWNERS, 1, 96), F32)], axis=2)
        partial, average, inverse = add_up(partials, from_row(row, 0), from_row(row, 1), runs[i])
        inner = inverse * (partial - average * scales[i])
        velocity = inner + shifts[i]
        noise = noise_ref[pl.ds(pl.multiple_of(place_ref[3] + i * HALF, 16), OWNED), :][:, :C].astype(F32)
        samples = noise - time_ref[i] * velocity
        packed.append(jnp.concatenate([samples[:8], samples[8:]], axis=1))
        at = slice(i * OWNED, (i + 1) * OWNED)
        keep_ref[0, at, :] = samples
        keep_ref[1, at, :] = inner
        keep_ref[2, at, :] = jnp.broadcast_to(average, (OWNED, C))
        keep_ref[3, at, :] = jnp.broadcast_to(inverse, (OWNED, C))
    out_ref[...] = jnp.broadcast_to(jnp.concatenate(packed, axis=0)[None], out_ref.shape)


def mix(samples, noise, t):
    return ((1.0 - t) * samples + t * noise).astype(BF16)


def score_kernel(place_ref, time_ref, got_ref, own_ref, other_ref,
                 t_embed_ref, f_embed_ref, t_mods_ref, f_mods_ref, t_final_ref, f_final_ref, own_w_ref, other_w_ref,
                 part_ref, samples_ref, shaped_ref, pre_ref, res_ref,
                 t_w_ref, f_w_ref, t_gram_ref, f_gram_ref, t_mean_ref, f_mean_ref, t_shaped_ref, f_shaped_ref, x_ref, sum_ref):
    i = pl.program_id(0)
    v = place_ref[0]

    @pl.when(i == 0)
    def _():
        embed_moments(t_embed_ref, t_gram_ref, t_mean_ref)
        embed_moments(f_embed_ref, f_gram_ref, f_mean_ref)
        unpack_weights(place_ref, own_w_ref, other_w_ref, 1, t_w_ref)
        unpack_weights(place_ref, own_w_ref, other_w_ref, 2, f_w_ref)
        sum_ref[:, 48:, :] = jnp.zeros((OWNERS, 16, 128), F32)
    got = got_ref[:, pl.ds(pl.multiple_of(i * 8, 8), 8), :]
    samples = jnp.concatenate([got[:, :, :C], got[:, :, C:]], axis=1).reshape(TOKENS, C)
    turned = jnp.concatenate([samples[:HALF], samples[HALF:]], axis=1).T
    samples_ref[0] = jnp.where(v == 0, turned[:C], turned[C:])
    own, other = own_ref[:, C:].astype(F32), other_ref[:, C:].astype(F32)
    noise = jnp.concatenate(in_order(v, own, other), axis=0)
    noised = mix(samples, noise, time_ref[i])
    x_ref[i] = noised
    tokens = pl.ds(pl.multiple_of(i * TOKENS, TOKENS), TOKENS)

    def t_store(cut, shaped):
        t_shaped_ref[tokens, cut] = shaped

    def f_store(cut, shaped):
        f_shaped_ref[tokens, cut] = shaped
        shaped_ref[0, :, cut] = shaped

    shape_tokens(noised, t_embed_ref, t_mods_ref, i, t_gram_ref, t_mean_ref, t_store)
    shape_tokens(noised, f_embed_ref, f_mods_ref, i, f_gram_ref, f_mean_ref, f_store)

    @pl.when(i == IMAGES - 1)
    def _():
        t_pre = dot(t_shaped_ref[...], t_w_ref[...])
        f_pre = dot(f_shaped_ref[...], f_w_ref[...])
        for n in range(IMAGES):
            x = x_ref[n]
            rows = slice(n * TOKENS, (n + 1) * TOKENS)
            _, t_partial, t_total, t_square = finish(t_pre[rows], x, t_embed_ref, t_mods_ref, n, t_final_ref, place_ref)
            res, f_partial, f_total, f_square = finish(f_pre[rows], x, f_embed_ref, f_mods_ref, n, f_final_ref, place_ref)
            pre_ref[n] = f_pre[rows]
            res_ref[n] = res
            sum_ref[:, 16 * n : 16 * n + 16, :] = owned(jnp.concatenate([t_partial, f_partial], axis=1))
            pieces = row_pieces([owned(v) for v in (t_total, t_square, f_total, f_square)], 64)
            for k in range(2):
                sum_ref[:, 48 + 2 * n + k : 49 + 2 * n + k, :] = pieces[k]
        part_ref[...] = sum_ref[...].astype(BF16)


def cotangent_kernel(place_ref, gen_time_ref, time_ref, got_ref, noise_ref, keep_ref, sums_ref, out_ref):
    loss_scale = 1.0 / math.sqrt(IMAGES * S)
    t_runs, t_scales, t_shifts = read_sums(sums_ref, 1)
    f_runs, f_scales, f_shifts = read_sums(sums_ref, 2)
    got = got_ref[...].astype(F32)
    lane = lax.broadcasted_iota(jnp.int32, (1, 128), 1)
    cots, rows = [], []
    for i in range(IMAGES):
        block = got[:, 16 * i : 16 * i + 16]
        row = got[:, 48 + 2 * i : 50 + 2 * i]
        row = row[:, :1, :64] + row[:, :1, 64:] + row[:, 1:, :64]
        row = jnp.concatenate([row, jnp.zeros((OWNERS, 1, 64), F32)], axis=2)

        def inner(partials, k, runs, scale):
            partial, average, inverse = add_up(partials, from_row(row, k), from_row(row, k + 1), runs)
            return inverse * (partial - average * scale), average, inverse

        t_inner, _, _ = inner(block[:, :, :C], 0, t_runs[i], t_scales[i])
        f_inner, f_average, f_inverse = inner(block[:, :, C:], 2, f_runs[i], f_scales[i])
        teacher, fake = t_inner + t_shifts[i], f_inner + f_shifts[i]
        at = slice(i * OWNED, (i + 1) * OWNED)
        samples, g_inner = keep_ref[0, at, :], keep_ref[1, at, :]
        g_average, g_inverse = keep_ref[2, at, 0:1], keep_ref[3, at, 0:1]
        noise = noise_ref[pl.ds(pl.multiple_of(place_ref[3] + i * HALF, 16), OWNED), :][:, C:].astype(F32)
        t = time_ref[i]
        noised = mix(samples, noise, t).astype(F32)
        distance = jnp.sum(jnp.abs(samples - noised + t * teacher))
        gen_cot = (-(gen_time_ref[i] * t * loss_scale) * (teacher - fake)).astype(BF16).astype(F32)
        fake_cot = (loss_scale * (fake - noise + samples)).astype(BF16).astype(F32)
        numbers = []
        for cot, column, value, average, inverse in (
            (fake_cot, f_scales[i], f_inner, f_average, f_inverse),
            (gen_cot, sums_ref[0, 48 + i : 49 + i], g_inner, g_average, g_inverse),
        ):
            first = jnp.sum(cot * column, axis=1, keepdims=True) / D
            second = jnp.sum(cot * value, axis=1, keepdims=True) / D
            slope = inverse * inverse * second
            numbers += [inverse, slope, average * slope - inverse * first]
        cots.append(jnp.concatenate([fake_cot, gen_cot], axis=1))
        numbers_row = to_row([number[None] for number in numbers])[0]
        numbers_row = jnp.where(lane == 96, distance, numbers_row)
        for _ in range(3):
            rounded = numbers_row.astype(BF16).astype(F32)
            rows.append(rounded)
            numbers_row = numbers_row - rounded
    rows.append(jnp.zeros((7, 128), F32))
    packed = jnp.concatenate(cots + rows, axis=0).astype(BF16)
    out_ref[...] = jnp.broadcast_to(packed[None], out_ref.shape)


def gelu_slope(v):
    a, b = math.sqrt(2.0 / math.pi), 0.044715
    t = jnp.tanh(a * (v + b * (v * v * v)))
    return 0.5 * (1.0 + t) + 0.5 * v * (1.0 - t * t) * (a * (1.0 + 3.0 * b * (v * v)))


def gradient_kernel(net, place_ref, got_ref, *refs):
    gap_ref, refs = (refs[0], refs[1:]) if net == 1 else (None, refs)
    mods_ref, final_ref, pre_ref, res_ref, shaped_ref, keep_ref, send_ref, left_ref = refs

    @pl.when(pl.program_id(0) == 0)
    def _():
        final = local_lanes(lambda at: final_ref[:, at], place_ref)
        if net == 1:
            gaps = jnp.sum(gap_ref[...], axis=0)
        for i in range(IMAGES):
            row = got_ref[:, 48:64, :].astype(F32)
            row = row[:, 3 * i : 3 * i + 1] + row[:, 3 * i + 1 : 3 * i + 2] + row[:, 3 * i + 2 : 3 * i + 3]
            inverse, slope, offset = [from_row(row, 3 * net + k).reshape(TOKENS, 1) for k in range(3)]
            cot = got_ref[:, 16 * i : 16 * i + 16, :].reshape(TOKENS, 128)[:, net * C : (net + 1) * C]
            out_grad = dot(cot, final)
            scale = local_lanes(lambda at: mods_ref[i, 4:5, at], place_ref)
            gate = local_lanes(lambda at: mods_ref[i, 2:3, at], place_ref)
            res_grad = inverse * (out_grad * (1.0 + scale)) - slope * res_ref[i] + offset
            act_grad = res_grad * gate
            if net == 1:
                lane = lax.broadcasted_iota(jnp.int32, gaps.shape, 1)
                total = jnp.sum(jnp.where(lane == i, gaps, 0.0), axis=1, keepdims=True)
                act_grad = act_grad * (1.0 / (total / (S * C) + gap_epsilon))
            grad = act_grad * gelu_slope(pre_ref[i])
            turned = jnp.concatenate([grad, jnp.zeros((TOKENS, NARROW), F32)], axis=1).T
            left_ref[:, i * TOKENS : (i + 1) * TOKENS] = turned[:COLS].astype(BF16)

    grad = dot(left_ref[...], shaped_ref[...].reshape(IMAGES * TOKENS, 768))
    tiles = grad[:WIDE].T.astype(BF16)
    parts = jnp.concatenate([grad[WIDE:, :384], grad[WIDE:, 384:]], axis=0).T.astype(BF16)
    first = place_ref[4] == 0
    for w in range(2):
        sides = []
        for h in range(2):
            at = [(w * 2 + v) * ROWS for v in range(2)]
            lanes = slice(h * NARROW, (h + 1) * NARROW)
            narrow = jnp.concatenate([parts[k : k + ROWS, lanes] for k in at], axis=1)
            sides.append([tiles[h * 384 + k : h * 384 + k + ROWS] for k in at] + [narrow])
        for n, (low, high) in enumerate(zip(*sides, strict=True)):
            keep_ref[w, n * ROWS : (n + 1) * ROWS, :] = jnp.where(first, low, high)
            send_ref[w, n * ROWS : (n + 1) * ROWS, :] = jnp.where(first, high, low)


def add_kernel(f_keep_ref, f_got_ref, g_keep_ref, g_got_ref, out_ref):
    for n, (keep_ref, got_ref) in enumerate(((f_keep_ref, f_got_ref), (g_keep_ref, g_got_ref))):
        for k in range(CHUNKS):
            total = keep_ref[k].astype(F32) + got_ref[k].astype(F32)
            out_ref[k, n * GEN_ROWS : (n + 1) * GEN_ROWS] = total.astype(BF16)


def sum_kernel(place_ref, got_ref, keep_ref, send_ref):
    v = place_ref[0]
    for n in range(2):
        rows = slice(n * GEN_ROWS, (n + 1) * GEN_ROWS)
        total = got_ref[0, rows].astype(F32)
        for k in range(1, CHUNKS):
            total = total + got_ref[k, rows].astype(F32)
        def folded(rows, part):
            return jnp.concatenate([rows, jnp.concatenate([part[:48], part[48:]], axis=1)], axis=0)

        low = folded(total[:ROWS], total[2 * ROWS :, :NARROW])
        high = folded(total[ROWS : 2 * ROWS], total[2 * ROWS :, NARROW:])
        keep_ref[n] = jnp.where(v == 0, low, high).astype(BF16)
        send_ref[n] = jnp.where(v == 0, high, low).astype(BF16)


def place_kernel(place_ref, keep_ref, other_ref, fake_ref, gen_ref):
    for n, ref in enumerate((fake_ref, gen_ref)):
        low, high = in_order(place_ref[0], keep_ref[n].astype(F32), other_ref[n].astype(F32))
        ref[:, :128] = low[:ROWS]
        ref[:48, 128:256] = jnp.concatenate([low[ROWS:, :NARROW], high[ROWS:, :NARROW]], axis=1)
        ref[48:, 128:256] = jnp.concatenate([low[ROWS:, NARROW:], high[ROWS:, NARROW:]], axis=1)
        ref[:, 256:] = high[:ROWS]


def in_hbm(*arrays):
    return [pltpu.with_memory_space_constraint(a, pltpu.HBM) for a in arrays]


def exchange(value, axes):
    return lax.all_to_all(value, axes, 0, 0)


def shards(
    gen_noise,
    score_noise,
    gen_steps,
    score_steps,
    gen_embed,
    gen_modulation,
    gen_proj,
    gen_final,
    teacher_embed,
    teacher_modulation,
    teacher_proj,
    teacher_final,
    fake_embed,
    fake_modulation,
    fake_proj,
    fake_final,
):
    v, s = lax.axis_index("v"), lax.axis_index("s")
    start = (lax.rem(lax.axis_index("g") + 2, 4) * 2 + lax.axis_index("h")) * 384
    member = lax.axis_index(("h", "g"))
    place = jnp.stack([v, start + 256 * v, start + 128, member * OWNED, s]).astype(jnp.int32)
    gen_final, teacher_final, fake_final = gen_final.T, teacher_final.T, fake_final.T

    times, conds = time_features(jnp.concatenate([gen_steps, score_steps]), gen_modulation.shape[0])
    gen_time, score_time = times[:3], times[3:]
    halves = jax.ShapeDtypeStruct((SENT_ROWS, 128), BF16)
    mine, other, noise = pl.pallas_call(
        split_kernel,
        grid=(1,),
        in_specs=[smem(), whole((6, 256))] + [whole((IMAGES, C, HALF))] * 2 + [whole((ROWS, 384))] * 3
        + [whole((480, 256))] * 3,
        out_specs=[whole((SENT_ROWS, 128))] * 2 + [whole((NOISE_ROWS, 128))],
        out_shape=[halves, halves, jax.ShapeDtypeStruct((NOISE_ROWS, 128), BF16)],
        compiler_params=params(60),
        name="split",
    )(place, conds, gen_noise.transpose(0, 2, 1), score_noise.transpose(0, 2, 1), gen_proj, teacher_proj, fake_proj,
      gen_modulation.T, teacher_modulation.T, fake_modulation.T)
    mine = lax.ppermute(mine, PLACES, SWAP)
    other = lax.ppermute(other, PLACES, SWAP_TURNED)

    def pack(kernel, rows):
        return pl.pallas_call(
            kernel,
            grid=(1,),
            in_specs=[smem()] + [whole((SENT_ROWS, 128))] * 2,
            out_specs=whole((CHUNKS, rows, 128)),
            out_shape=jax.ShapeDtypeStruct((CHUNKS, rows, 128), BF16),
            compiler_params=params(6),
            name="pack",
        )(place, mine, other)

    g_packed = pack(pack_kernel, GEN_CHUNK)
    g_packed = exchange(g_packed, GATHER)
    g_packed, mine, other, noise = lax.optimization_barrier((g_packed, mine, other, noise))
    own_noise = lax.ppermute(noise, PLACES, NEAR)
    other_noise = lax.ppermute(noise, PLACES, NEAR_TURNED)
    packed = pack(pack_score_kernel, SCORE_ROWS)
    g_other = lax.ppermute(g_packed, "s", SIBLING)
    packed, g_packed, g_other = lax.optimization_barrier((packed, g_packed, g_other))
    packed = exchange(packed, GATHER)
    low, high = (a[:, GEN_ROWS : GEN_ROWS + 2 * MODS_ROWS] for a in in_order(s, g_packed, g_other))
    mods = jnp.stack([low, high]).reshape(2, 4, 2, 2, 4, 9, 128).transpose(5, 1, 0, 2, 3, 4, 6)
    mods = mods.reshape(9, 32, 512)[:, :, :480].reshape(9, 5, D).astype(F32)
    mods = jnp.pad(mods, ((0, 0), (0, 3), (0, 0)))

    by_image = lambda *shape: pl.BlockSpec((1, *shape), lambda i: (i,) + (0,) * len(shape))
    noise_rows = pl.BlockSpec((HALF, 128), lambda i: (i, 0))
    net_mods = lambda net: pl.BlockSpec((IMAGES, 8, D), lambda *_: (net, 0, 0))
    mods_of = lambda net: pl.BlockSpec((1, 8, D), lambda i: (3 * net + i, 0, 0))
    local = pltpu.HBM((IMAGES, TOKENS, COLS), F32)
    wide = pltpu.HBM((IMAGES, TOKENS, D), BF16)
    gen_embed, teacher_embed, fake_embed = in_hbm(gen_embed, teacher_embed, fake_embed)
    gen_final, teacher_final, fake_final = in_hbm(gen_final, teacher_final, fake_final)

    sums = pl.pallas_call(
        sums_kernel,
        grid=(1,),
        in_specs=[whole((C, D))] * 3 + [whole((9, 8, D))],
        out_specs=whole((3, 56, C)),
        out_shape=jax.ShapeDtypeStruct((3, 56, C), F32),
        compiler_params=params(16),
        name="sums",
    )(gen_final, teacher_final, fake_final, mods)

    part, g_shaped, g_pre, g_res = pl.pallas_call(
        generator_kernel,
        grid=(IMAGES,),
        in_specs=[
            smem(), noise_rows, noise_rows, whole((C, D)), net_mods(0), whole((C, D)),
            *([whole((CHUNKS, GEN_CHUNK, 128))] * 2),
        ],
        out_specs=[whole((OWNERS, 32, 128)), by_image(TOKENS, D), *([whole((IMAGES, TOKENS, COLS))] * 2)],
        out_shape=[jax.ShapeDtypeStruct((OWNERS, 32, 128), BF16), wide, local, local],
        scratch_shapes=[pltpu.VMEM((D, COLS), BF16), pltpu.VMEM((C, 3 * C), BF16), pltpu.VMEM((C, 128), F32),
                        pltpu.VMEM((OWNERS, 32, 128), F32), pltpu.VMEM((IMAGES * TOKENS, D), BF16),
                        pltpu.VMEM((IMAGES, TOKENS, C), BF16)],
        compiler_params=params(24),
        cost_estimate=pl.CostEstimate(flops=12 * 10**9, bytes_accessed=30 * 10**6, transcendentals=0),
        name="generator",
    )(place, own_noise, other_noise, gen_embed, mods, gen_final, g_packed, g_other)
    packed, part = lax.optimization_barrier((packed, part))
    part = exchange(part, COMBINE)

    pack1, keep = pl.pallas_call(
        samples_kernel,
        grid=(1,),
        in_specs=[
            smem(), smem(), whole((OWNERS, 32, 128)), whole((NOISE_ROWS, 128)), whole((3, 56, C)),
        ],
        out_specs=[whole((OWNERS, 24, 128)), whole((4, 48, C))],
        out_shape=[
            jax.ShapeDtypeStruct((OWNERS, 24, 128), F32),
            jax.ShapeDtypeStruct((4, 48, C), F32),
        ],
        compiler_params=params(5),
        name="samples",
    )(place, gen_time, part, own_noise, sums)
    packed, pack1 = lax.optimization_barrier((packed, pack1))
    pack1 = exchange(pack1, COMBINE)
    other_packed = lax.ppermute(packed, "s", SIBLING)

    part2, samples, f_shaped, f_pre, f_res = pl.pallas_call(
        score_kernel,
        grid=(IMAGES,),
        in_specs=[
            smem(), smem(), whole((OWNERS, 24, 128)), noise_rows, noise_rows,
            whole((C, D)), whole((C, D)), net_mods(1), net_mods(2), whole((C, D)), whole((C, D)),
            *([whole((CHUNKS, SCORE_ROWS, 128))] * 2),
        ],
        out_specs=[
            whole((OWNERS, 64, 128)), by_image(C, HALF), by_image(TOKENS, D), whole((IMAGES, TOKENS, COLS)),
            whole((IMAGES, TOKENS, COLS)),
        ],
        out_shape=[
            jax.ShapeDtypeStruct((OWNERS, 64, 128), BF16),
            jax.ShapeDtypeStruct((IMAGES, C, HALF), F32),
            wide, local, local,
        ],
        scratch_shapes=[
            *([pltpu.VMEM((D, COLS), BF16)] * 2), *([pltpu.VMEM((C, 3 * C), BF16)] * 2),
            *([pltpu.VMEM((C, 128), F32)] * 2), *([pltpu.VMEM((IMAGES * TOKENS, D), BF16)] * 2),
            pltpu.VMEM((IMAGES, TOKENS, C), BF16),
            pltpu.VMEM((OWNERS, 64, 128), F32),
        ],
        compiler_params=params(34),
        cost_estimate=pl.CostEstimate(flops=24 * 10**9, bytes_accessed=50 * 10**6, transcendentals=0),
        name="score",
    )(place, score_time, pack1, own_noise, other_noise, teacher_embed, fake_embed, mods, mods,
      teacher_final, fake_final, packed, other_packed)
    part2 = exchange(part2, COMBINE)

    pack2 = pl.pallas_call(
        cotangent_kernel,
        grid=(1,),
        in_specs=[
            smem(), smem(), smem(), whole((OWNERS, 64, 128)), whole((NOISE_ROWS, 128)), whole((4, 48, C)),
            whole((3, 56, C)),
        ],
        out_specs=whole((OWNERS, 64, 128)),
        out_shape=jax.ShapeDtypeStruct((OWNERS, 64, 128), BF16),
        compiler_params=params(6),
        name="cotangents",
    )(place, gen_time, score_time, part2, own_noise, keep, sums)
    pack2 = exchange(pack2, COMBINE)
    samples, pack2 = lax.optimization_barrier((samples, pack2))
    own_samples = samples
    samples = lax.ppermute(samples, "s", SIBLING)

    gap = jnp.sum(pack2[:, 48:57, 96].astype(F32).reshape(OWNERS, 3, 3), axis=(0, 2))
    gap = jnp.broadcast_to(jnp.pad(gap, (0, 125)), (16, 1, 128))
    gap = exchange(gap, TOKEN_AXES)
    samples, gap = lax.optimization_barrier((samples, gap))
    samples = jnp.where(lax.axis_index("h") == s, own_samples, samples).transpose(0, 2, 1)

    by_columns = pl.BlockSpec((IMAGES, TOKENS, 768), lambda x: (0, 0, x))
    partial = jax.ShapeDtypeStruct((CHUNKS, GEN_ROWS, 128), BF16)
    partial_spec = pl.BlockSpec((2, GEN_ROWS, 128), lambda x: (x, 0, 0))

    def gradient(net, gaps, mods_net, final, pre, res, shaped):
        kept, sent = pl.pallas_call(
            functools.partial(gradient_kernel, net),
            grid=(4,),
            in_specs=[
                smem(), whole((OWNERS, 64, 128)), *([whole((16, 1, 128))] * len(gaps)), net_mods(mods_net),
                whole((C, D)), *([whole((IMAGES, TOKENS, COLS))] * 2), by_columns,
            ],
            out_specs=[partial_spec, partial_spec],
            out_shape=[partial, partial],
            scratch_shapes=[pltpu.VMEM((COLS, IMAGES * TOKENS), BF16)],
            compiler_params=params(13),
            cost_estimate=pl.CostEstimate(flops=7 * 10**9, bytes_accessed=20 * 10**6, transcendentals=0),
        name="gradient",
        )(place, pack2, *gaps, mods, final, *in_hbm(pre, res, shaped))
        return kept, lax.ppermute(sent, "s", SIBLING)

    pieces = gradient(0, (), 2, fake_final, f_pre, f_res, f_shaped)
    pieces += gradient(1, (gap,), 0, gen_final, g_pre, g_res, g_shaped)
    both = pl.pallas_call(
        add_kernel,
        grid=(1,),
        in_specs=[whole((CHUNKS, GEN_ROWS, 128))] * 4,
        out_specs=whole((CHUNKS, 2 * GEN_ROWS, 128)),
        out_shape=jax.ShapeDtypeStruct((CHUNKS, 2 * GEN_ROWS, 128), BF16),
        compiler_params=params(16),
        name="add",
    )(*pieces)
    tiles = jax.ShapeDtypeStruct((2, 144, 128), BF16)
    kept, sent = pl.pallas_call(
        sum_kernel,
        grid=(1,),
        in_specs=[smem(), whole((CHUNKS, 2 * GEN_ROWS, 128))],
        out_specs=[whole((2, 144, 128))] * 2,
        out_shape=[tiles, tiles],
        compiler_params=params(8),
        name="sum",
    )(place, exchange(both, GATHER))
    kept = lax.ppermute(kept, PLACES, SWAP)
    sent = lax.ppermute(sent, PLACES, SWAP_TURNED)
    fake_grad, gen_grad = pl.pallas_call(
        place_kernel,
        grid=(1,),
        in_specs=[smem(), whole((2, 144, 128)), whole((2, 144, 128))],
        out_specs=[whole((ROWS, 384))] * 2,
        out_shape=[jax.ShapeDtypeStruct((ROWS, 384), F32)] * 2,
        compiler_params=params(4),
        name="place",
    )(place, kept, sent)
    return (samples, gen_grad, fake_grad)


def solution(mesh):
    split = Mesh(mesh.devices.reshape(4, 4, 2, 2, 2, 2), ("g", "x", "h", "w", "v", "s"))
    tokens = P(None, ROW_AXES, None)
    columns = P(None, ROW_AXES)
    block = P(ROW_AXES, ("g", "s"))
    net = (P(), columns, block, P())
    return jax.shard_map(
        shards,
        mesh=split,
        in_specs=(tokens, tokens, P(), P(), *net, *net, *net),
        out_specs=(tokens, block, block),
        check_vma=False,
    )
```

```python
import functools
import math

import jax
import jax.numpy as jnp
from jax import lax
from jax.experimental import pallas as pl
from jax.experimental.pallas import tpu as pltpu
from jax.sharding import Mesh
from jax.sharding import PartitionSpec as P

S = 4096
STEPS = 1000
D = 3072
C = 64
IMAGES = 3

norm_epsilon = 1e-06
gap_epsilon = 1e-05

F32 = jnp.float32
BF16 = jnp.bfloat16

GATHER = ("x", "w")
ROW_AXES = ("x", "h", "w", "v")
COMBINE = ("v", "h", "g")
TOKEN_AXES = ("x", "w", "s")
OWNERS = 16
TOKENS = 256
HALF = 128
OWNED = 16
ROWS = 96
WIDE = 128
NARROW = 64
COLS = WIDE + NARROW
GEN_ROWS = 288
NOISE_ROWS = 384
MODS_AT = 480
MODS_ROWS = 36
SENT_ROWS = 528
GEN_CHUNK = 368
SCORE_ROWS = 576
CHUNKS = 8
OFFSETS = [(2, 1), (1, 1), (3, 1), (2, 0), (1, 0), (3, 0), (0, 1), (0, 0)]
BLOCK = 512

PLACES = ("g", "h", "v", "s")


def number(g, h, v, s):
    return g * 8 + h * 4 + v * 2 + s


EVERY = [(g, h, v, s) for g in range(4) for h in range(2) for v in range(2) for s in range(2)]
SWAP, SWAP_TURNED = [
    [(number(g, h, v, s), number((g + 2) % 4, s, v ^ turn, h)) for g, h, v, s in EVERY] for turn in range(2)
]
NEAR, NEAR_TURNED = [
    [(number(g, h, v, s), number(g if h == s else 3 - g, s, v ^ turn, h)) for g, h, v, s in EVERY] for turn in range(2)
]
SIBLING = [(0, 1), (1, 0)]


def params(mib):
    return pltpu.CompilerParams(vmem_limit_bytes=mib * 1024 * 1024)


def smem():
    return pl.BlockSpec(memory_space=pltpu.SMEM)


def whole(shape):
    zeros = (0,) * len(shape)
    return pl.BlockSpec(shape, lambda *_: zeros)


def dot(a, b):
    return jnp.dot(a, b, preferred_element_type=F32)


def dot_turned(a, b):
    return lax.dot_general(a, b, (((1,), (1,)), ((), ())), preferred_element_type=F32)


def time_features(steps, embed_width):
    times = (steps.astype(F32) + 1.0) / (STEPS + 1.0)
    half = embed_width // 2
    frequency = jnp.exp(-jnp.log(10000.0) * jnp.arange(half, dtype=F32) / half)
    angles = 1000.0 * times[:, None] * frequency[None, :]
    embedding = jnp.concatenate([jnp.cos(angles), jnp.sin(angles)], axis=1)
    return (times, jax.nn.silu(embedding).astype(BF16))


def to_row(numbers):
    shape = (numbers[0].shape[0], OWNED, 128)
    lane = lax.broadcasted_iota(jnp.int32, shape, 2)
    token = lax.broadcasted_iota(jnp.int32, shape, 1)
    total = jnp.zeros(shape, F32)
    for k, number in enumerate(numbers):
        total = jnp.where(lane == token + OWNED * k, number, total)
    return jnp.sum(total, axis=1, keepdims=True)


def row_pieces(numbers, stride):
    row = to_row(numbers)
    per_row = 128 // stride
    rows = [row.astype(BF16).astype(F32)]
    row = row - rows[0]
    rows.append(row.astype(BF16).astype(F32))
    rows.append((row - rows[1]).astype(BF16).astype(F32))
    packed = [jnp.concatenate([r[:, :, :stride] for r in rows[:per_row]], axis=2)]
    if len(rows) > per_row:
        packed.append(jnp.concatenate([rows[per_row][:, :, :stride], jnp.zeros_like(row)[:, :, : 128 - stride]], axis=2))
    else:
        packed[0] = jnp.concatenate([packed[0], jnp.zeros_like(row)[:, :, : 128 - 3 * stride]], axis=2)
    return packed


def from_row(row, k):
    shape = (row.shape[0], OWNED, 128)
    lane = lax.broadcasted_iota(jnp.int32, shape, 2)
    token = lax.broadcasted_iota(jnp.int32, shape, 1)
    return jnp.sum(jnp.where(lane == token + OWNED * k, row, 0.0), axis=2, keepdims=True)


def local_lanes(load, place_ref):
    tile = load(pl.ds(pl.multiple_of(place_ref[1], 128), 128))
    middle = load(pl.ds(pl.multiple_of(place_ref[2], 128), 128))
    part = jnp.where(place_ref[0] == 0, middle[:, :NARROW], middle[:, NARROW:])
    return jnp.concatenate([tile, part], axis=1)


def unpack_weights(place_ref, own_ref, other_ref, net, w_ref):
    s = place_ref[4]
    for packed_ref, side in ((own_ref, s), (other_ref, 1 - s)):
        for chunk in range(CHUNKS):
            x, w = chunk // 2, chunk % 2
            for v in range(2):
                k = pl.multiple_of((x * 8 + w * 2 + v) * ROWS + side * (4 * ROWS), 32)
                first = max(net - 1, 0) * 192 + v * ROWS
                w_ref[pl.ds(k, ROWS), :WIDE] = packed_ref[chunk, first : first + ROWS, :]
                if net == 0:
                    part = packed_ref[chunk, 192:288, v * NARROW : (v + 1) * NARROW]
                else:
                    part = packed_ref[chunk, 384 + v * ROWS : 384 + (v + 1) * ROWS, (net - 1) * NARROW : net * NARROW]
                w_ref[pl.ds(k, ROWS), WIDE:] = part


def split_bits(value, count):
    pieces = []
    for _ in range(count):
        piece = value.astype(BF16)
        pieces.append(piece)
        value = value - piece.astype(F32)
    return pieces


def embed_moments(embed_ref, gram_ref, mean_ref):
    embed = embed_ref[...]
    ones = jnp.ones((8, D), BF16)
    column = dot_turned(embed, ones)[:, 0:1] / D
    row = dot_turned(ones, embed)[0:1] / D
    gram = dot_turned(embed, embed) / D - column * row
    gram_ref[...] = jnp.concatenate(split_bits(gram, 3), axis=1)
    mean_ref[...] = jnp.broadcast_to(column, mean_ref.shape)


def shape_tokens(x, embed_ref, mods_ref, image, gram_ref, mean_ref, store):
    turned = dot(x, gram_ref[...])
    turned = turned[:, :C] + turned[:, C : 2 * C] + turned[:, 2 * C :]
    inverse = lax.rsqrt(jnp.sum(turned * x.astype(F32), axis=1, keepdims=True) + norm_epsilon)
    inverse = jnp.broadcast_to(inverse, (TOKENS, BLOCK))
    twice = jnp.concatenate([x, x], axis=1)
    mean = mean_ref[:, 0:1]
    for b in range(D // BLOCK):
        cut = slice(b * BLOCK, (b + 1) * BLOCK)
        scaled = (embed_ref[:, cut].astype(F32) - mean) * (1.0 + mods_ref[image, 1:2, cut])
        scaled = jnp.concatenate(split_bits(scaled, 2), axis=0)
        store(cut, (dot(twice, scaled) * inverse + mods_ref[image, 0:1, cut]).astype(BF16))


def finish(preactivation, x, embed_ref, mods_ref, image, final_ref, place_ref):
    activated = jax.nn.gelu(preactivation, approximate=True).astype(BF16).astype(F32)
    own_hidden = dot(x, local_lanes(lambda at: embed_ref[:, at], place_ref))
    gate = local_lanes(lambda at: mods_ref[image, 2:3, at], place_ref)
    scale = local_lanes(lambda at: mods_ref[image, 4:5, at], place_ref)
    residual = own_hidden + gate * activated
    total = jnp.sum(residual, axis=1, keepdims=True)
    total_square = jnp.sum(residual * residual, axis=1, keepdims=True)
    own_mean = total / COLS
    final = local_lanes(lambda at: final_ref[:, at], place_ref)
    centred = ((residual - own_mean) * (1.0 + scale)).astype(BF16)
    partial = dot_turned(centred, final)
    return residual, partial, total, total_square


def owned(value):
    return value.reshape(OWNERS, OWNED, value.shape[-1])


def sums_kernel(g_final_ref, t_final_ref, f_final_ref, mods_ref, out_ref):
    run = lax.broadcasted_iota(jnp.int32, (OWNERS, D), 1) // COLS
    own = run == lax.broadcasted_iota(jnp.int32, (OWNERS, D), 0)
    for net, final_ref in enumerate((g_final_ref, t_final_ref, f_final_ref)):
        scales = [mods_ref[3 * net + i, 4:5, :] for i in range(IMAGES)]
        shifts = [mods_ref[3 * net + i, 3:4, :] for i in range(IMAGES)]
        left = [jnp.where(own, row, 0.0) for row in scales + [jnp.ones((1, D), F32)]]
        left = jnp.concatenate(left + shifts + [jnp.zeros((5, D), F32)], axis=0).astype(BF16)
        sums = dot_turned(left, final_ref[...])
        ones = sums[3 * OWNERS : 4 * OWNERS]
        runs = [sums[i * OWNERS : (i + 1) * OWNERS] + ones for i in range(IMAGES)]
        totals = [jnp.sum(r, axis=0, keepdims=True) for r in runs]
        out_ref[net] = jnp.concatenate(runs + totals + [sums[64:67], jnp.zeros((2, C), F32)], axis=0)


def read_sums(sums_ref, net):
    runs = [sums_ref[net, i * OWNERS : (i + 1) * OWNERS] for i in range(IMAGES)]
    return runs, [sums_ref[net, 48 + i : 49 + i] for i in range(IMAGES)], [sums_ref[net, 51 + i : 52 + i] for i in range(IMAGES)]


def add_up(partials, totals, squares, runs):
    means = totals * (1.0 / COLS)
    ordered = [((g + 2) % 4 * 2 + h) * 2 + v for v in range(2) for h in range(2) for g in range(4)]
    ordered = jnp.concatenate([runs[run : run + 1][None] for run in ordered], axis=0)
    partial = jnp.sum(partials + means * ordered, axis=0)
    average = jnp.sum(totals, axis=0) / D
    inverse = lax.rsqrt(jnp.sum(squares, axis=0) / D - average * average + norm_epsilon)
    return partial, average, inverse


def split_kernel(place_ref, cond_ref, gen_noise_ref, score_noise_ref, gen_ref, teacher_ref, fake_ref,
                 gen_mod_ref, teacher_mod_ref, fake_mod_ref, mine_ref, other_ref, noise_ref):
    for i in range(IMAGES):
        noise = jnp.concatenate([gen_noise_ref[i], score_noise_ref[i]], axis=0).astype(F32).T.astype(BF16)
        noise_ref[i * HALF : (i + 1) * HALF] = noise
    cond = cond_ref[...]
    mods = [dot_turned(cond, ref[...]) for ref in (gen_mod_ref, teacher_mod_ref, fake_mod_ref)]
    mods = jnp.concatenate([mods[0][0:3], mods[1][3:6], mods[2][3:6]], axis=0)
    mods = jnp.concatenate([mods, jnp.zeros((9, 32), F32)], axis=1)
    mods = jnp.concatenate([mods[:, 128 * p : 128 * (p + 1)] for p in range(4)] + [jnp.zeros((12, 128), F32)], axis=0)
    mine_ref[MODS_AT:] = mods.astype(BF16)
    other_ref[MODS_AT:] = mods.astype(BF16)
    first = place_ref[0] == 0
    mine, other = [], []
    for n, ref in enumerate((gen_ref, teacher_ref, fake_ref)):
        rows = slice(n * ROWS, (n + 1) * ROWS)
        low, high = ref[:, :128], ref[:, 256:]
        mine_ref[rows] = jnp.where(first, low, high)
        other_ref[rows] = jnp.where(first, high, low)
        low, high = ref[:, 128:192], ref[:, 192:256]
        mine.append(jnp.where(first, low, high))
        other.append(jnp.where(first, high, low))
    for ref, parts in ((mine_ref, mine), (other_ref, other)):
        ref[3 * ROWS : 4 * ROWS] = jnp.concatenate(parts[1:], axis=1)
        ref[4 * ROWS : MODS_AT] = jnp.concatenate([parts[0], parts[0]], axis=1)


def in_order(v, mine, other):
    return jnp.where(v == 0, mine, other), jnp.where(v == 0, other, mine)


def pack_kernel(place_ref, mine_ref, other_ref, out_ref):
    v = place_ref[0]
    tiles = in_order(v, mine_ref[:ROWS], other_ref[:ROWS])
    parts = in_order(v, mine_ref[4 * ROWS : MODS_AT], other_ref[4 * ROWS : MODS_AT])
    parts = jnp.concatenate([part[:, :NARROW] for part in parts], axis=1)
    mods = in_order(v, mine_ref[MODS_AT:].astype(F32), other_ref[MODS_AT:].astype(F32))
    mods = jnp.concatenate([mods[0][:MODS_ROWS], mods[1][:MODS_ROWS], jnp.zeros((8, 128), F32)], axis=0)
    gen = jnp.concatenate([*tiles, parts, mods.astype(BF16)], axis=0)
    for k in range(CHUNKS):
        out_ref[k] = gen


def pack_score_kernel(place_ref, mine_ref, other_ref, out_ref):
    cuts = [slice(n * ROWS, (n + 1) * ROWS) for n in (1, 2, 3)]
    ordered = [in_order(place_ref[0], mine_ref[rows], other_ref[rows]) for rows in cuts]
    score = jnp.concatenate([block for pair in ordered for block in pair], axis=0)
    for k in range(CHUNKS):
        out_ref[k] = score


def generator_kernel(place_ref, own_ref, other_ref, embed_ref, mods_ref, final_ref, own_w_ref, other_w_ref,
                     part_ref, shaped_ref, pre_ref, res_ref, w_ref, gram_ref, mean_ref, sum_ref):
    i = pl.program_id(0)
    v = place_ref[0]

    @pl.when(i == 0)
    def _():
        embed_moments(embed_ref, gram_ref, mean_ref)
        unpack_weights(place_ref, own_w_ref, other_w_ref, 0, w_ref)
        sum_ref[:, 24:, :] = jnp.zeros((OWNERS, 8, 128), F32)

    x = jnp.concatenate(in_order(v, own_ref[:, :C], other_ref[:, :C]), axis=0)

    def store(cut, shaped):
        shaped_ref[0, :, cut] = shaped

    shape_tokens(x, embed_ref, mods_ref, 0, gram_ref, mean_ref, store)
    pre = dot(shaped_ref[0], w_ref[...])
    res, partial, total, square = finish(pre, x, embed_ref, mods_ref, 0, final_ref, place_ref)
    pre_ref[0] = pre
    res_ref[0] = res
    pieces = owned(partial)
    pieces = jnp.concatenate([pieces[:, :8], pieces[:, 8:]], axis=2)
    rows = row_pieces([owned(total), owned(square)], 32)
    sum_ref[:, pl.ds(pl.multiple_of(i * 8, 8), 8), :] = pieces
    sum_ref[:, pl.ds(24 + i, 1), :] = rows[0]

    @pl.when(i == IMAGES - 1)
    def _():
        part_ref[...] = sum_ref[...].astype(BF16)


def samples_kernel(place_ref, time_ref, got_ref, noise_ref, sums_ref, out_ref, keep_ref):
    runs, scales, shifts = read_sums(sums_ref, 0)
    got = got_ref[...].astype(F32)
    packed = []
    for i in range(IMAGES):
        block = got[:, 8 * i : 8 * i + 8]
        partials = jnp.concatenate([block[:, :, :C], block[:, :, C:]], axis=1)
        row = got[:, 24 + i : 25 + i]
        row = row[:, :, :32] + row[:, :, 32:64] + row[:, :, 64:96]
        row = jnp.concatenate([row, jnp.zeros((OWNERS, 1, 96), F32)], axis=2)
        partial, average, inverse = add_up(partials, from_row(row, 0), from_row(row, 1), runs[i])
        inner = inverse * (partial - average * scales[i])
        velocity = inner + shifts[i]
        noise = noise_ref[pl.ds(pl.multiple_of(place_ref[3] + i * HALF, 16), OWNED), :][:, :C].astype(F32)
        samples = noise - time_ref[i] * velocity
        packed.append(jnp.concatenate([samples[:8], samples[8:]], axis=1))
        at = slice(i * OWNED, (i + 1) * OWNED)
        keep_ref[0, at, :] = samples
        keep_ref[1, at, :] = inner
        keep_ref[2, at, :] = jnp.broadcast_to(average, (OWNED, C))
        keep_ref[3, at, :] = jnp.broadcast_to(inverse, (OWNED, C))
    out_ref[...] = jnp.broadcast_to(jnp.concatenate(packed, axis=0)[None], out_ref.shape)


def mix(samples, noise, t):
    return ((1.0 - t) * samples + t * noise).astype(BF16)


def score_kernel(place_ref, time_ref, got_ref, own_ref, other_ref,
                 t_embed_ref, f_embed_ref, t_mods_ref, f_mods_ref, t_final_ref, f_final_ref, own_w_ref, other_w_ref,
                 part_ref, samples_ref, shaped_ref, pre_ref, res_ref,
                 t_w_ref, f_w_ref, t_gram_ref, f_gram_ref, t_mean_ref, f_mean_ref, t_shaped_ref, f_shaped_ref, x_ref, sum_ref):
    i = pl.program_id(0)
    v = place_ref[0]

    @pl.when(i == 0)
    def _():
        embed_moments(t_embed_ref, t_gram_ref, t_mean_ref)
        embed_moments(f_embed_ref, f_gram_ref, f_mean_ref)
        unpack_weights(place_ref, own_w_ref, other_w_ref, 1, t_w_ref)
        unpack_weights(place_ref, own_w_ref, other_w_ref, 2, f_w_ref)
        sum_ref[:, 48:, :] = jnp.zeros((OWNERS, 16, 128), F32)
    got = got_ref[:, pl.ds(pl.multiple_of(i * 8, 8), 8), :]
    samples = jnp.concatenate([got[:, :, :C], got[:, :, C:]], axis=1).reshape(TOKENS, C)
    turned = jnp.concatenate([samples[:HALF], samples[HALF:]], axis=1).T
    samples_ref[0] = jnp.where(v == 0, turned[:C], turned[C:])
    own, other = own_ref[:, C:].astype(F32), other_ref[:, C:].astype(F32)
    noise = jnp.concatenate(in_order(v, own, other), axis=0)
    noised = mix(samples, noise, time_ref[i])
    x_ref[i] = noised
    tokens = pl.ds(pl.multiple_of(i * TOKENS, TOKENS), TOKENS)

    def t_store(cut, shaped):
        t_shaped_ref[tokens, cut] = shaped

    def f_store(cut, shaped):
        f_shaped_ref[tokens, cut] = shaped
        shaped_ref[0, :, cut] = shaped

    shape_tokens(noised, t_embed_ref, t_mods_ref, i, t_gram_ref, t_mean_ref, t_store)
    shape_tokens(noised, f_embed_ref, f_mods_ref, i, f_gram_ref, f_mean_ref, f_store)

    @pl.when(i == IMAGES - 1)
    def _():
        t_pre = dot(t_shaped_ref[...], t_w_ref[...])
        f_pre = dot(f_shaped_ref[...], f_w_ref[...])
        for n in range(IMAGES):
            x = x_ref[n]
            rows = slice(n * TOKENS, (n + 1) * TOKENS)
            _, t_partial, t_total, t_square = finish(t_pre[rows], x, t_embed_ref, t_mods_ref, n, t_final_ref, place_ref)
            res, f_partial, f_total, f_square = finish(f_pre[rows], x, f_embed_ref, f_mods_ref, n, f_final_ref, place_ref)
            pre_ref[n] = f_pre[rows]
            res_ref[n] = res
            sum_ref[:, 16 * n : 16 * n + 16, :] = owned(jnp.concatenate([t_partial, f_partial], axis=1))
            pieces = row_pieces([owned(v) for v in (t_total, t_square, f_total, f_square)], 64)
            for k in range(2):
                sum_ref[:, 48 + 2 * n + k : 49 + 2 * n + k, :] = pieces[k]
        part_ref[...] = sum_ref[...].astype(BF16)


def cotangent_kernel(place_ref, gen_time_ref, time_ref, got_ref, noise_ref, keep_ref, sums_ref, out_ref):
    loss_scale = 1.0 / math.sqrt(IMAGES * S)
    t_runs, t_scales, t_shifts = read_sums(sums_ref, 1)
    f_runs, f_scales, f_shifts = read_sums(sums_ref, 2)
    got = got_ref[...].astype(F32)
    lane = lax.broadcasted_iota(jnp.int32, (1, 128), 1)
    cots, rows = [], []
    for i in range(IMAGES):
        block = got[:, 16 * i : 16 * i + 16]
        row = got[:, 48 + 2 * i : 50 + 2 * i]
        row = row[:, :1, :64] + row[:, :1, 64:] + row[:, 1:, :64]
        row = jnp.concatenate([row, jnp.zeros((OWNERS, 1, 64), F32)], axis=2)

        def inner(partials, k, runs, scale):
            partial, average, inverse = add_up(partials, from_row(row, k), from_row(row, k + 1), runs)
            return inverse * (partial - average * scale), average, inverse

        t_inner, _, _ = inner(block[:, :, :C], 0, t_runs[i], t_scales[i])
        f_inner, f_average, f_inverse = inner(block[:, :, C:], 2, f_runs[i], f_scales[i])
        teacher, fake = t_inner + t_shifts[i], f_inner + f_shifts[i]
        at = slice(i * OWNED, (i + 1) * OWNED)
        samples, g_inner = keep_ref[0, at, :], keep_ref[1, at, :]
        g_average, g_inverse = keep_ref[2, at, 0:1], keep_ref[3, at, 0:1]
        noise = noise_ref[pl.ds(pl.multiple_of(place_ref[3] + i * HALF, 16), OWNED), :][:, C:].astype(F32)
        t = time_ref[i]
        noised = mix(samples, noise, t).astype(F32)
        distance = jnp.sum(jnp.abs(samples - noised + t * teacher))
        gen_cot = (-(gen_time_ref[i] * t * loss_scale) * (teacher - fake)).astype(BF16).astype(F32)
        fake_cot = (loss_scale * (fake - noise + samples)).astype(BF16).astype(F32)
        numbers = []
        for cot, column, value, average, inverse in (
            (fake_cot, f_scales[i], f_inner, f_average, f_inverse),
            (gen_cot, sums_ref[0, 48 + i : 49 + i], g_inner, g_average, g_inverse),
        ):
            first = jnp.sum(cot * column, axis=1, keepdims=True) / D
            second = jnp.sum(cot * value, axis=1, keepdims=True) / D
            slope = inverse * inverse * second
            numbers += [inverse, slope, average * slope - inverse * first]
        cots.append(jnp.concatenate([fake_cot, gen_cot], axis=1))
        numbers_row = to_row([number[None] for number in numbers])[0]
        numbers_row = jnp.where(lane == 96, distance, numbers_row)
        for _ in range(3):
            rounded = numbers_row.astype(BF16).astype(F32)
            rows.append(rounded)
            numbers_row = numbers_row - rounded
    rows.append(jnp.zeros((7, 128), F32))
    packed = jnp.concatenate(cots + rows, axis=0).astype(BF16)
    out_ref[...] = jnp.broadcast_to(packed[None], out_ref.shape)


def gelu_slope(v):
    a, b = math.sqrt(2.0 / math.pi), 0.044715
    t = jnp.tanh(a * (v + b * (v * v * v)))
    return 0.5 * (1.0 + t) + 0.5 * v * (1.0 - t * t) * (a * (1.0 + 3.0 * b * (v * v)))


def gradient_kernel(net, place_ref, got_ref, *refs):
    gap_ref, refs = (refs[0], refs[1:]) if net == 1 else (None, refs)
    mods_ref, final_ref, pre_ref, res_ref, shaped_ref, keep_ref, send_ref, left_ref = refs

    @pl.when(pl.program_id(0) == 0)
    def _():
        final = local_lanes(lambda at: final_ref[:, at], place_ref)
        if net == 1:
            gaps = jnp.sum(gap_ref[...], axis=0)
        for i in range(IMAGES):
            row = got_ref[:, 48:64, :].astype(F32)
            row = row[:, 3 * i : 3 * i + 1] + row[:, 3 * i + 1 : 3 * i + 2] + row[:, 3 * i + 2 : 3 * i + 3]
            inverse, slope, offset = [from_row(row, 3 * net + k).reshape(TOKENS, 1) for k in range(3)]
            cot = got_ref[:, 16 * i : 16 * i + 16, :].reshape(TOKENS, 128)[:, net * C : (net + 1) * C]
            out_grad = dot(cot, final)
            scale = local_lanes(lambda at: mods_ref[i, 4:5, at], place_ref)
            gate = local_lanes(lambda at: mods_ref[i, 2:3, at], place_ref)
            res_grad = inverse * (out_grad * (1.0 + scale)) - slope * res_ref[i] + offset
            act_grad = res_grad * gate
            if net == 1:
                inverse_gap = 1.0 / (gaps[i : i + 1, :] / (S * C) + gap_epsilon)
                act_grad = act_grad * jnp.concatenate([inverse_gap, inverse_gap[:, :NARROW]], axis=1)
            grad = act_grad * gelu_slope(pre_ref[i])
            turned = jnp.concatenate([grad, jnp.zeros((TOKENS, NARROW), F32)], axis=1).T
            left_ref[:, i * TOKENS : (i + 1) * TOKENS] = turned[:COLS].astype(BF16)

    grad = dot(left_ref[...], shaped_ref[...].reshape(IMAGES * TOKENS, 768))
    tiles = grad[:WIDE].T.astype(BF16)
    parts = jnp.concatenate([grad[WIDE:, :384], grad[WIDE:, 384:]], axis=0).T.astype(BF16)
    first = place_ref[4] == 0
    for w in range(2):
        sides = []
        for h in range(2):
            at = [(w * 2 + v) * ROWS for v in range(2)]
            lanes = slice(h * NARROW, (h + 1) * NARROW)
            narrow = jnp.concatenate([parts[k : k + ROWS, lanes] for k in at], axis=1)
            sides.append([tiles[h * 384 + k : h * 384 + k + ROWS] for k in at] + [narrow])
        for n, (low, high) in enumerate(zip(*sides, strict=True)):
            keep_ref[w, n * ROWS : (n + 1) * ROWS, :] = jnp.where(first, low, high)
            send_ref[w, n * ROWS : (n + 1) * ROWS, :] = jnp.where(first, high, low)


def add_kernel(place_ref, f_keep_ref, f_got_ref, g_keep_ref, g_got_ref, *out_refs):
    for (dx, dw), out_ref in zip(OFFSETS, out_refs, strict=True):
        at = lax.rem(place_ref[5] + dx, 4) * 2 + lax.rem(place_ref[6] + dw, 2)
        for n, (keep_ref, got_ref) in enumerate(((f_keep_ref, f_got_ref), (g_keep_ref, g_got_ref))):
            total = keep_ref[at].astype(F32) + got_ref[at].astype(F32)
            out_ref[n * GEN_ROWS : (n + 1) * GEN_ROWS] = total.astype(BF16)


def sum_kernel(place_ref, *refs):
    got_refs, (keep_ref, send_ref) = refs[:CHUNKS], refs[CHUNKS:]
    v = place_ref[0]
    for n in range(2):
        rows = slice(n * GEN_ROWS, (n + 1) * GEN_ROWS)
        total = got_refs[0][rows].astype(F32)
        for got_ref in got_refs[1:]:
            total = total + got_ref[rows].astype(F32)
        def folded(rows, part):
            return jnp.concatenate([rows, jnp.concatenate([part[:48], part[48:]], axis=1)], axis=0)

        low = folded(total[:ROWS], total[2 * ROWS :, :NARROW])
        high = folded(total[ROWS : 2 * ROWS], total[2 * ROWS :, NARROW:])
        keep_ref[n] = jnp.where(v == 0, low, high).astype(BF16)
        send_ref[n] = jnp.where(v == 0, high, low).astype(BF16)


def place_kernel(place_ref, keep_ref, other_ref, fake_ref, gen_ref):
    for n, ref in enumerate((fake_ref, gen_ref)):
        low, high = in_order(place_ref[0], keep_ref[n].astype(F32), other_ref[n].astype(F32))
        ref[:, :128] = low[:ROWS]
        ref[:48, 128:256] = jnp.concatenate([low[ROWS:, :NARROW], high[ROWS:, :NARROW]], axis=1)
        ref[48:, 128:256] = jnp.concatenate([low[ROWS:, NARROW:], high[ROWS:, NARROW:]], axis=1)
        ref[:, 256:] = high[:ROWS]


def in_hbm(*arrays):
    return [pltpu.with_memory_space_constraint(a, pltpu.HBM) for a in arrays]


def exchange(value, axes):
    return lax.all_to_all(value, axes, 0, 0)


def shards(
    gen_noise,
    score_noise,
    gen_steps,
    score_steps,
    gen_embed,
    gen_modulation,
    gen_proj,
    gen_final,
    teacher_embed,
    teacher_modulation,
    teacher_proj,
    teacher_final,
    fake_embed,
    fake_modulation,
    fake_proj,
    fake_final,
):
    v, s = lax.axis_index("v"), lax.axis_index("s")
    start = (lax.rem(lax.axis_index("g") + 2, 4) * 2 + lax.axis_index("h")) * 384
    member = lax.axis_index(("h", "g"))
    place = jnp.stack(
        [v, start + 256 * v, start + 128, member * OWNED, s, lax.axis_index("x"), lax.axis_index("w")]
    ).astype(jnp.int32)
    gen_final, teacher_final, fake_final = gen_final.T, teacher_final.T, fake_final.T

    times, conds = time_features(jnp.concatenate([gen_steps, score_steps]), gen_modulation.shape[0])
    gen_time, score_time = times[:3], times[3:]
    halves = jax.ShapeDtypeStruct((SENT_ROWS, 128), BF16)
    mine, other, noise = pl.pallas_call(
        split_kernel,
        grid=(1,),
        in_specs=[smem(), whole((6, 256))] + [whole((IMAGES, C, HALF))] * 2 + [whole((ROWS, 384))] * 3
        + [whole((480, 256))] * 3,
        out_specs=[whole((SENT_ROWS, 128))] * 2 + [whole((NOISE_ROWS, 128))],
        out_shape=[halves, halves, jax.ShapeDtypeStruct((NOISE_ROWS, 128), BF16)],
        compiler_params=params(60),
        name="split",
    )(place, conds, gen_noise.transpose(0, 2, 1), score_noise.transpose(0, 2, 1), gen_proj, teacher_proj, fake_proj,
      gen_modulation.T, teacher_modulation.T, fake_modulation.T)
    mine = lax.ppermute(mine, PLACES, SWAP)
    other = lax.ppermute(other, PLACES, SWAP_TURNED)
    mine, other, noise = lax.optimization_barrier((mine, other, noise))
    own_noise = lax.ppermute(noise, PLACES, NEAR)
    other_noise = lax.ppermute(noise, PLACES, NEAR_TURNED)

    def pack(kernel, rows):
        return pl.pallas_call(
            kernel,
            grid=(1,),
            in_specs=[smem()] + [whole((SENT_ROWS, 128))] * 2,
            out_specs=whole((CHUNKS, rows, 128)),
            out_shape=jax.ShapeDtypeStruct((CHUNKS, rows, 128), BF16),
            compiler_params=params(6),
            name="pack",
        )(place, mine, other)

    g_packed = pack(pack_kernel, GEN_CHUNK)
    g_packed = exchange(g_packed, GATHER)
    mine, other, own_noise, other_noise = lax.optimization_barrier((mine, other, own_noise, other_noise))
    packed = pack(pack_score_kernel, SCORE_ROWS)
    g_packed, own_noise, other_noise = lax.optimization_barrier((g_packed, own_noise, other_noise))
    g_other = lax.ppermute(g_packed, "s", SIBLING)
    packed, g_packed, g_other = lax.optimization_barrier((packed, g_packed, g_other))
    packed = exchange(packed, GATHER)
    low, high = (a[:, GEN_ROWS : GEN_ROWS + 2 * MODS_ROWS] for a in in_order(s, g_packed, g_other))
    mods = jnp.stack([low, high]).reshape(2, 4, 2, 2, 4, 9, 128).transpose(5, 1, 0, 2, 3, 4, 6)
    mods = mods.reshape(9, 32, 512)[:, :, :480].reshape(9, 5, D).astype(F32)
    mods = jnp.pad(mods, ((0, 0), (0, 3), (0, 0)))

    by_image = lambda *shape: pl.BlockSpec((1, *shape), lambda i: (i,) + (0,) * len(shape))
    noise_rows = pl.BlockSpec((HALF, 128), lambda i: (i, 0))
    mods_of = lambda net: pl.BlockSpec((1, 8, D), lambda i: (3 * net + i, 0, 0))
    local = pltpu.HBM((IMAGES, TOKENS, COLS), F32)
    wide = pltpu.HBM((IMAGES, TOKENS, D), BF16)
    gen_embed, teacher_embed, fake_embed = in_hbm(gen_embed, teacher_embed, fake_embed)
    gen_final, teacher_final, fake_final = in_hbm(gen_final, teacher_final, fake_final)

    sums = pl.pallas_call(
        sums_kernel,
        grid=(1,),
        in_specs=[whole((C, D))] * 3 + [whole((9, 8, D))],
        out_specs=whole((3, 56, C)),
        out_shape=jax.ShapeDtypeStruct((3, 56, C), F32),
        compiler_params=params(16),
        name="sums",
    )(gen_final, teacher_final, fake_final, mods)

    part, g_shaped, g_pre, g_res = pl.pallas_call(
        generator_kernel,
        grid=(IMAGES,),
        in_specs=[
            smem(), noise_rows, noise_rows, whole((C, D)), mods_of(0), whole((C, D)),
            *([whole((CHUNKS, GEN_CHUNK, 128))] * 2),
        ],
        out_specs=[whole((OWNERS, 32, 128)), by_image(TOKENS, D), by_image(TOKENS, COLS), by_image(TOKENS, COLS)],
        out_shape=[jax.ShapeDtypeStruct((OWNERS, 32, 128), BF16), wide, local, local],
        scratch_shapes=[pltpu.VMEM((D, COLS), BF16), pltpu.VMEM((C, 3 * C), BF16), pltpu.VMEM((C, 128), F32),
                        pltpu.VMEM((OWNERS, 32, 128), F32)],
        compiler_params=params(16),
        cost_estimate=pl.CostEstimate(flops=12 * 10**9, bytes_accessed=30 * 10**6, transcendentals=0),
        name="generator",
    )(place, own_noise, other_noise, gen_embed, mods, gen_final, g_packed, g_other)
    packed, part, sums = lax.optimization_barrier((packed, part, sums))
    part = exchange(part, COMBINE)

    net_mods = lambda net: pl.BlockSpec((IMAGES, 8, D), lambda *_: (net, 0, 0))
    pack1, keep = pl.pallas_call(
        samples_kernel,
        grid=(1,),
        in_specs=[
            smem(), smem(), whole((OWNERS, 32, 128)), whole((NOISE_ROWS, 128)), whole((3, 56, C)),
        ],
        out_specs=[whole((OWNERS, 24, 128)), whole((4, 48, C))],
        out_shape=[
            jax.ShapeDtypeStruct((OWNERS, 24, 128), F32),
            jax.ShapeDtypeStruct((4, 48, C), F32),
        ],
        compiler_params=params(5),
        name="samples",
    )(place, gen_time, part, own_noise, sums)
    packed, pack1 = lax.optimization_barrier((packed, pack1))
    pack1 = exchange(pack1, COMBINE)
    other_packed = lax.ppermute(packed, "s", SIBLING)

    part2, samples, f_shaped, f_pre, f_res = pl.pallas_call(
        score_kernel,
        grid=(IMAGES,),
        in_specs=[
            smem(), smem(), whole((OWNERS, 24, 128)), noise_rows, noise_rows,
            whole((C, D)), whole((C, D)), net_mods(1), net_mods(2), whole((C, D)), whole((C, D)),
            *([whole((CHUNKS, SCORE_ROWS, 128))] * 2),
        ],
        out_specs=[
            whole((OWNERS, 64, 128)), by_image(C, HALF), by_image(TOKENS, D), whole((IMAGES, TOKENS, COLS)),
            whole((IMAGES, TOKENS, COLS)),
        ],
        out_shape=[
            jax.ShapeDtypeStruct((OWNERS, 64, 128), BF16),
            jax.ShapeDtypeStruct((IMAGES, C, HALF), F32),
            wide, local, local,
        ],
        scratch_shapes=[
            *([pltpu.VMEM((D, COLS), BF16)] * 2), *([pltpu.VMEM((C, 3 * C), BF16)] * 2),
            *([pltpu.VMEM((C, 128), F32)] * 2), *([pltpu.VMEM((IMAGES * TOKENS, D), BF16)] * 2),
            pltpu.VMEM((IMAGES, TOKENS, C), BF16),
            pltpu.VMEM((OWNERS, 64, 128), F32),
        ],
        compiler_params=params(34),
        cost_estimate=pl.CostEstimate(flops=24 * 10**9, bytes_accessed=50 * 10**6, transcendentals=0),
        name="score",
    )(place, score_time, pack1, own_noise, other_noise, teacher_embed, fake_embed, mods, mods,
      teacher_final, fake_final, packed, other_packed)
    part2 = exchange(part2, COMBINE)

    pack2 = pl.pallas_call(
        cotangent_kernel,
        grid=(1,),
        in_specs=[
            smem(), smem(), smem(), whole((OWNERS, 64, 128)), whole((NOISE_ROWS, 128)), whole((4, 48, C)),
            whole((3, 56, C)),
        ],
        out_specs=whole((OWNERS, 64, 128)),
        out_shape=jax.ShapeDtypeStruct((OWNERS, 64, 128), BF16),
        compiler_params=params(6),
        name="cotangents",
    )(place, gen_time, score_time, part2, own_noise, keep, sums)
    pack2 = exchange(pack2, COMBINE)
    samples, pack2 = lax.optimization_barrier((samples, pack2))
    own_samples = samples
    samples = lax.ppermute(samples, "s", SIBLING)

    gap = jnp.sum(pack2[:, 48:57, 96].astype(F32).reshape(OWNERS, 3, 3), axis=(0, 2))
    gap = jnp.broadcast_to(jnp.pad(gap, (0, 5))[None, :, None], (16, 8, 128))
    gap = exchange(gap, TOKEN_AXES)
    samples, gap = lax.optimization_barrier((samples, gap))
    samples = jnp.where(lax.axis_index("h") == s, own_samples, samples).transpose(0, 2, 1)

    by_columns = pl.BlockSpec((IMAGES, TOKENS, 768), lambda x: (0, 0, x))
    partial = jax.ShapeDtypeStruct((CHUNKS, GEN_ROWS, 128), BF16)
    partial_spec = pl.BlockSpec((2, GEN_ROWS, 128), lambda x: (x, 0, 0))

    def gradient(net, gaps, mods_net, final, pre, res, shaped):
        kept, sent = pl.pallas_call(
            functools.partial(gradient_kernel, net),
            grid=(4,),
            in_specs=[
                smem(), whole((OWNERS, 64, 128)), *([whole((16, 8, 128))] * len(gaps)), net_mods(mods_net),
                whole((C, D)), *([whole((IMAGES, TOKENS, COLS))] * 2), by_columns,
            ],
            out_specs=[partial_spec, partial_spec],
            out_shape=[partial, partial],
            scratch_shapes=[pltpu.VMEM((COLS, IMAGES * TOKENS), BF16)],
            compiler_params=params(13),
            cost_estimate=pl.CostEstimate(flops=7 * 10**9, bytes_accessed=20 * 10**6, transcendentals=0),
        name="gradient",
        )(place, pack2, *gaps, mods, final, *in_hbm(pre, res, shaped))
        return kept, lax.ppermute(sent, "s", SIBLING)

    pieces = gradient(0, (), 2, fake_final, f_pre, f_res, f_shaped)
    pieces += gradient(1, (gap,), 0, gen_final, g_pre, g_res, g_shaped)
    partials = pl.pallas_call(
        add_kernel,
        grid=(1,),
        in_specs=[smem()] + [whole((CHUNKS, GEN_ROWS, 128))] * 4,
        out_specs=[whole((2 * GEN_ROWS, 128))] * CHUNKS,
        out_shape=[jax.ShapeDtypeStruct((2 * GEN_ROWS, 128), BF16)] * CHUNKS,
        compiler_params=params(16),
        name="add",
    )(place, *pieces)
    partials = [
        lax.ppermute(
            part, GATHER, [(x * 2 + w, (x + dx) % 4 * 2 + (w + dw) % 2) for x in range(4) for w in range(2)]
        ) if dx or dw else part
        for (dx, dw), part in zip(OFFSETS, partials, strict=True)
    ]
    tiles = jax.ShapeDtypeStruct((2, 144, 128), BF16)
    kept, sent = pl.pallas_call(
        sum_kernel,
        grid=(1,),
        in_specs=[smem()] + [whole((2 * GEN_ROWS, 128))] * CHUNKS,
        out_specs=[whole((2, 144, 128))] * 2,
        out_shape=[tiles, tiles],
        compiler_params=params(8),
        name="sum",
    )(place, *partials)
    kept = lax.ppermute(kept, PLACES, SWAP)
    sent = lax.ppermute(sent, PLACES, SWAP_TURNED)
    fake_grad, gen_grad = pl.pallas_call(
        place_kernel,
        grid=(1,),
        in_specs=[smem(), whole((2, 144, 128)), whole((2, 144, 128))],
        out_specs=[whole((ROWS, 384))] * 2,
        out_shape=[jax.ShapeDtypeStruct((ROWS, 384), F32)] * 2,
        compiler_params=params(4),
        name="place",
    )(place, kept, sent)
    return (samples, gen_grad, fake_grad)


def solution(mesh):
    split = Mesh(mesh.devices.reshape(4, 4, 2, 2, 2, 2), ("g", "x", "h", "w", "v", "s"))
    tokens = P(None, ROW_AXES, None)
    columns = P(None, ROW_AXES)
    block = P(ROW_AXES, ("g", "s"))
    net = (P(), columns, block, P())
    return jax.shard_map(
        shards,
        mesh=split,
        in_specs=(tokens, tokens, P(), P(), *net, *net, *net),
        out_specs=(tokens, block, block),
        check_vma=False,
    )
```
